32 devices in a mesh: dp: 8 (over y, x, core), tensor: 4 (over z).
Axes of the slice: x: 2, y: 2, z: 4, core: 2. Of those that a mesh axis runs over, the one named last changes fastest.
Arguments:
- tokens: bfloat16 [16384, 768], P(('dp', 'tensor')), may hold values from -6 to 6
- segment_ids: int32 [16384], P(('dp', 'tensor')), may hold values from 0 to 3, as said below
- cotangent: bfloat16 [16384, 768], P(('dp', 'tensor')), may hold values from -6 to 6
- norm1_gain: float32 [768], replicated, may hold values from 0.1 to 1.9
- norm1_shift: float32 [768], replicated, may hold values from -1.75 to 1.75
- qkv_weight: bfloat16 [768, 3, 768], P(None, None, 'tensor'), may hold values from -0.3125 to 0.3125
- conv_kernel: float32 [3, 3, 768], P(None, None, 'tensor'), may hold values from -3.5 to 3.5
- out_weight: bfloat16 [768, 768], P('tensor'), may hold values from -0.875 to 0.875
- out_bias: float32 [768], replicated, may hold values from -1.75 to 1.75
- norm2_gain: float32 [768], replicated, may hold values from 0.1 to 1.9
- norm2_shift: float32 [768], replicated, may hold values from -1.75 to 1.75
- up_weight: bfloat16 [768, 3072], P(None, 'tensor'), may hold values from -0.21875 to 0.21875
- up_bias: float32 [3072], P('tensor'), may hold values from -3 to 3
- down_weight: bfloat16 [3072, 768], P('tensor'), may hold values from -0.109375 to 0.109375
- down_bias: float32 [768], replicated, may hold values from -1.75 to 1.75
Outputs:
- result: bfloat16 [16384, 768], P(('dp', 'tensor'))
- grad_tokens: float32 [16384, 768], P(('dp', 'tensor'))
- grad_norm1_gain: float32 [768], replicated
- grad_norm1_shift: float32 [768], replicated
- grad_qkv_weight: float32 [768, 3, 768], P(None, None, 'tensor')
- grad_conv_kernel: float32 [3, 3, 768], P(None, None, 'tensor')
- grad_out_weight: float32 [768, 768], P('tensor')
- grad_out_bias: float32 [768], replicated
- grad_norm2_gain: float32 [768], replicated
- grad_norm2_shift: float32 [768], replicated
- grad_up_weight: float32 [768, 3072], P(None, 'tensor')
- grad_up_bias: float32 [3072], P('tensor')
- grad_down_weight: float32 [3072, 768], P('tensor')
- grad_down_bias: float32 [768], replicated
The draws below stay inside these ranges and needn't reach their ends.
Inputs may be any that keep to these rules, and one draw needn't show every extreme that they name: `segment_ids`: each sequence of 2048 tokens holds four documents numbered 0, 1, 2, 3 in order, each of one token or more.
All inputs are finite; a program needn't handle non-finite values.
Results may differ from the reference program's by a relative error of at most 0.02.
The reference program's roundings to bfloat16 on the way count: a program that leaves them out, or rounds other values in their place, can miss the bound.
Values may be sent and summed in bfloat16 or wider, within the bound.
A program may use at most 128 MiB of HBM per device.

```python
import jax
import jax.numpy as jnp
from jax import lax

D = 768
HEADS = 12
HD = 64
FF = 3072
LEN = 2048
TOKENS = 16384


def draw_segment_ids(key, part):
    key = jax.random.fold_in(key, 11)
    count_seqs = TOKENS // LEN
    seq_keys = jax.random.split(key, count_seqs)

    def one_sequence(seq_key):
        key_start, key_first, key_last = jax.random.split(seq_key, 3)
        first_cut = jax.random.randint(key_first, (), 2, max(LEN // 8, 3))
        start_cut = jax.random.randint(key_start, (), 1, first_cut)
        last_cut = jax.random.randint(key_last, (), LEN - LEN // 8, LEN)
        position = jnp.arange(LEN, dtype=jnp.int32)
        return (position >= start_cut).astype(jnp.int32) + (position >= first_cut).astype(jnp.int32) + (position >= last_cut).astype(jnp.int32)
    return jax.vmap(one_sequence)(seq_keys).reshape(TOKENS)


def levels(stream_key, shape, cuts, low, largest):
    level, own = 1.0, jax.random.fold_in(stream_key, 6)
    for dim, blocks in cuts:
        heights = jnp.exp(jax.random.uniform(jax.random.fold_in(own, dim), (blocks,), jnp.float32, low / len(cuts), largest / len(cuts)))
        level = level * jnp.repeat(heights, shape[dim] // blocks).reshape([-1 if axis == dim else 1 for axis in range(len(shape))])
    return level


def normal_values(own_key, dims, spread, limit, cuts=(), held_as=jnp.bfloat16):
    values = spread * jax.random.normal(own_key, dims, jnp.float32)
    if cuts:
        values = values * levels(own_key, dims, cuts, -0.22, 0.18)
    return jnp.clip(values, -limit, limit).astype(held_as)


def setup_inputs(seed: int = 0) -> dict:
    keys = jax.random.split(jax.random.key(seed), 16)
    tokens = normal_values(keys[0], (TOKENS, D), 1.0, 6.0, ((0, 32),))
    segment_ids = draw_segment_ids(jax.random.fold_in(keys[15], 71), 0)
    cotangent = normal_values(keys[2], (TOKENS, D), 1.0, 6.0, ((0, 32),))
    norm1_gain = jnp.clip(1.0 + 0.18 * jax.random.normal(keys[3], (D,), jnp.float32), 0.1, 1.9)
    norm1_shift = normal_values(keys[4], (D,), 0.3, 1.75, (), jnp.float32)
    qkv_weight = normal_values(keys[5], (D, 3, D), (D // 2) ** -0.5, 0.3125, ((2, 4),))
    conv_kernel = normal_values(keys[6], (3, 3, D), 0.6, 3.5, ((2, 4),), jnp.float32)
    out_weight = normal_values(keys[7], (D, D), (D // 16) ** -0.5, 0.875, ((0, 4),))
    out_bias = normal_values(keys[8], (D,), 0.3, 1.75, (), jnp.float32)
    norm2_gain = jnp.clip(1.0 + 0.18 * jax.random.normal(keys[9], (D,), jnp.float32), 0.1, 1.9)
    norm2_shift = normal_values(keys[10], (D,), 0.3, 1.75, (), jnp.float32)
    up_weight = normal_values(keys[11], (D, FF), D ** -0.5, 0.21875, ((1, 4),))
    up_bias = normal_values(keys[12], (FF,), 0.5, 3.0, ((0, 4),), jnp.float32)
    down_weight = normal_values(keys[13], (FF, D), FF ** -0.5, 0.109375, ((0, 4),))
    down_bias = normal_values(keys[14], (D,), 0.3, 1.75, (), jnp.float32)
    return {"tokens": tokens, "segment_ids": segment_ids, "cotangent": cotangent, "norm1_gain": norm1_gain, "norm1_shift": norm1_shift, "qkv_weight": qkv_weight, "conv_kernel": conv_kernel, "out_weight": out_weight, "out_bias": out_bias, "norm2_gain": norm2_gain, "norm2_shift": norm2_shift, "up_weight": up_weight, "up_bias": up_bias, "down_weight": down_weight, "down_bias": down_bias}


EPS = 1e-05
HIGH = lax.Precision.HIGHEST

@jax.custom_vjp
def low(v):
    return lax.optimization_barrier(v.astype(jnp.bfloat16)).astype(jnp.float32)

@jax.custom_vjp
def low_back(v):
    return v

def low_keep(v):
    return (low(v), None)

def low_pass(kept, grad):
    return (grad,)

def back_keep(v):
    return (v, None)

def back_low(kept, grad):
    return (low(grad),)
low.defvjp(low_keep, low_pass)
low_back.defvjp(back_keep, back_low)

def layer_norm(values, scale_gain, offset_shift):
    average = lax.optimization_barrier(jnp.mean(values, -1, keepdims=True))
    centred = values - average
    variance = lax.optimization_barrier(jnp.mean(centred * centred, -1, keepdims=True))
    return centred * lax.rsqrt(variance + EPS) * scale_gain + offset_shift

def mixing(projected, kernel, seg_ids):
    convolved = kernel[0] * projected
    for shift_lag in (1, 2):
        earlier = jnp.concatenate([jnp.zeros((shift_lag,) + projected.shape[1:], projected.dtype), projected[:-shift_lag]], 0)
        earlier_ids = jnp.concatenate([jnp.full((shift_lag,), -1, jnp.int32), seg_ids[:-shift_lag]], 0)
        keep_rows = (earlier_ids == seg_ids).astype(projected.dtype)[:, None, None]
        convolved = convolved + kernel[shift_lag] * earlier * keep_rows
    return convolved

def attention(queries, keys_all, values_all, seg_ids):
    block = min(512, LEN)
    scaling = float(HD) ** (-0.5)
    positions = jnp.arange(LEN, dtype=jnp.int32)

    @jax.checkpoint
    def one_block(block_index):
        row_start = block_index * block
        query_block = lax.dynamic_slice_in_dim(queries, row_start, block, 0)
        query_ids = lax.dynamic_slice_in_dim(seg_ids, row_start, block, 0)
        query_pos = row_start + jnp.arange(block, dtype=jnp.int32)
        scores = low_back(jnp.einsum('qhd,khd->hqk', query_block, keys_all, precision=HIGH) * scaling)
        allowed = (query_pos[:, None] >= positions[None, :]) & (query_ids[:, None] == seg_ids[None, :])
        scores = jnp.where(allowed[None], scores, -1e+30)
        row_max = lax.optimization_barrier(jnp.max(scores, -1, keepdims=True))
        exps = jnp.exp(scores - row_max)
        probabilities = exps / lax.optimization_barrier(jnp.sum(exps, -1, keepdims=True))
        return jnp.einsum('hqk,khd->qhd', low(probabilities), values_all, precision=HIGH)
    blocks = lax.map(one_block, jnp.arange(LEN // block, dtype=jnp.int32))
    return blocks.reshape(LEN, HEADS * HD)

def whole_layer(inputs, params, seg_ids):
    gain_one, shift_one, qkv_w, kernel, out_w, out_b, gain_two, shift_two, up_w, up_b, down_w, down_b = params
    first_norm = low(layer_norm(inputs, gain_one, shift_one))
    projected = low_back(jnp.einsum('td,dce->tce', first_norm, qkv_w, precision=HIGH))
    convolved = mixing(projected, kernel, seg_ids)
    queries = low(convolved[:, 0]).reshape(LEN, HEADS, HD)
    keys_all = low(convolved[:, 1]).reshape(LEN, HEADS, HD)
    values_all = low(convolved[:, 2]).reshape(LEN, HEADS, HD)
    attended = attention(queries, keys_all, values_all, seg_ids)
    attended = low_back(low(attended))
    branch = low_back(jnp.dot(attended, out_w, precision=HIGH))
    middle = inputs + branch + out_b
    second_norm = low(layer_norm(middle, gain_two, shift_two))
    hidden = low_back(jnp.dot(second_norm, up_w, precision=HIGH) + up_b)
    active = low(jnp.square(jax.nn.relu(hidden)))
    ffn_out = low_back(jnp.dot(active, down_w, precision=HIGH))
    return middle + ffn_out + down_b

def reference(tokens, segment_ids, cotangent, norm1_gain, norm1_shift, qkv_weight, conv_kernel, out_weight, out_bias, norm2_gain, norm2_shift, up_weight, up_bias, down_weight, down_bias):
    params = (norm1_gain, norm1_shift, qkv_weight.astype(jnp.float32), conv_kernel, out_weight.astype(jnp.float32), out_bias, norm2_gain, norm2_shift, up_weight.astype(jnp.float32), up_bias, down_weight.astype(jnp.float32), down_bias)
    count_seqs = TOKENS // LEN
    inputs = tokens.astype(jnp.float32).reshape(count_seqs, LEN, D)
    id_rows = segment_ids.reshape(count_seqs, LEN)
    cot_rows = cotangent.astype(jnp.float32).reshape(count_seqs, LEN, D)

    def per_sequence(running, sequence_items):
        seq_inputs, seq_ids, seq_cot = sequence_items

        def apply_layer(layer_in, layer_params):
            return whole_layer(layer_in, layer_params, seq_ids)
        layer_out, pullback = jax.vjp(apply_layer, seq_inputs, params)
        grad_in, grad_params = pullback(seq_cot)
        running = jax.tree.map(jnp.add, running, grad_params)
        return (running, (layer_out, grad_in))
    zero_grads = jax.tree.map(jnp.zeros_like, params)
    totals, (outputs, grad_inputs) = lax.scan(per_sequence, zero_grads, (inputs, id_rows, cot_rows))
    return (outputs.reshape(TOKENS, D).astype(jnp.bfloat16), grad_inputs.reshape(TOKENS, D), totals[0], totals[1], totals[2], totals[3], totals[4], totals[5], totals[6], totals[7], totals[8], totals[9], totals[10], totals[11])
```

```python
import functools
import jax, jax.numpy as jnp
from jax import lax
from jax.experimental import pallas as pl
from jax.experimental.pallas import tpu as pltpu
from jax.sharding import PartitionSpec as P_

HD=64
BF=jnp.bfloat16; F32=jnp.float32
BIG=1e30
def nt(a,b): return lax.dot_general(a,b,(((1,),(1,)),((),())),preferred_element_type=F32)
def tn(a,b): return lax.dot_general(a,b,(((0,),(0,)),((),())),preferred_element_type=F32)
def nn(a,b): return jnp.dot(a,b,preferred_element_type=F32)

def keep_rows(ids):
    n=ids.shape[1]
    pos=lax.broadcasted_iota(jnp.int32,(1,n),1)
    out=[]
    for j in (1,2):
        prev=pltpu.roll(ids,j,1)
        out.append(jnp.where((prev==ids)&(pos>=j),1.0,0.0).astype(F32))
    return out

def mix(v,ck,keeps,r):
    out=ck[r:r+HD,0:1]*v
    for j in (1,2):
        out=out+ck[r:r+HD,j:j+1]*(pltpu.roll(v,j,1)*keeps[j-1])
    return out

def feats(ids,rows,kind):
    n=ids.shape[1]
    r=lax.broadcasted_iota(jnp.int32,(rows,n),0)
    idb=jnp.broadcast_to(ids,(rows,n))
    if kind=="q":
        return jnp.where((r<4)&(idb!=r),-BIG,0.0).astype(F32)
    return jnp.where(((r<4)&(idb==r))|((r>=4)&(r<7)),1.0,0.0).astype(F32)

def fwd_kernel(n,heads,bq,x_ref,wt_ref,ck_ref,ids_ref, att_ref,proj_ref,lse_ref,of_ref, qt,kk,vt):
    for s in range(0,n,512):
        proj_ref[:,s:s+512]=nt(wt_ref[...],x_ref[s:s+512,:])
    ids=ids_ref[...]
    keeps=keep_rows(ids)
    fq=feats(ids,64,"q").astype(BF); fk=feats(ids,64,"k")
    lw=heads*HD
    ck=ck_ref[...]
    for h in range(heads):
        r=h*HD
        q=mix(proj_ref[r:r+HD,:],ck,keeps,r)
        qt[h,0:64,:]=(q.astype(BF).astype(F32)*0.125).astype(BF)
        qt[h,64:128,:]=fq
        r=lw+h*HD
        k=mix(proj_ref[r:r+HD,:],ck,keeps,r)
        kt=jnp.concatenate([k,fk],0)
        kk[h]=kt.T.astype(BF)
        r=2*lw+h*HD
        v=mix(proj_ref[r:r+HD,:],ck,keeps,r)
        vt[h,0:64,:]=v.astype(BF)
        vt[h,64:80,:]=jnp.ones((16,n),BF)
    tri=lax.broadcasted_iota(jnp.int32,(bq,bq),0)<=lax.broadcasted_iota(jnp.int32,(bq,bq),1)
    def head(h,_):
        for iq in range(n//bq):
            qs=iq*bq
            qb=qt[h,:,qs:qs+bq]
            ss=[]
            for j in range(iq+1):
                s=nn(kk[h,j*bq:(j+1)*bq,:],qb)
                if j==iq: s=jnp.where(tri,s,-BIG)
                ss.append(s)
            m=jnp.max(ss[0],axis=0,keepdims=True)
            for s in ss[1:]: m=jnp.maximum(m,jnp.max(s,axis=0,keepdims=True))
            o=jnp.zeros((80,bq),F32)
            for j,s in enumerate(ss):
                p=jnp.exp(s-m).astype(BF)
                o=o+nn(vt[h,:,j*bq:(j+1)*bq],p)
            l=o[64:65,:]
            of=o[0:64,:]/l
            rr=pl.multiple_of(h*HD,HD)
            of_ref[pl.ds(rr,HD),qs:qs+bq]=of
            att_ref[qs//512,pl.ds(rr,HD),qs%512:qs%512+bq]=of.astype(BF)
            lse_ref[h,:,qs:qs+bq]=jnp.broadcast_to(m+jnp.log(l),(8,bq))
        return 0
    lax.fori_loop(0,heads,head,0)

def attn_fwd(x,wt,ck,ids,bq=256):
    n,heads=x.shape[0],wt.shape[0]//3//HD
    lw=heads*HD
    vm=pl.BlockSpec(memory_space=pltpu.VMEM)
    return pl.pallas_call(
        functools.partial(fwd_kernel,n,heads,bq),
        out_shape=(jax.ShapeDtypeStruct((n//512,lw,512),BF),jax.ShapeDtypeStruct((3*lw,n),F32),jax.ShapeDtypeStruct((heads,8,n),F32),jax.ShapeDtypeStruct((lw,n),F32)),
        in_specs=[vm]*4,out_specs=(vm,)*4,
        scratch_shapes=[pltpu.VMEM((heads,128,n),BF),pltpu.VMEM((heads,n,128),BF),pltpu.VMEM((heads,80,n),BF)],
        compiler_params=pltpu.CompilerParams(vmem_limit_bytes=60*2**20),
    )(x,wt,ck,ids)

def split3(x):
    hi=x.astype(BF).astype(F32); r=x-hi; mid=r.astype(BF).astype(F32); lo=r-mid
    return hi,mid,lo

def bwd_kernel(n,heads,B,x_ref,wt_ref,ck_ref,ids_ref,proj_ref,lse_ref,of_ref,ga_ref, gf_ref,gw_ref,gc_ref, qt,qn,kk,kt_s,vn,dot_s,don,dq,dkv,gconv,gp):
    ids=ids_ref[...]
    keeps=keep_rows(ids)
    fq=feats(ids,64,"q"); fk=feats(ids,64,"k")
    r8=lax.broadcasted_iota(jnp.int32,(64,n),0)
    lw=heads*HD
    ck=ck_ref[...]
    zl=jnp.zeros((64,n),F32)
    for h in range(heads):
        r=h*HD
        q=mix(proj_ref[r:r+HD,:],ck,keeps,r).astype(BF).astype(F32)*0.125
        hi,mid,lo=split3(-lse_ref[h,0:1,:])
        f=fq+jnp.where(r8==4,hi,0.0)+jnp.where(r8==5,mid,0.0)+jnp.where(r8==6,lo,0.0)
        qt[h,0:64,:]=q.astype(BF); qt[h,64:128,:]=f.astype(BF)
        qn[h]=jnp.concatenate([zl,q],0).T.astype(BF)
        r=lw+h*HD
        k=mix(proj_ref[r:r+HD,:],ck,keeps,r)
        kt_s[h]=k.astype(BF)
        kk[h]=jnp.concatenate([k,fk],0).T.astype(BF)
        r=2*lw+h*HD
        v=mix(proj_ref[r:r+HD,:],ck,keeps,r)
        vn[h]=jnp.concatenate([v,jnp.where(r8<3,1.0,0.0)],0).T.astype(BF)
        do=jnp.concatenate([ga_ref[s,h*HD:(h+1)*HD,:] for s in range(n//512)],axis=1).astype(F32)
        D=jnp.sum(do*of_ref[h*HD:(h+1)*HD,:],axis=0,keepdims=True)
        hi,mid,lo=split3(-D)
        f=jnp.where(r8==0,hi,0.0)+jnp.where(r8==1,mid,0.0)+jnp.where(r8==2,lo,0.0)
        dot_s[h,0:64,:]=do.astype(BF); dot_s[h,64:128,:]=f.astype(BF)
        don[h]=jnp.concatenate([do,zl],0).T.astype(BF)
    tri=lax.broadcasted_iota(jnp.int32,(B,B),0)<=lax.broadcasted_iota(jnp.int32,(B,B),1)
    nb=n//B
    def head(h,_):
        for j in range(nb):
            js=j*B
            acc=jnp.zeros((B,128),F32)
            for i in range(j,nb):
                s_=i*B
                st=nn(kk[h,js:js+B,:],qt[h,:,s_:s_+B])
                p=jnp.exp(st)
                if i==j: p=jnp.where(tri,p,0.0)
                dp=nn(vn[h,js:js+B,:],dot_s[h,:,s_:s_+B])
                ds=(p*dp).astype(BF)
                acc=acc+nn(p.astype(BF),don[h,s_:s_+B,:])+nn(ds,qn[h,s_:s_+B,:])
                t=nn(kt_s[h,:,js:js+B],ds)
                if j==0: dq[:,s_:s_+B]=t
                else: dq[:,s_:s_+B]+=t
            dkv[js:js+B,:]=acc
        r=pl.multiple_of(h*HD,HD)
        gconv[pl.ds(r,HD),:]=dq[...]*0.125
        tt=dkv[...].T
        gconv[pl.ds(pl.multiple_of(2*lw+h*HD,HD),HD),:]=tt[0:64]
        gconv[pl.ds(pl.multiple_of(lw+h*HD,HD),HD),:]=tt[64:128]
        return 0
    lax.fori_loop(0,heads,head,0)
    for b in range(3*heads):
        r=b*HD
        g=gconv[r:r+HD,:]
        pr=proj_ref[r:r+HD,:]
        cols=[jnp.sum(g*pr,axis=1,keepdims=True)]
        o=ck[r:r+HD,0:1]*g
        for jj in (1,2):
            kg=g*keeps[jj-1]
            cols.append(jnp.sum(kg*pltpu.roll(pr,jj,1),axis=1,keepdims=True))
            o=o+ck[r:r+HD,jj:jj+1]*pltpu.roll(kg,n-jj,1)
        gp[r:r+HD,:]=o.astype(BF)
        gc_ref[r:r+HD,:]=jnp.concatenate(cols,1)
    gw_ref[...]=nn(gp[...],x_ref[...]).astype(BF)
    for s in range(0,n,512):
        gf_ref[s:s+512,:]=tn(gp[:,s:s+512],wt_ref[...]).astype(BF)

def attn_bwd(x,wt,ck,ids,proj,lse,of,ga,B=256):
    n,heads=x.shape[0],wt.shape[0]//3//HD
    lw=heads*HD
    vm=pl.BlockSpec(memory_space=pltpu.VMEM)
    V=pltpu.VMEM
    return pl.pallas_call(
        functools.partial(bwd_kernel,n,heads,B),
        out_shape=(jax.ShapeDtypeStruct((n,768),BF),jax.ShapeDtypeStruct((3*lw,768),BF),jax.ShapeDtypeStruct((3*lw,3),F32)),
        in_specs=[vm]*8,out_specs=(vm,)*3,
        scratch_shapes=[V((heads,128,n),BF),V((heads,n,128),BF),V((heads,n,128),BF),V((heads,64,n),BF),V((heads,n,128),BF),V((heads,128,n),BF),V((heads,n,128),BF),V((64,n),F32),V((n,128),F32),V((3*lw,n),F32),V((3*lw,n),BF)],
        compiler_params=pltpu.CompilerParams(vmem_limit_bytes=60*2**20),
    )(x,wt,ck,ids,proj,lse,of,ga)
EPS=1e-5
def ln(x):
    mu=jnp.mean(x,-1,keepdims=True)
    c=x-mu
    inv=lax.rsqrt(jnp.mean(c*c,-1,keepdims=True)+EPS)
    return c*inv,inv
def ln_back(g,unit,inv,gain):
    s=g*gain
    return (s-jnp.mean(s,-1,keepdims=True)-unit*jnp.mean(s*unit,-1,keepdims=True))*inv
def ffn_kernel(att_ref,tok_ref,cot_ref,ow_ref,up_ref,dn_ref,outb,g2,s2,upb,dnb,
               res_ref,gm_ref,ga_ref,gow_ref,gup_ref,gdn_ref,small_ref,gupb_ref, sec,act,gh,gsec):
    T=up_ref.shape[0]
    unit_mid=tok_ref[...].astype(F32)+tn(att_ref[...],ow_ref[...])+outb[...]
    unit,inv=ln(unit_mid)
    sec[...]=(unit*g2[...]+s2[...]).astype(BF)
    cot=cot_ref[...]
    gsec[...]=jnp.zeros_like(gsec)
    def blk(b,_):
        rl=jnp.maximum(nn(sec[...],up_ref[b])+upb[pl.ds(b,1),:],0.0)
        act[b]=(rl*rl).astype(BF)
        g=(nt(cot,dn_ref[b])*(2.0*rl)).astype(BF)
        gh[b]=g
        gupb_ref[pl.ds(b,1),:]=jnp.sum(g.astype(F32),0,keepdims=True)
        gsec[...]+=nt(g,up_ref[b])
        return 0
    lax.fori_loop(0,T,blk,0)
    gs=gsec[...]
    cf=cot.astype(F32)
    gm=cf+ln_back(gs,unit,inv,g2[...])
    gm_ref[...]=gm
    gmb=gm.astype(BF)
    lw=ow_ref.shape[0]//T
    for m in range(T):
        ga_ref[m]=nt(ow_ref[m*lw:(m+1)*lw,:],gmb).astype(BF)
    small_ref[0:1]=jnp.sum(gm,0,keepdims=True)
    small_ref[1:2]=jnp.sum(gs*unit,0,keepdims=True)
    small_ref[2:3]=jnp.sum(gs,0,keepdims=True)
    small_ref[3:4]=jnp.sum(cf,0,keepdims=True)
    small_ref[4:8]=jnp.zeros((4,cf.shape[1]),F32)
    gow_ref[...]=nn(att_ref[...],gmb).astype(BF)
    gsec[...]=unit_mid+dnb[...]
    def blk2(b,_):
        gsec[...]+=nn(act[b],dn_ref[b])
        gup_ref[b]=tn(sec[...],gh[b]).astype(BF)
        gdn_ref[b]=tn(act[b],cot_ref[...]).astype(BF)
        return 0
    lax.fori_loop(0,T,blk2,0)
    res_ref[...]=gsec[...].astype(BF)

def ffn(att,tok,cot,ow,up,dn,outb,g2,s2,upb,dnb):
    n,D=tok.shape; T=up.shape[0]; lw=ow.shape[0]//T; fb=up.shape[2]
    vm=pl.BlockSpec(memory_space=pltpu.VMEM); V=pltpu.VMEM
    S=jax.ShapeDtypeStruct
    return pl.pallas_call(ffn_kernel,
        out_shape=(S((n,D),BF),S((n,D),F32),S((T,lw,n),BF),S(ow.shape,BF),S(up.shape,BF),S(dn.shape,BF),S((8,D),F32),S((T,fb),F32)),
        in_specs=[vm]*11,out_specs=(vm,)*8,
        scratch_shapes=[V((n,D),BF),V((T,n,fb),BF),V((T,n,fb),BF),V((n,D),F32)],
        compiler_params=pltpu.CompilerParams(vmem_limit_bytes=60*2**20),
    )(att,tok,cot,ow,up,dn,outb,g2,s2,upb,dnb)
MESH=pl.DeviceIdType.MESH

class Place:
    def __init__(self):
        d=lax.axis_index("dp"); t=lax.axis_index("tensor")
        self.d,self.t=d,t
        b=d%2; p=t//2; q=t%2; base=d-b
        self.b,self.p,self.q=b,p,q
        self.member=2*q+b
        self.quarter=(d//2)%4
        self.sib=(base+1-b,t)
        self.opp=(d,2*p+1-q)
        self.cross=(base+1-b,2*p+1-q)
        self.other=(d,2*(1-p)+q)
        self.dest=(base+q,2*b+p)
        self.source=(base+p,2*q+b)
        self.fixed=jnp.logical_and(b==p,b==q)
        dx=d+2-4*((d//2)%2); dy=d+4-8*((d//4)%2)
        self.x=(dx,t); self.y=(dy,t); self.xy=(dx+dy-d,t)
    def zed(self,r): return (self.d,(self.t+r)%4)
    def column(self):
        base=self.d-self.b
        out=[]
        for r in range(1,4):
            out.append((self.d,(self.t+r)%4))
        for r in range(4):
            out.append((base+1-self.b,(self.t+r)%4))
        return out

def meet(peers):
    bar=pltpu.get_barrier_semaphore()
    for dev in peers:
        pl.semaphore_signal(bar,inc=1,device_id=dev,device_id_type=MESH)
    pl.semaphore_wait(bar,len(peers))

class Net:
    def __init__(self,send,recv):
        self.send,self.recv,self.k=send,recv,0
    def to(self,src,dst,dev):
        k=self.k; self.k+=1
        return pltpu.make_async_remote_copy(src_ref=src,dst_ref=dst,send_sem=self.send.at[k],recv_sem=self.recv.at[k],device_id=dev,device_id_type=MESH)

class Swap:
    def __init__(self,net,src,dst,dev,fixed):
        self.r=net.to(src,dst,dev); self.fixed=fixed
        self.l=pltpu.make_async_copy(src,dst,net.recv.at[net.k-1])
    def start(self):
        pl.when(jnp.logical_not(self.fixed))(self.r.start)
        pl.when(self.fixed)(self.l.start)
    def wait_recv(self): self.l.wait()
    def wait_send(self): pl.when(jnp.logical_not(self.fixed))(self.r.wait_send)

def rows(ref,start,size): return ref.at[pl.ds(start,size)]

NC=2
def gather_kernel(tok,ids,cot,wt,ck,ow,up,dn,upb,g1,s1,
                  x_all,ids_all,tok_p,cot_p,wt_p,ck_p,ow_a,up_a,dn_a,upb_a,
                  tokv,xn,send,recv,lsem):
    P=Place()
    meet(P.column()+[P.x,P.y,P.xy])
    net=Net(send,recv)
    n=tok.shape[0]; D=tok.shape[1]
    R=n//NC; H=R//2
    def swap(src,dst): return Swap(net,src,dst,P.dest,P.fixed)
    tk=[swap(rows(tok,k*R,R),rows(tokv,k*R,R)) for k in range(NC)]
    for c in tk: c.start()
    Q=wt.shape[0]//4
    w0=pl.multiple_of(P.quarter*Q,16)
    wq=swap(rows(wt,w0,Q),rows(wt_p,w0,Q)); wq.start()
    ckc=swap(ck,ck_p); ckc.start()
    idc=swap(ids,ids_all.at[4]); idc.start()
    def part(ref,tt):
        L=ref.shape[2]//2; r=ref.shape[1]//4
        return ref.at[tt,pl.ds(pl.multiple_of(P.quarter*r,16),r),pl.ds(pl.multiple_of(P.b*L,128),L)]
    def part_in(ref):
        L=ref.shape[1]//2; r=ref.shape[0]//4
        return ref.at[pl.ds(pl.multiple_of(P.quarter*r,16),r),pl.ds(pl.multiple_of(P.b*L,128),L)]
    ins=(ow,up,dn); alls=(ow_a,up_a,dn_a)
    own=[pltpu.make_async_copy(part_in(a),part(b,P.t),lsem.at[j]) for j,(a,b) in enumerate(zip(ins,alls))]
    for c in own: c.start()
    bias=[net.to(upb,upb_a.at[P.t],P.zed(r)) for r in (1,2,3)]
    for c in bias: c.start()
    ownb=pltpu.make_async_copy(upb,upb_a.at[P.t],lsem.at[3]); ownb.start()
    m=P.member
    halves={}
    for k in range(NC):
        tk[k].wait_recv()
        unit,_=ln(tokv[k*R:(k+1)*R,:].astype(F32))
        xn[k*R:(k+1)*R,:]=(unit*g1[...]+s1[...]).astype(BF)
        oh=pl.multiple_of(k*R+P.b*H,16); xh=pl.multiple_of(k*R+(1-P.b)*H,16)
        cs=[net.to(rows(xn,oh,H),x_all.at[m,pl.ds(oh,H)],P.opp),
            net.to(rows(xn,xh,H),x_all.at[m,pl.ds(xh,H)],P.cross),
            net.to(rows(xn,k*R,R),x_all.at[m,pl.ds(k*R,R)],P.sib)]
        for c in cs: c.start()
        halves[k]=cs
    ownx=pltpu.make_async_copy(xn,x_all.at[m],lsem.at[4]); ownx.start()
    ownt=pltpu.make_async_copy(tokv,tok_p,lsem.at[5]); ownt.start()
    cc=swap(cot,cot_p); cc.start()
    zs={}
    for r in (1,2,3):
        zs[r]=[net.to(part_in(a),part(b,P.t),P.zed(4-r)) for a,b in zip(ins,alls)]
        for c in zs[r]: c.start()
    idc.wait_recv()
    idown=pltpu.make_async_copy(ids_all.at[4],ids_all.at[m],lsem.at[6]); idown.start()
    idg=[net.to(ids_all.at[4],ids_all.at[m],dev) for dev in (P.sib,P.opp,P.cross)]
    for c in idg: c.start()
    wq.wait_recv()
    wf=[net.to(rows(wt_p,w0,Q),rows(wt_p,w0,Q),dev) for dev in (P.x,P.y,P.xy)]
    for c in wf: c.start()
    fw=[]
    om=2*(1-P.q)+P.b; xm=2*(1-P.q)+1-P.b
    for k in range(NC):
        oh=pl.multiple_of(k*R+P.b*H,16)
        for src,mm in ((0,om),(1,xm)):
            halves[k][src].wait_recv()
        a=net.to(x_all.at[om,pl.ds(oh,H)],x_all.at[om,pl.ds(oh,H)],P.sib)
        b=net.to(x_all.at[xm,pl.ds(oh,H)],x_all.at[xm,pl.ds(oh,H)],P.sib)
        a.start(); b.start(); fw+=[a,b]
    tail=[]
    for c in own: c.wait()
    for r in range(4):
        tt=(P.t+r)%4
        if r:
            for c in zs[r]: c.wait_recv()
        blk=[part(a,tt) for a in alls]
        one={}
        for name,dev in (("x",P.x),("y",P.y),("s",P.sib)):
            one[name]=[net.to(z,z,dev) for z in blk]
            for c in one[name]: c.start()
        def theirs(dq):
            out=[]
            for a in alls:
                L=a.shape[2]//2; rr=a.shape[1]//4
                out.append(a.at[tt,pl.ds(pl.multiple_of(dq*rr,16),rr),pl.ds(pl.multiple_of(P.b*L,128),L)])
            return out
        qx=(P.x[0]//2)%4; qy=(P.y[0]//2)%4; qd=(P.xy[0]//2)%4
        bx=theirs(qx); by=theirs(qy); bd=theirs(qd)
        for c in one["x"]: c.wait_recv()
        dg=[net.to(bx[0],bx[0],P.y),net.to(bx[1],bx[1],P.y)]
        for c in dg: c.start()
        sx=[net.to(z,z,P.sib) for z in bx]
        for c in sx: c.start()
        for c in one["y"]: c.wait_recv()
        dh=[net.to(by[2],by[2],P.x)]
        for c in dh: c.start()
        sy=[net.to(z,z,P.sib) for z in by]
        for c in sy: c.start()
        for c in dg+dh: c.wait_recv()
        sd=[net.to(z,z,P.sib) for z in bd]
        for c in sd: c.start()
        tail.append((one,dg+dh,sx+sy+sd))
    for r in range(4):
        one,dd,ss=tail[r]
        for c in one["s"]+ss: c.wait_recv()
        for c in one["x"]+one["y"]+one["s"]+dd+ss: c.wait_send()
        if r:
            for c in zs[r]: c.wait_send()
    for c in bias: c.wait()
    for c in idg: c.wait()
    for c in wf: c.wait()
    for k in range(NC):
        halves[k][2].wait_recv()
        for c in halves[k]: c.wait_send()
    for c in fw: c.wait()
    for c in tk+[wq,ckc,idc,cc]: c.wait_send()
    ckc.wait_recv(); cc.wait_recv()
    for c in (ownb,ownx,ownt,idown): c.wait()

def gather(tok,ids,cot,wt,ck,ow,up,dn,upb,g1,s1):
    n,D=tok.shape; S=jax.ShapeDtypeStruct
    any_=pl.BlockSpec(memory_space=pl.ANY); vm=pl.BlockSpec(memory_space=pltpu.VMEM)
    outs=(S((4,n,D),BF),S((5,1,n),jnp.int32),S((n,D),BF),S((n,D),BF),S(wt.shape,BF),S(ck.shape,F32),
          S((4,)+ow.shape,BF),S((4,)+up.shape,BF),S((4,)+dn.shape,BF),S((4,)+upb.shape,F32))
    return pl.pallas_call(gather_kernel,out_shape=outs,
        in_specs=[any_]*9+[vm]*2,out_specs=(any_,)*len(outs),
        scratch_shapes=[pltpu.VMEM((n,D),BF),pltpu.VMEM((n,D),BF),pltpu.SemaphoreType.DMA((140,)),pltpu.SemaphoreType.DMA((140,)),pltpu.SemaphoreType.DMA((8,))],
        compiler_params=pltpu.CompilerParams(collective_id=0,has_side_effects=True,vmem_limit_bytes=32*2**20),
        name="gather_inputs",
    )(tok,ids,cot,wt,ck,ow,up,dn,upb,g1,s1)

def lanes(start,size): return pl.ds(pl.multiple_of(start,128),size)
def rws(start,size): return pl.ds(pl.multiple_of(start,16),size)

def exchange_kernel(src,dst,send,recv,lsem):
    P=Place(); meet([P.sib,P.opp,P.cross])
    net=Net(send,recv); m=P.member
    ms=[2*P.q+1-P.b,2*(1-P.q)+P.b,2*(1-P.q)+1-P.b]
    cs=[net.to(src.at[k],dst.at[m],dev) for k,dev in zip(ms,(P.sib,P.opp,P.cross))]
    for c in cs[1:]+cs[:1]: c.start()
    own=pltpu.make_async_copy(src.at[m],dst.at[m],lsem.at[0]); own.start()
    for c in cs: c.wait()
    own.wait()

def exchange(x,cid,name):
    any_=pl.BlockSpec(memory_space=pl.ANY)
    return pl.pallas_call(exchange_kernel,out_shape=jax.ShapeDtypeStruct(x.shape,x.dtype),in_specs=[any_],out_specs=any_,
        scratch_shapes=[pltpu.SemaphoreType.DMA((4,)),pltpu.SemaphoreType.DMA((4,)),pltpu.SemaphoreType.DMA((1,))],
        compiler_params=pltpu.CompilerParams(collective_id=cid,has_side_effects=True),name=name)(x)

def reduce_kernel(gf,gm,tok,res,gow,gup,gdn,gw,small,g1,
                  res_o,gt_o,ow_o,up_o,dn_o,w_o,small_o,
                  land1,land2,land3,acc,gtv,
                  c_ow,c_up,c_dn,x_ow,x_up,y_dn,z_ow,z_up,z_dn,w1,w2,w3,f_ow,f_up,f_dn,f_w,sl,send,recv,lsem):
    P=Place(); meet(P.column()+[P.x,P.y,P.xy])
    net=Net(send,recv); m=P.member; b=P.b
    n=gm.shape[0]; D=gm.shape[1]; H=n//2; L=D//2
    f=lambda v: v.astype(F32)
    started=[]
    def push(src,dst,dev):
        c=net.to(src,dst,dev); c.start(); started.append(c); return c
    rs=Swap(net,res,res_o,P.source,P.fixed); rs.start()
    h0=pl.multiple_of(b*H,16); h1=pl.multiple_of((1-b)*H,16)
    e1=push(gf.at[:,pl.ds(h1,H),:],land1,P.sib)
    lo=P.b*L; lx=(1-P.b)*L
    cs=[push(a.at[:,:,lanes(lx,L)],z,P.sib) for a,z in ((gow,c_ow),(gup,c_up),(gdn,c_dn))]
    qr=P.quarter; qx=(P.x[0]//2)%4; qy=(P.y[0]//2)%4; qd=(P.xy[0]//2)%4
    def side(ref,k,rows_): return ref.at[:,rws(k*rows_,rows_),:]
    Q=gw.shape[0]//4
    wx=[push(gw.at[rws(k*Q,Q)],w1.at[j],P.x) for j,k in ((0,qx),(1,qd))]
    e1.wait_recv()
    for s in range(4):
        land1[s]=(f(land1[s])+f(gf[s,pl.ds(h0,H),:])).astype(BF)
    om=2*(1-P.q)
    e2=push(land1.at[pl.ds(om,2)],land2,P.opp)
    for c,a,z in zip(cs,(gow,gup,gdn),(c_ow,c_up,c_dn)):
        c.wait_recv()
        def add(t,_,a=a,z=z):
            z[t]=(f(z[t])+f(a[t,:,lanes(lo,L)])).astype(BF); return 0
        lax.fori_loop(0,4,add,0)
    ro,ru=gow.shape[1]//4,gup.shape[1]//4
    p1=[push(side(c_ow,k,ro),x_ow.at[j],P.x) for j,k in ((0,qx),(1,qd))]
    p1+=[push(side(c_up,k,ru),x_up.at[j],P.x) for j,k in ((0,qx),(1,qd))]
    p2=[push(side(c_dn,k,ru),y_dn.at[j],P.y) for j,k in ((0,qy),(1,qd))]
    e2.wait_recv()
    land2[0]=(f(land2[0])+f(land1[2*P.q])).astype(BF)
    land2[1]=(f(land2[1])+f(land1[2*P.q+1])).astype(BF)
    e3=push(land2.at[1-b],land3,P.sib)
    for c in wx: c.wait_recv()
    for j,k in ((0,qr),(1,qy)):
        w1[j]=(f(w1[j])+f(gw[rws(k*Q,Q)])).astype(BF)
    wy=push(w1.at[1],w2,P.y)
    e3.wait_recv()
    gtv[pl.ds(h0,H),:]=f(land2[b]); gtv[pl.ds(h1,H),:]=f(land3[...])
    unit,inv=ln(f(tok[...]))
    g=gtv[...]
    sl[5]=small[...]
    sl[5,4:5]=jnp.sum(g*unit,0,keepdims=True)
    sl[5,5:6]=jnp.sum(g,0,keepdims=True)
    acc[...]=(gm[...]+ln_back(g,unit,inv,g1[...])).astype(BF)
    gs=Swap(net,acc,gt_o,P.source,P.fixed); gs.start()
    sp=push(sl.at[5],sl.at[0],P.sib)
    for c in p1: c.wait_recv()
    for z,c0,r_ in ((x_ow,c_ow,ro),(x_up,c_up,ru)):
        for j,k in ((0,qr),(1,qy)):
            z[j]=(f(z[j])+f(c0[:,rws(k*r_,r_),:])).astype(BF)
    p3=[push(x_ow.at[1],z_ow.at[0],P.y),push(x_up.at[1],z_up.at[0],P.y)]
    for c in p2: c.wait_recv()
    for j,k in ((0,qr),(1,qx)):
        y_dn[j]=(f(y_dn[j])+f(c_dn[:,rws(k*ru,ru),:])).astype(BF)
    p4=push(y_dn.at[1],z_dn.at[0],P.x)
    sp.wait_recv(); sl[0]=sl[0]+sl[5]
    sp=push(sl.at[0],sl.at[1],P.x)
    wy.wait_recv()
    w1[0]=(f(w1[0])+f(w2[...])).astype(BF)
    wz=push(w1.at[0,:,lanes((1-P.p)*L,L)],w3.at[0],P.other)
    sp.wait_recv(); sl[1]=sl[1]+sl[0]
    sp=push(sl.at[1],sl.at[2],P.y)
    for c in p3+[p4]: c.wait_recv()
    zz=[]
    for z,own in ((z_ow,x_ow),(z_up,x_up),(z_dn,y_dn)):
        z[0]=(f(z[0])+f(own[0])).astype(BF)
        zz.append([push(z.at[0,1-P.q],z.at[1,0],P.opp),push(z.at[0,3-P.q],z.at[1,1],P.opp)])
    wz.wait_recv()
    w3[0]=(f(w3[0])+f(w1[0,:,lanes(P.p*L,L)])).astype(BF)
    ws=Swap(net,w3.at[0],w3.at[1],P.source,P.fixed); ws.start()
    sp.wait_recv(); sl[2]=sl[2]+sl[1]
    sp=push(sl.at[2],sl.at[3],P.opp)
    z2=[]
    for (z,fin),cc in zip(((z_ow,f_ow),(z_up,f_up),(z_dn,f_dn)),zz):
        for c in cc: c.wait_recv()
        for k in range(2):
            z[1,k]=(f(z[1,k])+f(z[0,2*k+P.q])).astype(BF)
        z2.append(push(z.at[1,1-P.p],fin.at[0],P.other))
    sp.wait_recv(); sl[3]=sl[3]+sl[2]
    sp=push(sl.at[3],sl.at[4],P.other)
    outs=((ow_o,f_ow,ro),(up_o,f_up,ru),(dn_o,f_dn,ru))
    def place(o,k,r_): return o.at[rws(k*r_,r_),lanes(lo,L)]
    ag=[]
    for (z,(o,fin,r_)),c in zip(zip((z_ow,z_up,z_dn),outs),z2):
        c.wait_recv()
        fin[1]=(f(fin[0])+f(z[1,P.p])).astype(BF)
        ag.append((o,fin.at[1],r_))
    ws.wait_recv()
    ag.append((w_o,w3.at[1],Q))
    ag=ag[::-1]
    own=[]; sx=[];sy=[];ss=[]
    for j,(o,s_,r_) in enumerate(ag):
        c=pltpu.make_async_copy(s_,place(o,qr,r_),lsem.at[j]); c.start(); own.append(c)
        sx.append(push(s_,place(o,qr,r_),P.x)); sy.append(push(s_,place(o,qr,r_),P.y)); ss.append(push(s_,place(o,qr,r_),P.sib))
    dg=[]
    for j,(o,s_,r_) in enumerate(ag):
        sx[j].wait_recv()
        if j%2==0: dg.append(push(place(o,qx,r_),place(o,qx,r_),P.y))
        ss.append(push(place(o,qx,r_),place(o,qx,r_),P.sib))
        sy[j].wait_recv()
        if j%2==1: dg.append(push(place(o,qy,r_),place(o,qy,r_),P.x))
        ss.append(push(place(o,qy,r_),place(o,qy,r_),P.sib))
    sp.wait_recv()
    small_o[...]=sl[4]+sl[3]
    for j,(o,s_,r_) in enumerate(ag):
        dg[j].wait_recv()
        ss.append(push(place(o,qd,r_),place(o,qd,r_),P.sib))
    for c in ss: c.wait_recv()
    for c in own: c.wait()
    for c in started: c.wait_send()
    for c in (rs,gs,ws): c.wait_send()
    rs.wait_recv(); gs.wait_recv()

def reduce(gf,gm,tok,res,gow,gup,gdn,gw,small,g1):
    S=jax.ShapeDtypeStruct; V=pltpu.VMEM
    any_=pl.BlockSpec(memory_space=pl.ANY); vm=pl.BlockSpec(memory_space=pltpu.VMEM)
    n,D=gm.shape; H=n//2; L=D//2
    a,bq=gow.shape[1],gup.shape[1]; w=gw.shape[0]; k=small.shape[0]
    outs=(S((n,D),BF),S((n,D),BF),S((a,D),BF),S((bq,D),BF),S((bq,D),BF),S((w,D),BF),S((k,D),F32))
    sc=[V((4,H,D),BF),V((2,H,D),BF),V((H,D),BF),V((n,D),BF),V((n,D),F32),
        V((4,a,L),BF),V((4,bq,L),BF),V((4,bq,L),BF),
        V((2,4,a//4,L),BF),V((2,4,bq//4,L),BF),V((2,4,bq//4,L),BF),
        V((2,4,a//4,L),BF),V((2,4,bq//4,L),BF),V((2,4,bq//4,L),BF),
        V((2,w//4,D),BF),V((w//4,D),BF),V((2,w//4,L),BF),
        V((2,a//4,L),BF),V((2,bq//4,L),BF),V((2,bq//4,L),BF),V((w//4,L),BF),V((6,k,D),F32),
        pltpu.SemaphoreType.DMA((80,)),pltpu.SemaphoreType.DMA((80,)),pltpu.SemaphoreType.DMA((8,))]
    return pl.pallas_call(reduce_kernel,out_shape=outs,
        in_specs=[vm,vm,vm,any_]+[vm]*6,out_specs=(any_,)*6+(vm,),scratch_shapes=sc,
        compiler_params=pltpu.CompilerParams(collective_id=3,has_side_effects=True,vmem_limit_bytes=60*2**20),name="reduce_gradients",
    )(gf,gm,tok,res,gow,gup,gdn,gw,small,g1)


def per_device(planes, tokens, segment_ids, cotangent, norm1_gain, norm1_shift, qkv_weight, conv_kernel, out_weight, out_bias, norm2_gain, norm2_shift, up_weight, up_bias, down_weight, down_bias):
    n, D = tokens.shape
    lw = qkv_weight.shape[2]
    row = lambda v: v.reshape(1, -1)
    wt = jnp.transpose(qkv_weight, (1, 2, 0)).reshape(3 * lw, D)
    x_all, ids_all, tok, cot, wtp, ckp, ow, up, dn, upb = gather(
        tokens, row(segment_ids), cotangent, wt, conv_kernel, out_weight, up_weight, down_weight, row(up_bias), row(norm1_gain), row(norm1_shift))
    x = x_all.reshape(4 * n, D)
    ids = ids_all[:4].reshape(1, 4 * n)
    ck = jnp.transpose(ckp, (1, 2, 0)).reshape(3 * lw, 3)
    att, proj, lse, of = attn_fwd(x, wtp, ck, ids, bq=512)
    att = exchange(att, 1, "exchange_attended").reshape(4 * lw, n)
    res, gm, ga, gow, gup, gdn, s4, gupb = ffn(
        att, tok, cot, ow.reshape(4 * lw, D), up, dn, row(out_bias), row(norm2_gain), row(norm2_shift), upb.reshape(4, -1), row(down_bias))
    ga = exchange(ga, 2, "exchange_grads")
    gf, gw, gc = attn_bwd(x, wtp, ck, ids, proj, lse, of, ga, B=512)
    d, t = lax.axis_index("dp"), lax.axis_index("tensor")
    member = 2 * (t % 2) + d % 2
    conv = jnp.zeros((4, 3, D), F32)
    conv = lax.dynamic_update_slice(conv, jnp.pad(gc.T, ((0, 0), (0, D - 3 * lw)))[None], (member, 0, 0)).reshape(12, D)
    small = jnp.concatenate([s4[:6], gupb, conv, jnp.zeros((2, D), F32)], 0)
    res, gt, ow_o, up_o, dn_o, w_o, sm = reduce(gf.reshape(4, n, D), gm, tok, res, gow.reshape(4, lw, D), gup, gdn, gw, small, row(norm1_gain))
    f = lambda v: v.astype(F32)
    sums = (f(w_o), f(ow_o), f(up_o), f(dn_o), sm)
    if planes is not None:
        sums = lax.psum(sums, "dp", axis_index_groups=planes)
    w_o, ow_o, up_o, dn_o, sm = sums
    gqkv = jnp.transpose(w_o.reshape(3, lw, D), (2, 0, 1))
    gck = lax.dynamic_slice(sm, (10 + 3 * t, 0), (3, 3 * lw)).reshape(3, 3, lw)
    gub = lax.dynamic_slice(sm, (6 + t, 0), (1, D)).reshape(-1)
    return (res, f(gt), sm[4], sm[5], gqkv, gck, ow_o, sm[0], sm[1], sm[2], up_o, gub, dn_o, sm[3])


def solution(mesh):
    dp = mesh.shape["dp"]
    planes = None
    if dp > 8:
        planes = [[8 * k + j for k in range(dp // 8)] for j in range(8)]
    rows_, rep = P_(("dp", "tensor"), None), P_()
    third, cols, first = P_(None, None, "tensor"), P_(None, "tensor"), P_("tensor", None)
    return jax.shard_map(
        functools.partial(per_device, planes),
        mesh=mesh,
        in_specs=(rows_, P_(("dp", "tensor")), rows_, rep, rep, third, third, first, rep, rep, rep, cols, P_("tensor"), first, rep),
        out_specs=(rows_, rows_, rep, rep, third, third, first, rep, rep, rep, cols, P_("tensor"), first, rep),
        check_vma=False,
    )
```

```python
import functools
import jax, jax.numpy as jnp
from jax import lax
from jax.experimental import pallas as pl
from jax.experimental.pallas import tpu as pltpu
from jax.sharding import PartitionSpec as P_

HD=64
BF=jnp.bfloat16; F32=jnp.float32
BIG=1e30
def nt(a,b): return lax.dot_general(a,b,(((1,),(1,)),((),())),preferred_element_type=F32)
def tn(a,b): return lax.dot_general(a,b,(((0,),(0,)),((),())),preferred_element_type=F32)
def nn(a,b): return jnp.dot(a,b,preferred_element_type=F32)

def keep_rows(ids):
    n=ids.shape[1]
    pos=lax.broadcasted_iota(jnp.int32,(1,n),1)
    out=[]
    for j in (1,2):
        prev=pltpu.roll(ids,j,1)
        out.append(jnp.where((prev==ids)&(pos>=j),1.0,0.0).astype(F32))
    return out

def feats(ids,rows,kind):
    n=ids.shape[1]
    r=lax.broadcasted_iota(jnp.int32,(rows,n),0)
    idb=jnp.broadcast_to(ids,(rows,n))
    if kind=="q":
        return jnp.where((r<4)&(idb!=r),-BIG,0.0).astype(F32)
    return jnp.where(((r<4)&(idb==r))|((r>=4)&(r<7)),1.0,0.0).astype(F32)

def split3(x):
    hi=x.astype(BF).astype(F32); r=x-hi; mid=r.astype(BF).astype(F32); lo=r-mid
    return hi,mid,lo

EPS=1e-5
def ln(x):
    mu=jnp.mean(x,-1,keepdims=True)
    c=x-mu
    inv=lax.rsqrt(jnp.mean(c*c,-1,keepdims=True)+EPS)
    return c*inv,inv
def ln_back(g,unit,inv,gain):
    s=g*gain
    return (s-jnp.mean(s,-1,keepdims=True)-unit*jnp.mean(s*unit,-1,keepdims=True))*inv
MESH=pl.DeviceIdType.MESH

class Place:
    def __init__(self):
        d=lax.axis_index("dp"); t=lax.axis_index("tensor")
        self.d,self.t=d,t
        b=d%2; p=t//2; q=t%2; base=d-b
        self.b,self.p,self.q,self.base=b,p,q,base
        self.same=1-(b+p)%2
        self.home=self.same==1
        self.near=(p+q)%2==1
        self.member=2*q+b
        self.quarter=(d//2)%4
        self.sib=(base+1-b,t)
        self.opp=(d,2*p+1-q)
        self.cross=(base+1-b,2*p+1-q)
        self.other=(d,2*(1-p)+q)
        self.dest=(base+q,2*b+p)
        self.source=(base+p,2*q+b)
        self.fixed=jnp.logical_and(b==p,b==q)
        dx=d+2-4*((d//2)%2); dy=d+4-8*((d//4)%2)
        self.x=(dx,t); self.y=(dy,t); self.xy=(dx+dy-d,t)
    def zed(self,r): return (self.d,(self.t+r)%4)
    def column(self):
        base=self.d-self.b
        out=[]
        for r in range(1,4):
            out.append((self.d,(self.t+r)%4))
        for r in range(4):
            out.append((base+1-self.b,(self.t+r)%4))
        return out

def meet(peers):
    bar=pltpu.get_barrier_semaphore()
    for dev in peers:
        pl.semaphore_signal(bar,inc=1,device_id=dev,device_id_type=MESH)
    pl.semaphore_wait(bar,len(peers))

class Net:
    def __init__(self,send,recv):
        self.send,self.recv,self.k=send,recv,0
    def to(self,src,dst,dev):
        k=self.k; self.k+=1
        return pltpu.make_async_remote_copy(src_ref=src,dst_ref=dst,send_sem=self.send.at[k],recv_sem=self.recv.at[k],device_id=dev,device_id_type=MESH)

class Swap:
    def __init__(self,net,src,dst,dev,fixed):
        self.r=net.to(src,dst,dev); self.fixed=fixed
        self.l=pltpu.make_async_copy(src,dst,net.recv.at[net.k-1])
    def start(self):
        pl.when(jnp.logical_not(self.fixed))(self.r.start)
        pl.when(self.fixed)(self.l.start)
    def wait_recv(self): self.l.wait()
    def wait_send(self): pl.when(jnp.logical_not(self.fixed))(self.r.wait_send)

def rows(ref,start,size): return ref.at[pl.ds(start,size)]

def lanes(start,size): return pl.ds(pl.multiple_of(start,128),size)
def rws(start,size): return pl.ds(pl.multiple_of(start,16),size)


class ToHeads:
    def __init__(self,net,P,src,dst):
        self.k=net.k; net.k+=4
        self.P,self.net,self.dst=P,net,dst
        self.far=[]
        for mm in range(4):
            c=pltpu.make_async_remote_copy(src_ref=src(mm),dst_ref=dst.at[P.t],send_sem=net.send.at[self.k+mm],recv_sem=net.recv.at[self.k+P.t],
                                           device_id=(P.base+mm%2,2*P.b+mm//2),device_id_type=MESH)
            l=pltpu.make_async_copy(src(mm),dst.at[P.t],net.recv.at[self.k+P.t])
            self.far.append((jnp.logical_and(P.home,P.member==mm),c,l))
    def start(self):
        for me,c,l in self.far:
            pl.when(jnp.logical_not(me))(c.start)
            pl.when(me)(l.start)
    def wait_recv(self):
        for s in range(4):
            pltpu.make_async_copy(self.dst.at[s],self.dst.at[s],self.net.recv.at[self.k+s]).wait()
    def wait_send(self):
        for me,c,l in self.far: pl.when(jnp.logical_not(me))(c.wait_send)

def mix2(v, cks, r, c, keeps):
    out = cks[pl.ds(r, HD), c:c + 1] * v
    for j in (1, 2):
        out = out + cks[pl.ds(r, HD), 3 * j + c:3 * j + c + 1] * (pltpu.roll(v, j, 1) * keeps[j - 1])
    return out

def tap_columns(ckv, tmp, cks):
    lw = ckv.shape[2]
    tmp[...] = jnp.zeros(tmp.shape, F32)
    for j in range(3):
        for c in range(3):
            tmp[3 * j + c:3 * j + c + 1, 0:lw] = ckv[j, c:c + 1, :]
    cks[...] = tmp[...].T

NC = 4
def first_kernel(tok, ids, cot, wt, ck, ow, up, dn, upb, g1, s1, outb, g2, s2, dnb,
                 x_o, ids_o, wt_o, ck_o, proj_o, lse_o, of_o, res_o, gm_o, ga_in, ow_o, up_o, dn_o, small_o, gupb_o,
                 xv, xn, cotv, idv, wtv, ckv, tmp, cks, proj, qt, kk, vt, att, attin, of, lse,
                 ow_a, up_a, dn_a, upb_a, sec, act, gh, gsec, gms, gas, c_ow, c_up, c_dn, send, recv, lsem, wsem):
    P = Place()
    meet(P.column() + [P.x, P.y, P.xy])
    net = Net(send, recv)
    n, D = tok.shape
    N = 4 * n
    heads = wt.shape[0] // (3 * HD)
    lw = heads * HD
    R = n // NC; H = R // 2
    m = P.member; t = P.t
    sends = []
    def later(src, dst, dev):
        c = net.to(src, dst, dev); sends.append(c); return c
    def push(src, dst, dev):
        c = later(src, dst, dev); c.start(); return c
    def swap(src, dst, dev):
        c = Swap(net, src, dst, dev, P.fixed); sends.append(c); return c
    Q = wt.shape[0] // 4
    w0 = pl.multiple_of(P.quarter * Q, 16)
    idg = ToHeads(net, P, lambda mm: ids, idv)
    idg.start()
    wq = swap(rows(wt, w0, Q), rows(wtv, w0, Q), P.dest); wq.start()
    ckc = swap(ck, ckv, P.dest); ckc.start()
    cotl = pltpu.make_async_copy(cot, cotv, lsem.at[15]); cotl.start()
    def part(ref, tt, k):
        L = ref.shape[2] // 2; r = ref.shape[1] // 4
        return ref.at[tt, pl.ds(pl.multiple_of(k * r, 16), r), pl.ds(pl.multiple_of(P.b * L, 128), L)]
    def part_in(ref):
        L = ref.shape[1] // 2; r = ref.shape[0] // 4
        return ref.at[pl.ds(pl.multiple_of(P.quarter * r, 16), r), pl.ds(pl.multiple_of(P.b * L, 128), L)]
    qx = (P.x[0] // 2) % 4; qy = (P.y[0] // 2) % 4; qd = (P.xy[0] // 2) % 4
    order = [t, t - 1 + 2 * (1 - (t + 3) // 4), 2 + t // 2 - 2 * (t // 3), 3 - 3 * (t // 2)]
    right = (P.d, (t + 1) % 4); left = (P.d, (t + 3) % 4)
    guarded = []
    class Spread:
        def __init__(self, ins, alls, b0):
            self.zr = net.k; net.k += 4 * len(ins)
            self.w = len(ins)
            def z_push(src, tt, j, cond, dev):
                k = net.k; net.k += 1
                c = pltpu.make_async_remote_copy(src_ref=src, dst_ref=part(alls[j], tt, P.quarter), send_sem=send.at[k],
                                                 recv_sem=recv.at[self.zr + self.w * tt + j], device_id=dev, device_id_type=MESH)
                guarded.append((cond, c))
                return lambda: pl.when(cond)(c.start)
            self.first = [z_push(part_in(ins[j]), t, j, cond, dev) for j in range(self.w) for cond, dev in ((t < 3, right), (t > 0, left))]
            self.steps = {}
            for r in (1, 2, 3):
                tt = order[r]
                arrive = []
                for j in range(self.w):
                    z = part(alls[j], tt, P.quarter)
                    wait = pltpu.make_async_copy(z, z, recv.at[self.zr + self.w * tt + j])
                    arrive.append([wait.wait, z_push(z, tt, j, jnp.logical_and(tt < t, t < 3), right),
                                   z_push(z, tt, j, jnp.logical_and(tt > t, t > 0), left)])
                mine = [part(a, tt, P.quarter) for a in alls]
                bx = [part(a, tt, qx) for a in alls]; by = [part(a, tt, qy) for a in alls]; bd = [part(a, tt, qd) for a in alls]
                ax = [later(z, z, P.x) for z in mine]; ay = [later(z, z, P.y) for z in mine]; asib = [later(z, z, P.sib) for z in mine]
                dx = [later(z, z, P.y) for z in bx[:b0]]; dy = [later(z, z, P.x) for z in by[b0:]]
                xs = [later(z, z, P.sib) for z in bx]; ys = [later(z, z, P.sib) for z in by]; ds_ = [later(z, z, P.sib) for z in bd]
                self.steps[r] = (arrive, ax, ay, asib, dx, dy, xs, ys, ds_)
        def start(self):
            for f in self.first: f()
        def a(self, r):
            arrive, ax, ay, asib = self.steps[r][:4]
            for step in arrive:
                for f in step: f()
            for c in ax + ay + asib: c.start()
        def b(self, r):
            _, ax, ay, _, dx, dy, xs, ys, _ = self.steps[r]
            for c in ax: c.wait_recv()
            for c in dx + xs: c.start()
            for c in ay: c.wait_recv()
            for c in dy + ys: c.start()
        def c(self, r):
            _, _, _, _, dx, dy, _, _, ds_ = self.steps[r]
            for c in dx + dy: c.wait_recv()
            for c in ds_: c.start()
        def end(self, r):
            _, _, _, asib, _, _, xs, ys, ds_ = self.steps[r]
            for c in asib + xs + ys + ds_: c.wait_recv()
    so = Spread((ow,), (ow_a,), 1)
    sw = Spread((up, dn), (up_a, dn_a), 1)
    so.start()
    own = [pltpu.make_async_copy(a, b.at[t], lsem.at[j]) for j, (a, b) in enumerate(((ow, ow_a), (up, up_a), (dn, dn_a), (upb, upb_a)))]
    for c in own: c.start()
    bias = [push(upb, upb_a.at[t], P.zed(r)) for r in (1, 2, 3)]
    opp_shard = 2 * P.p + 1 - P.q
    target = P.same * opp_shard + (1 - P.same) * (1 + P.b)
    far_shards = (2 * (1 - P.p), 2 * (1 - P.p) + 1)
    ka = net.k; kb = ka + 4 * NC; kc = kb + NC; kd = kc + 4 * NC; net.k = kd + 4 * NC
    def raw(src, dst, ks, kr, dev):
        return pltpu.make_async_remote_copy(src_ref=src, dst_ref=dst, send_sem=send.at[ks], recv_sem=recv.at[kr], device_id=dev, device_id_type=MESH)
    sent = []
    def give_piece(k):
        z = pl.ds(k * R, R)
        unit, _ = ln(tok[k * R:(k + 1) * R, :].astype(F32))
        xn[k * R:(k + 1) * R, :] = (unit * g1[...] + s1[...]).astype(BF)
        for h in range(2):
            zh = pl.ds(k * R + h * H, H)
            c = raw(xn.at[zh], xv.at[t, zh], ka + 4 * k + h, ka + 4 * k + t, (P.base + h, target)); c.start(); sent.append(c)
        c = raw(xn.at[z], xv.at[t, z], kb + k, kb + k, P.sib)
        pl.when(P.home)(c.start); guarded.append((P.home, c))
    def relay(k):
        zb = pl.ds(pl.multiple_of(k * R + P.b * H, 16), H)
        for j, s in enumerate((opp_shard,) + far_shards):
            blk = xv.at[s, zb]
            if j == 0:
                pltpu.make_async_copy(blk, blk, recv.at[ka + 4 * k + s]).wait()
            else:
                on = raw(blk, blk, kd + 4 * k + j, kd + 4 * k + s, P.opp)
                @pl.when(P.near)
                def _():
                    pltpu.make_async_copy(blk, blk, recv.at[ka + 4 * k + s]).wait()
                    on.start()
                guarded.append((P.near, on))
                @pl.when(jnp.logical_not(P.near))
                def _():
                    pltpu.make_async_copy(blk, blk, recv.at[kd + 4 * k + s]).wait()
            c = raw(blk, blk, kc + 4 * k + j, kc + 4 * k + s, P.sib); c.start(); sent.append(c)
    give_piece(0); give_piece(1)
    relay(0)
    so.a(1)
    give_piece(2)
    wq.wait_recv()
    wf = [push(rows(wtv, w0, Q), rows(wtv, w0, Q), dev) for dev in (P.x, P.y, P.xy)]
    relay(1)
    so.a(2); so.b(1)
    give_piece(3)
    relay(2)
    so.a(3); so.b(2); so.c(1)
    sw.start()
    relay(3)
    @pl.when(P.home)
    def _(): xv[t] = xn[...]
    for c in wf: c.wait_recv()
    def project(s):
        proj[:, pl.ds(pl.multiple_of(s * n, 128), n)] = nt(wtv[...], xv[s])
    @pl.when(jnp.logical_not(P.home))
    def _():
        for k in range(NC): pltpu.make_async_copy(xv.at[t, pl.ds(k * R, R)], xv.at[t, pl.ds(k * R, R)], recv.at[kb + k]).wait()
    project(t)
    so.b(3); so.c(2)
    for k in range(NC):
        zo = pl.ds(pl.multiple_of(k * R + (1 - P.b) * H, 16), H)
        pltpu.make_async_copy(xv.at[opp_shard, zo], xv.at[opp_shard, zo], recv.at[kc + 4 * k + opp_shard]).wait()
    project(opp_shard)
    so.c(3)
    for k in range(NC):
        zo = pl.ds(pl.multiple_of(k * R + (1 - P.b) * H, 16), H)
        for s in far_shards:
            pltpu.make_async_copy(xv.at[s, zo], xv.at[s, zo], recv.at[kc + 4 * k + s]).wait()
    for s in far_shards: project(s)
    idg.wait_recv()
    ckc.wait_recv()
    outs = [pltpu.make_async_copy(a, b, lsem.at[4 + k]) for k, (a, b) in enumerate(
        ((xv, x_o), (wtv, wt_o), (proj, proj_o), (ckv, ck_o)))]
    for c in outs: c.start()
    idrow = jnp.concatenate([idv[s] for s in range(4)], axis=1)
    idv_out = pltpu.make_async_copy(idv, ids_o, lsem.at[9]); idv_out.start()
    keeps = keep_rows(idrow)
    tap_columns(ckv, tmp, cks)
    fq = feats(idrow, 64, "q").astype(BF); fk = feats(idrow, 64, "k")
    qt[64:128, :] = fq
    vt[64:80, :] = jnp.ones((16, N), BF)
    tri = lax.broadcasted_iota(jnp.int32, (n, n), 0) <= lax.broadcasted_iota(jnp.int32, (n, n), 1)
    eb = net.k; net.k += 4 * heads
    def give(h, tt):
        r = pl.ds(pl.multiple_of(h * HD, HD), HD)
        return raw(att.at[tt, r], attin.at[m, r], eb + 4 * h + tt, eb + 4 * h + m, (P.base + P.p, tt))
    def not_me(tt): return jnp.logical_not(jnp.logical_and(P.home, t == tt))
    def not_mine(mm): return jnp.logical_not(jnp.logical_and(P.home, m == mm))
    def head(h, _):
        r = pl.multiple_of(h * HD, HD)
        def part_rows(c): return proj[pl.ds(pl.multiple_of(c * lw + h * HD, HD), HD), :]
        q = mix2(part_rows(0), cks, r, 0, keeps)
        qt[0:64, :] = (q.astype(BF).astype(F32) * 0.125).astype(BF)
        k = mix2(part_rows(1), cks, r, 1, keeps)
        kk[...] = jnp.concatenate([k, fk], 0).T.astype(BF)
        vt[0:64, :] = mix2(part_rows(2), cks, r, 2, keeps).astype(BF)
        for iq in range(4):
            if iq == 2:
                @pl.when(h == 0)
                def _(): sw.a(1)
                @pl.when(h == 1)
                def _(): sw.a(2); sw.b(1)
                @pl.when(h == 2)
                def _(): sw.a(3); sw.b(2); sw.c(1)
            qs = iq * n
            qb = qt[:, qs:qs + n]
            ss = []
            for j in range(iq + 1):
                s = nn(kk[j * n:(j + 1) * n, :], qb)
                if j == iq: s = jnp.where(tri, s, -BIG)
                ss.append(s)
            mx = jnp.max(ss[0], axis=0, keepdims=True)
            for s in ss[1:]: mx = jnp.maximum(mx, jnp.max(s, axis=0, keepdims=True))
            o = jnp.zeros((80, n), F32)
            for j, s in enumerate(ss):
                o = o + nn(vt[:, j * n:(j + 1) * n], jnp.exp(s - mx).astype(BF))
            l = o[64:65, :]
            f = o[0:64, :] / l
            of[pl.ds(r, HD), qs:qs + n] = f
            att[iq, pl.ds(r, HD), :] = f.astype(BF)
            lse[h, :, qs:qs + n] = jnp.broadcast_to(mx + jnp.log(l), (8, n))
        for tt in range(4): pl.when(not_me(tt))(give(h, tt).start)
        return 0
    lax.fori_loop(0, heads, head, 0)
    @pl.when(P.home)
    def _(): attin[m] = att[t]
    ends = [pltpu.make_async_copy(a, b, lsem.at[11 + k]) for k, (a, b) in enumerate(((of, of_o), (lse, lse_o)))]
    for c in ends: c.start()
    for r in (1, 2, 3): so.end(r)
    for c in own: c.wait()
    for h in range(heads):
        r = pl.ds(h * HD, HD)
        for mm in range(4):
            pl.when(not_mine(mm))(pltpu.make_async_copy(attin.at[mm, r], attin.at[mm, r], recv.at[eb + 4 * h + mm]).wait)
            pl.when(not_me(mm))(give(h, mm).wait_send)
    attT = attin[...].reshape(4 * lw, n)
    gms[...] = tok[...].astype(F32) + tn(attT, ow_a[...].reshape(4 * lw, D)) + outb[...]
    unit, inv = ln(gms[...])
    sec[...] = (unit * g2[...] + s2[...]).astype(BF)
    for c in bias: c.wait_recv()
    sw.b(3); sw.c(2)
    cotl.wait()
    gsec[...] = jnp.zeros_like(gsec)
    def chain(tt):
        rl = jnp.maximum(nn(sec[...], up_a[tt]) + upb_a[tt], 0.0)
        act[tt] = (rl * rl).astype(BF)
        g = (nt(cotv[...], dn_a[tt]) * (2.0 * rl)).astype(BF)
        gh[tt] = g
        gupb_o[tt] = jnp.sum(g.astype(F32), 0, keepdims=True)
        gsec[...] += nt(g, up_a[tt])
    chain(order[0])
    sw.end(1); chain(order[1])
    sw.c(3)
    sw.end(2); chain(order[2])
    sw.end(3); chain(order[3])
    mid = gms[...]
    unit, inv = ln(mid)
    gs = gsec[...]
    cf = cotv[...].astype(F32)
    gm = cf + ln_back(gs, unit, inv, g2[...])
    gmb = gm.astype(BF)
    gb = ToHeads(net, P, lambda mm: gas.at[mm], ga_in)
    for mm in range(4):
        gas[mm] = nt(ow_a[mm], gmb).astype(BF)
    gb.start()
    gsec[...] = gm
    gmo = pltpu.make_async_copy(gsec, gm_o, lsem.at[14]); gmo.start()
    small_o[0:1] = jnp.sum(gm, 0, keepdims=True)
    small_o[1:2] = jnp.sum(gs * unit, 0, keepdims=True)
    small_o[2:3] = jnp.sum(gs, 0, keepdims=True)
    small_o[3:4] = jnp.sum(cf, 0, keepdims=True)
    small_o[4:8] = jnp.zeros((4, D), F32)
    out = mid + dnb[...]
    for b in range(4): out = out + nn(act[b], dn_a[b])
    res_o[...] = out.astype(BF)
    for c in sends: c.wait_send()
    for c in sent: c.wait_send()
    for cond, c in guarded: pl.when(cond)(c.wait_send)
    gb.wait_send()
    L = D // 2
    lo, lx = P.b * L, (1 - P.b) * L
    halves = []
    def half(g, cref, b):
        c = net.to(g.at[b, :, lanes(lx, L)], cref.at[b], P.sib); c.start()
        halves.append((c, g, cref, b))
    def gow_step():
        ow_a[...] = nn(attT, gmb).astype(BF).reshape(ow_a.shape)
        for b in range(4): half(ow_a, c_ow, b)
    for b in range(4):
        dn_a[b] = tn(act[b], cotv[...]).astype(BF)
        half(dn_a, c_dn, b)
        up_a[b] = tn(sec[...], gh[b]).astype(BF)
        half(up_a, c_up, b)
    gow_step()
    fin = []
    for k, (c, g, cref, b) in enumerate(halves):
        c.wait_recv()
        cref[b] = (cref[b].astype(F32) + g[b, :, lanes(lo, L)].astype(F32)).astype(BF)
        o = {id(c_ow): ow_o, id(c_up): up_o, id(c_dn): dn_o}[id(cref)]
        z = pltpu.make_async_copy(cref.at[b], o.at[b], wsem.at[k]); z.start(); fin.append(z)
    for c, g, cref, b in halves: c.wait_send()
    gb.wait_recv()
    idg.wait_send()
    for c in outs + [idv_out, gmo] + ends + fin: c.wait()

def first(tok, ids, cot, wt, ck, ow, up, dn, upb, g1, s1, outb, g2, s2, dnb):
    n, D = tok.shape; S = jax.ShapeDtypeStruct; V = pltpu.VMEM
    lw = wt.shape[0] // 3; heads = lw // HD; N = 4 * n; fb = up.shape[1]
    any_ = pl.BlockSpec(memory_space=pl.ANY); vm = pl.BlockSpec(memory_space=pltpu.VMEM)
    outs = [(S((4, n, D), BF), any_), (S((4, 1, n), jnp.int32), any_), (S(wt.shape, BF), any_), (S(ck.shape, F32), any_),
            (S((3 * lw, N), F32), any_), (S((heads, 8, N), F32), any_), (S((lw, N), F32), any_),
            (S((n, D), BF), vm), (S((n, D), F32), any_), (S((4, lw, n), BF), any_),
            (S((4, lw, D // 2), BF), any_), (S((4, D, fb // 2), BF), any_), (S((4, fb, D // 2), BF), any_), (S((8, D), F32), vm), (S((4, 1, fb), F32), vm)]
    return pl.pallas_call(first_kernel, out_shape=tuple(o[0] for o in outs),
        in_specs=[vm] + [any_] * 8 + [vm] * 6, out_specs=tuple(o[1] for o in outs),
        scratch_shapes=[V((4, n, D), BF), V((n, D), BF), V((n, D), BF), V((4, 1, n), jnp.int32), V(wt.shape, BF), V(ck.shape, F32), V((128, 256), F32), V((256, 128), F32),
                        V((3 * lw, N), F32), V((128, N), BF), V((N, 128), BF), V((80, N), BF), V((4, lw, n), BF), V((4, lw, n), BF), V((lw, N), F32), V((heads, 8, N), F32),
                        V((4, lw, D), BF), V((4, D, fb), BF), V((4, fb, D), BF), V((4, 1, fb), F32),
                        V((n, D), BF), V((4, n, fb), BF), V((4, n, fb), BF), V((n, D), F32), V((n, D), F32), V((4, lw, n), BF),
                        V((4, lw, D // 2), BF), V((4, D, fb // 2), BF), V((4, fb, D // 2), BF),
                        pltpu.SemaphoreType.DMA((240,)), pltpu.SemaphoreType.DMA((240,)), pltpu.SemaphoreType.DMA((16,)), pltpu.SemaphoreType.DMA((12,))],
        compiler_params=pltpu.CompilerParams(collective_id=0, has_side_effects=True, vmem_limit_bytes=60 * 2**20),
        name="forward_and_feed",
    )(tok, ids, cot, wt, ck, ow, up, dn, upb, g1, s1, outb, g2, s2, dnb)
def second_kernel(x_h, wt, ck, ids, proj_h, lse, of_h, ga, tok, gm, s_ow, s_up, s_dn, s4, gupb, g1,
                  gt_o, ow_o, up_o, dn_o, w_o, small_o,
                  x, proj, qt, qn, kk, kt, vn, dot, don, dkv, gconv, gp, gw, gwb, gfs, land1, land2, fin, g_s,
                  tmp, cks, cacc, own_x, own_y, own_o, x_ow, x_up, y_dn, z_ow, z_up, z_dn, o_ow, o_up, o_dn, f_ow, f_up, f_dn,
                  w1, w2, f_w, sl, sa, sb, sc, send, recv, lsem):
    P = Place()
    plane = []
    for r in (P.x, P.y, P.xy): plane += [r, (r[0] + 1 - 2 * P.b, r[1])]
    meet(P.column() + plane)
    net = Net(send, recv)
    n, D = tok.shape; N = 4 * n; H = n // 2; L = D // 2
    heads = wt.shape[0] // (3 * HD); lw = heads * HD
    m, t, b, p = P.member, P.t, P.b, P.p
    f32 = lambda v: v.astype(F32)
    started, guarded = [], []
    def later(src, dst, dev):
        c = net.to(src, dst, dev); started.append(c); return c
    def push(src, dst, dev):
        c = later(src, dst, dev); c.start(); return c
    def raw(src, dst, ks, kr, dev):
        return pltpu.make_async_remote_copy(src_ref=src, dst_ref=dst, send_sem=send.at[ks], recv_sem=recv.at[kr], device_id=dev, device_id_type=MESH)
    qr = P.quarter; qx = (P.x[0] // 2) % 4; qy = (P.y[0] // 2) % 4; qd = (P.xy[0] // 2) % 4
    lo = b * L
    ro, ru = s_ow.shape[1] // 4, s_up.shape[1] // 4
    blocks = [1 - P.q, 3 - P.q, 2 * (1 - p) + P.q, t]
    lc = [0]
    def local(src, dst):
        c = pltpu.make_async_copy(src, dst, lsem.at[lc[0]]); lc[0] += 1; c.start(); return c
    class Block:
        def __init__(self, j):
            tt = blocks[j]
            self.j, self.tt = j, tt
            q_ = lambda ref, k, r_: ref.at[tt, rws(k * r_, r_), :]
            self.p1x = [later(q_(s_ow, k, ro), x_ow.at[j, i], P.x) for i, k in ((0, qx), (1, qd))] + \
                       [later(q_(s_up, k, ru), x_up.at[j, i], P.x) for i, k in ((0, qx), (1, qd))]
            self.p1y = [later(q_(s_dn, k, ru), y_dn.at[j, i], P.y) for i, k in ((0, qy), (1, qd))]
            self.p3 = [later(x_ow.at[j, 1], z_ow.at[j], P.y), later(x_up.at[j, 1], z_up.at[j], P.y), later(y_dn.at[j, 1], z_dn.at[j], P.x)]
        def load(self):
            tt, j = self.tt, self.j
            q_ = lambda ref, k, r_: ref.at[tt, rws(k * r_, r_), :]
            self.loads = [local(q_(s_ow, k, ro), own_o.at[j, i]) for i, k in ((0, qr), (1, qy))] + \
                         [local(q_(s_up, k, ru), own_x.at[j, i]) for i, k in ((0, qr), (1, qy))] + \
                         [local(q_(s_dn, k, ru), own_y.at[j, i]) for i, k in ((0, qr), (1, qx))]
        def a(self):
            for c in self.p1x + self.p1y: c.start()
        def b(self):
            j = self.j
            for c in self.loads: c.wait()
            for c in self.p1x + self.p1y: c.wait_recv()
            for z, o in ((x_ow, own_o), (x_up, own_x), (y_dn, own_y)):
                z[j] = (f32(z[j]) + f32(o[j])).astype(BF)
            for c in self.p3: c.start()
        def c(self):
            j = self.j
            for c in self.p3: c.wait_recv()
            for z, o in ((z_ow, x_ow), (z_up, x_up), (z_dn, y_dn)):
                z[j] = (f32(z[j]) + f32(o[j, 0])).astype(BF)
    B = [Block(j) for j in range(4)]
    zs = ((z_ow, o_ow, f_ow), (z_up, o_up, f_up), (z_dn, o_dn, f_dn))
    zz = [[later(z.at[j], o.at[j], P.opp) for j in (0, 1)] for z, o, f in zs]
    z2 = [later(z.at[2], f.at[0], P.other) for z, o, f in zs]
    def opp_send(j):
        for cc in zz: cc[j].start()
    def opp_add():
        for (z, o, f), cc in zip(zs, zz):
            for c in cc: c.wait_recv()
            z[2] = (f32(z[2]) + f32(o[1 - p])).astype(BF)
        for c in z2: c.start()
    outs = ((ow_o, f_ow, ro), (up_o, f_up, ru), (dn_o, f_dn, ru))
    def place(o, k, r_): return o.at[rws(k * r_, r_), lanes(lo, L)]
    class Share:
        def __init__(self, o, src, r_, by_x):
            self.own = (src, place(o, qr, r_))
            self.sx = later(src, place(o, qr, r_), P.x); self.sy = later(src, place(o, qr, r_), P.y); self.ss = later(src, place(o, qr, r_), P.sib)
            px, py, pd = place(o, qx, r_), place(o, qy, r_), place(o, qd, r_)
            self.dg = later(px, px, P.y) if by_x else later(py, py, P.x)
            self.by_x = by_x
            self.fx, self.fy, self.fd = later(px, px, P.sib), later(py, py, P.sib), later(pd, pd, P.sib)
        def a(self):
            for c in (self.sx, self.sy, self.ss): c.start()
            self.l = local(*self.own)
        def b(self):
            self.sx.wait_recv()
            if self.by_x: self.dg.start()
            self.fx.start()
            self.sy.wait_recv()
            if not self.by_x: self.dg.start()
            self.fy.start()
        def c(self):
            self.dg.wait_recv(); self.fd.start()
        def end(self):
            for c in (self.ss, self.fx, self.fy, self.fd): c.wait_recv()
            self.l.wait()
    sh = [Share(o, f.at[1], r_, bx) for (o, f, r_), bx in zip(outs, (True, True, False))]
    shw = Share(w_o, f_w, wt.shape[0] // 4, False)
    def final_add():
        for (z, o, f), c in zip(zs, z2):
            c.wait_recv()
            f[1] = (f32(f[0]) + f32(z[3]) + f32(o[p])).astype(BF)
    for j in (0, 1): B[j].a()
    ldp = local(proj_h, proj)
    ldo = local(of_h, gconv.at[pl.ds(0, lw)])
    ldx = local(x_h, x)
    for j in range(4): B[j].load()
    idrow = jnp.concatenate([ids[s] for s in range(4)], axis=1)
    keeps = keep_rows(idrow)
    tap_columns(ck, tmp, cks)
    cacc[...] = jnp.zeros(cacc.shape, F32)
    fq = feats(idrow, 64, "q"); fk = feats(idrow, 64, "k")
    r8 = lax.broadcasted_iota(jnp.int32, (64, N), 0)
    zl = jnp.zeros((64, N), F32)
    ldp.wait(); ldo.wait()
    def setup(h, _):
        r = pl.multiple_of(h * HD, HD)
        def part_rows(c): return proj[pl.ds(pl.multiple_of(c * lw + h * HD, HD), HD), :]
        q = f32(mix2(part_rows(0), cks, r, 0, keeps).astype(BF)) * 0.125
        hi, mid, low = split3(-lse[h, 0:1, :])
        f = fq + jnp.where(r8 == 4, hi, 0.0) + jnp.where(r8 == 5, mid, 0.0) + jnp.where(r8 == 6, low, 0.0)
        qt[h, 0:64, :] = q.astype(BF); qt[h, 64:128, :] = f.astype(BF)
        qn[h] = jnp.concatenate([zl, q], 0).T.astype(BF)
        k = mix2(part_rows(1), cks, r, 1, keeps)
        kt[h] = k.astype(BF)
        kk[h] = jnp.concatenate([k, fk], 0).T.astype(BF)
        v = mix2(part_rows(2), cks, r, 2, keeps)
        vn[h] = jnp.concatenate([v, jnp.where(r8 < 3, 1.0, 0.0)], 0).T.astype(BF)
        do = f32(jnp.concatenate([ga[s, pl.ds(r, HD), :] for s in range(4)], axis=1))
        inner = jnp.sum(do * gconv[pl.ds(r, HD), :], axis=0, keepdims=True)
        hi, mid, low = split3(-inner)
        f = jnp.where(r8 == 0, hi, 0.0) + jnp.where(r8 == 1, mid, 0.0) + jnp.where(r8 == 2, low, 0.0)
        dot[h, 0:64, :] = do.astype(BF); dot[h, 64:128, :] = f.astype(BF)
        don[h] = jnp.concatenate([do, zl], 0).T.astype(BF)
        return 0
    lax.fori_loop(0, heads, setup, 0)
    B[2].a()
    tri = lax.broadcasted_iota(jnp.int32, (n, n), 0) <= lax.broadcasted_iota(jnp.int32, (n, n), 1)
    opp_shard = 2 * p + 1 - P.q
    h0 = pl.multiple_of(b * H, 16); h1 = pl.multiple_of((1 - b) * H, 16)
    e1 = [later(gfs.at[s, pl.ds(h1, H)], land1.at[s], P.sib) for s in range(4)]
    k2 = net.k; k3 = k2 + 4; k4 = k3 + 4; net.k = k4 + 2
    def far_side(s): return s // 2 != p
    def to_opp(s):
        cond = jnp.logical_or(opp_shard == s, jnp.logical_and(far_side(s), jnp.logical_not(P.near)))
        return cond, raw(land1.at[s], land2.at[s], k2 + s, k2 + s, P.opp)
    def summing(s): return jnp.logical_or(t == s, jnp.logical_and(far_side(s), P.near))
    def to_owner(s):
        cond = jnp.logical_and(summing(s), jnp.logical_not(jnp.logical_and(P.home, t == s)))
        return cond, raw(land2.at[s], fin.at[b], k3 + s, k4 + b, (P.base + p, s))
    opps = [to_opp(s) for s in range(4)]; owners = [to_owner(s) for s in range(4)]
    guarded += opps + owners
    def s1(s): e1[s].start()
    def s2(s):
        e1[s].wait_recv()
        land1[s] = (f32(land1[s]) + f32(gfs[s, pl.ds(h0, H)])).astype(BF)
        cond, c = opps[s]; pl.when(cond)(c.start)
    def s3(s):
        @pl.when(summing(s))
        def _():
            pltpu.make_async_copy(land2.at[s], land2.at[s], recv.at[k2 + s]).wait()
            land2[s] = (f32(land2[s]) + f32(land1[s])).astype(BF)
        cond, c = owners[s]; pl.when(cond)(c.start)
    def rows_of(i, points):
        qs = i * n
        def head(h, _):
            for k, f in points.items(): pl.when(h == k)(f)
            dq = jnp.zeros((64, n), F32)
            for j in range(i + 1):
                js = j * n
                st = nn(kk[h, js:js + n, :], qt[h, :, qs:qs + n])
                pr = jnp.exp(st)
                if i == j: pr = jnp.where(tri, pr, 0.0)
                dp = nn(vn[h, js:js + n, :], dot[h, :, qs:qs + n])
                ds = (pr * dp).astype(BF)
                add = nn(pr.astype(BF), don[h, qs:qs + n, :]) + nn(ds, qn[h, qs:qs + n, :])
                if i == 3: dkv[h, js:js + n, :] = add
                else: dkv[h, js:js + n, :] += add
                dq = dq + nn(kt[h, :, js:js + n], ds)
            gconv[pl.ds(pl.multiple_of(h * HD, HD), HD), qs:qs + n] = dq * 0.125
            tt = dkv[h, qs:qs + n, :].T
            gconv[pl.ds(pl.multiple_of(2 * lw + h * HD, HD), HD), qs:qs + n] = tt[0:64]
            gconv[pl.ds(pl.multiple_of(lw + h * HD, HD), HD), qs:qs + n] = tt[64:128]
            for c in range(3):
                r = pl.ds(pl.multiple_of(c * lw + h * HD, HD), HD); rk = pl.ds(pl.multiple_of(h * HD, HD), HD)
                g = gconv[r, qs:qs + n]
                nxt = jnp.zeros((HD, 128), F32) if i == 3 else gconv[r, qs + n:qs + n + 128]
                gx = jnp.concatenate([g, nxt], 1)
                pc = proj[r, qs:qs + n]
                prv = jnp.zeros((HD, 128), F32) if i == 0 else proj[r, qs - 128:qs]
                px = jnp.concatenate([prv, pc], 1)
                o = cks[rk, c:c + 1] * g
                cacc[rk, c:c + 1] += jnp.sum(g * pc, axis=1, keepdims=True)
                for jj in (1, 2):
                    kr = keeps[jj - 1][:, qs:qs + n]
                    kn = jnp.zeros((1, 128), F32) if i == 3 else keeps[jj - 1][:, qs + n:qs + n + 128]
                    kg = gx * jnp.concatenate([kr, kn], 1)
                    cacc[rk, 3 * jj + c:3 * jj + c + 1] += jnp.sum(kg[:, 0:n] * pltpu.roll(px, jj, 1)[:, 128:], axis=1, keepdims=True)
                    o = o + cks[rk, 3 * jj + c:3 * jj + c + 1] * pltpu.roll(kg, n + 128 - jj, 1)[:, 0:n]
                gp[r, :] = o.astype(BF)
            return 0
        lax.fori_loop(0, heads, head, 0)
        gfs[i] = tn(gp[...], wt[...]).astype(BF)
        s1(i)
        if i == 3: ldx.wait()
        g = nn(gp[...], x[i])
        if i == 3: gw[...] = g
        else: gw[...] += g
    def at(*fs):
        def run():
            for f in fs: f()
        return run
    rows_of(3, {1: at(B[0].b, B[3].a), 2: at(B[1].b)})
    rows_of(2, {0: at(B[0].c, lambda: opp_send(0), B[1].c, lambda: opp_send(1)), 1: at(lambda: s2(3), B[2].b)})
    rows_of(1, {0: at(B[3].b, lambda: s2(2)), 1: at(lambda: s3(3), B[2].c), 2: at(opp_add)})
    rows_of(0, {0: at(lambda: s2(1), lambda: s3(2)), 1: at(B[3].c)})
    Q = wt.shape[0] // 4
    gwb[...] = gw[...].astype(BF)
    wx = [push(gwb.at[rws(k * Q, Q)], w1.at[j], dev) for j, (k, dev) in enumerate(((qx, P.x), (qy, P.y), (qd, P.xy)))]
    final_add()
    for s in sh: s.a()
    s2(0); s3(1)
    unit, inv = ln(f32(tok[...]))
    s3(0)
    for c in wx: c.wait_recv()
    w1[0] = (f32(w1[0]) + f32(w1[1]) + f32(w1[2]) + f32(gwb[rws(qr * Q, Q)])).astype(BF)
    k5 = net.k; net.k += 2
    lam = []
    for h in range(2):
        me = jnp.logical_and(t == m, b == h)
        src, dst = w1.at[0, :, pl.ds(h * L, L)], w2.at[p]
        c = raw(src, dst, k5 + h, k5 + p, (P.base + h, m))
        l = pltpu.make_async_copy(src, dst, recv.at[k5 + p])
        pl.when(jnp.logical_not(me))(c.start); pl.when(me)(l.start)
        guarded.append((jnp.logical_not(me), c))
    for s in sh: s.b()
    mine = P.home
    @pl.when(mine)
    def _(): fin[b] = land2[t]
    @pl.when(jnp.logical_not(mine))
    def _(): pltpu.make_async_copy(fin.at[b], fin.at[b], recv.at[k4 + b]).wait()
    pltpu.make_async_copy(fin.at[1 - b], fin.at[1 - b], recv.at[k4 + 1 - b]).wait()
    g_s[0:H] = f32(fin[0]); g_s[H:n] = f32(fin[1])
    g = g_s[...]
    gt_o[...] = gm[...] + ln_back(g, unit, inv, g1[...])
    sl[...] = jnp.zeros(sl.shape, F32)
    def put(row, v): sl[row // 6, pl.ds(row % 6, 1), 0:v.shape[1]] = v
    for k in range(4): put(k, s4[k:k + 1])
    put(4, jnp.sum(g * unit, 0, keepdims=True)); put(5, jnp.sum(g, 0, keepdims=True))
    for k in range(4): put(6 + k, gupb[k])
    ct = cacc[...].T
    for k in range(9): put(10 + 9 * m + k, ct[k:k + 1, 0:lw])
    me = P.d % 8
    k6 = net.k; k7 = k6 + 8; k8 = k7 + 4; net.k = k8 + 8
    peers = plane + [P.sib]
    hop1 = [raw(sl.at[dev[0] % 8], sa.at[me], k6 + j, k6 + me, dev) for j, dev in enumerate(peers)]
    for c in hop1: c.start()
    sa[me] = sl[me]
    for dev in peers: pltpu.make_async_copy(sl.at[0], sa.at[dev[0] % 8], recv.at[k6 + dev[0] % 8]).wait()
    tot = sa[0]
    for k in range(1, 8): tot = tot + sa[k]
    sb[t] = tot
    hop2 = [raw(sb.at[t], sb.at[t], k7 + r, k7 + t, P.zed(r)) for r in (1, 2, 3)]
    for c in hop2: c.start()
    for s in sh: s.c()
    for r in (1, 2, 3): pltpu.make_async_copy(sb.at[(t + r) % 4], sb.at[(t + r) % 4], recv.at[k7 + (t + r) % 4]).wait()
    sc[me] = sb[0] + sb[1] + sb[2] + sb[3]
    hop3 = [raw(sc.at[me], sc.at[me], k8 + j, k8 + me, dev) for j, dev in enumerate(peers)]
    for c in hop3: c.start()
    for h in range(2): pltpu.make_async_copy(w2.at[h], w2.at[h], recv.at[k5 + h]).wait()
    f_w[...] = (f32(w2[0]) + f32(w2[1])).astype(BF)
    shw.a(); shw.b(); shw.c()
    for dev in peers: pltpu.make_async_copy(sc.at[0], sc.at[dev[0] % 8], recv.at[k8 + dev[0] % 8]).wait()
    small_o[...] = sc[...]
    for s in sh + [shw]: s.end()
    for c in hop1 + hop2 + hop3: c.wait_send()
    for c in started: c.wait_send()
    for cond, c in guarded: pl.when(cond)(c.wait_send)

def second(x, wt, ck, ids, proj, lse, of, ga, tok, gm, s_ow, s_up, s_dn, s4, gupb, g1):
    S = jax.ShapeDtypeStruct; V = pltpu.VMEM
    n, D = tok.shape; N = 4 * n; H = n // 2; L = D // 2
    w = wt.shape[0]; lw = w // 3; heads = lw // HD
    a, q, o = s_ow.shape[1] // 4, s_up.shape[1] // 4, w // 4
    any_ = pl.BlockSpec(memory_space=pl.ANY); vm = pl.BlockSpec(memory_space=pltpu.VMEM)
    outs = [(S((n, D), F32), vm), (S((4 * a, D), BF), any_), (S((4 * q, D), BF), any_), (S((4 * q, D), BF), any_), (S((w, D), BF), any_), (S((8, 8, D), F32), vm)]
    sc = [V((4, n, D), BF), V((w, N), F32), V((heads, 128, N), BF), V((heads, N, 128), BF), V((heads, N, 128), BF), V((heads, HD, N), BF),
          V((heads, N, 128), BF), V((heads, 128, N), BF), V((heads, N, 128), BF), V((heads, N, 128), F32), V((w, N), F32), V((w, n), BF),
          V((w, D), F32), V((w, D), BF), V((4, n, D), BF), V((4, H, D), BF), V((4, H, D), BF), V((2, H, D), BF), V((n, D), F32),
          V((128, 256), F32), V((256, 128), F32), V((256, 128), F32),
          V((4, 2, q, L), BF), V((4, 2, q, L), BF), V((4, 2, a, L), BF), V((4, 2, a, L), BF), V((4, 2, q, L), BF), V((4, 2, q, L), BF),
          V((4, a, L), BF), V((4, q, L), BF), V((4, q, L), BF), V((2, a, L), BF), V((2, q, L), BF), V((2, q, L), BF),
          V((2, a, L), BF), V((2, q, L), BF), V((2, q, L), BF),
          V((3, o, D), BF), V((2, o, L), BF), V((o, L), BF), V((8, 8, D), F32), V((8, 8, D), F32), V((4, 8, D), F32), V((8, 8, D), F32),
          pltpu.SemaphoreType.DMA((160,)), pltpu.SemaphoreType.DMA((160,)), pltpu.SemaphoreType.DMA((40,))]
    return pl.pallas_call(second_kernel, out_shape=tuple(z[0] for z in outs),
        in_specs=[any_, vm, vm, vm, any_, vm, any_, vm, vm, vm, any_, any_, any_, vm, vm, vm], out_specs=tuple(z[1] for z in outs), scratch_shapes=sc,
        compiler_params=pltpu.CompilerParams(collective_id=1, has_side_effects=True, vmem_limit_bytes=60 * 2**20), name="attend_back_and_reduce",
    )(x, wt, ck, ids, proj, lse, of, ga, tok, gm, s_ow, s_up, s_dn, s4, gupb, g1)


def per_device(planes, tokens, segment_ids, cotangent, norm1_gain, norm1_shift, qkv_weight, conv_kernel, out_weight, out_bias, norm2_gain, norm2_shift, up_weight, up_bias, down_weight, down_bias):
    n, D = tokens.shape
    lw = qkv_weight.shape[2]
    row = lambda v: v.reshape(1, -1)
    wt = jnp.transpose(qkv_weight, (1, 2, 0)).reshape(3 * lw, D)
    x, ids, wtp, ckp, proj, lse, of, res, gm, ga, s_ow, s_up, s_dn, s4, gupb = first(
        tokens, row(segment_ids), cotangent, wt, conv_kernel, out_weight, up_weight, down_weight, row(up_bias), row(norm1_gain), row(norm1_shift),
        row(out_bias), row(norm2_gain), row(norm2_shift), row(down_bias))
    gt, ow_o, up_o, dn_o, w_o, sm = second(x, wtp, ckp, ids, proj, lse, of, ga, tokens, gm, s_ow, s_up, s_dn, s4, gupb, row(norm1_gain))
    t = lax.axis_index("tensor")
    f = lambda v: v.astype(F32)
    sums = (f(w_o), f(ow_o), f(up_o), f(dn_o), sm[:, :6].reshape(48, D))
    if planes is not None:
        sums = lax.psum(sums, "dp", axis_index_groups=planes)
    w_o, ow_o, up_o, dn_o, sm = sums
    gqkv = jnp.transpose(w_o.reshape(3, lw, D), (2, 0, 1))
    gck = lax.dynamic_slice(sm, (10 + 9 * t, 0), (9, lw)).reshape(3, 3, lw)
    gub = lax.dynamic_slice(sm, (6 + t, 0), (1, D)).reshape(-1)
    return (res, gt, sm[4], sm[5], gqkv, gck, ow_o, sm[0], sm[1], sm[2], up_o, gub, dn_o, sm[3])


def solution(mesh):
    dp = mesh.shape["dp"]
    planes = None
    if dp > 8:
        planes = [[8 * k + j for k in range(dp // 8)] for j in range(8)]
    rows_, rep = P_(("dp", "tensor"), None), P_()
    third, cols, first = P_(None, None, "tensor"), P_(None, "tensor"), P_("tensor", None)
    return jax.shard_map(
        functools.partial(per_device, planes),
        mesh=mesh,
        in_specs=(rows_, P_(("dp", "tensor")), rows_, rep, rep, third, third, first, rep, rep, rep, cols, P_("tensor"), first, rep),
        out_specs=(rows_, rows_, rep, rep, third, third, first, rep, rep, rep, cols, P_("tensor"), first, rep),
        check_vma=False,
    )
```

```python
import functools
import jax, jax.numpy as jnp
from jax import lax
from jax.experimental import pallas as pl
from jax.experimental.pallas import tpu as pltpu
from jax.sharding import PartitionSpec as P_

HD=64
BF=jnp.bfloat16; F32=jnp.float32
BIG=1e30
def nt(a,b): return lax.dot_general(a,b,(((1,),(1,)),((),())),preferred_element_type=F32)
def tn(a,b): return lax.dot_general(a,b,(((0,),(0,)),((),())),preferred_element_type=F32)
def nn(a,b): return jnp.dot(a,b,preferred_element_type=F32)

def keep_rows(ids):
    n=ids.shape[1]
    pos=lax.broadcasted_iota(jnp.int32,(1,n),1)
    out=[]
    for j in (1,2):
        prev=pltpu.roll(ids,j,1)
        out.append(jnp.where((prev==ids)&(pos>=j),1.0,0.0).astype(F32))
    return out

def feats(ids,rows,kind):
    n=ids.shape[1]
    r=lax.broadcasted_iota(jnp.int32,(rows,n),0)
    idb=jnp.broadcast_to(ids,(rows,n))
    if kind=="q":
        return jnp.where((r<4)&(idb!=r),-BIG,0.0).astype(F32)
    return jnp.where(((r<4)&(idb==r))|((r>=4)&(r<7)),1.0,0.0).astype(F32)

def split3(x):
    hi=x.astype(BF).astype(F32); r=x-hi; mid=r.astype(BF).astype(F32); lo=r-mid
    return hi,mid,lo

EPS=1e-5
def ln(x):
    mu=jnp.mean(x,-1,keepdims=True)
    c=x-mu
    inv=lax.rsqrt(jnp.mean(c*c,-1,keepdims=True)+EPS)
    return c*inv,inv
def ln_back(g,unit,inv,gain):
    s=g*gain
    return (s-jnp.mean(s,-1,keepdims=True)-unit*jnp.mean(s*unit,-1,keepdims=True))*inv
MESH=pl.DeviceIdType.MESH

class Place:
    def __init__(self):
        d=lax.axis_index("dp"); t=lax.axis_index("tensor")
        self.d,self.t=d,t
        b=d%2; p=t//2; q=t%2; base=d-b
        self.b,self.p,self.q,self.base=b,p,q,base
        self.same=1-(b+p)%2
        self.home=self.same==1
        self.near=(p+q)%2==1
        self.member=2*q+b
        self.quarter=(d//2)%4
        self.sib=(base+1-b,t)
        self.opp=(d,2*p+1-q)
        self.cross=(base+1-b,2*p+1-q)
        self.other=(d,2*(1-p)+q)
        self.dest=(base+q,2*b+p)
        self.source=(base+p,2*q+b)
        self.fixed=jnp.logical_and(b==p,b==q)
        dx=d+2-4*((d//2)%2); dy=d+4-8*((d//4)%2)
        self.x=(dx,t); self.y=(dy,t); self.xy=(dx+dy-d,t)
    def zed(self,r): return (self.d,(self.t+r)%4)
    def column(self):
        base=self.d-self.b
        out=[]
        for r in range(1,4):
            out.append((self.d,(self.t+r)%4))
        for r in range(4):
            out.append((base+1-self.b,(self.t+r)%4))
        return out

def meet(peers):
    bar=pltpu.get_barrier_semaphore()
    for dev in peers:
        pl.semaphore_signal(bar,inc=1,device_id=dev,device_id_type=MESH)
    pl.semaphore_wait(bar,len(peers))

class Net:
    def __init__(self,send,recv):
        self.send,self.recv,self.k=send,recv,0
    def to(self,src,dst,dev):
        k=self.k; self.k+=1
        return pltpu.make_async_remote_copy(src_ref=src,dst_ref=dst,send_sem=self.send.at[k],recv_sem=self.recv.at[k],device_id=dev,device_id_type=MESH)

class Swap:
    def __init__(self,net,src,dst,dev,fixed):
        self.r=net.to(src,dst,dev); self.fixed=fixed
        self.l=pltpu.make_async_copy(src,dst,net.recv.at[net.k-1])
    def start(self):
        pl.when(jnp.logical_not(self.fixed))(self.r.start)
        pl.when(self.fixed)(self.l.start)
    def wait_recv(self): self.l.wait()
    def wait_send(self): pl.when(jnp.logical_not(self.fixed))(self.r.wait_send)

def rows(ref,start,size): return ref.at[pl.ds(start,size)]

def lanes(start,size): return pl.ds(pl.multiple_of(start,128),size)
def rws(start,size): return pl.ds(pl.multiple_of(start,16),size)


class ToHeads:
    def __init__(self,net,P,src,dst):
        self.k=net.k; net.k+=4
        self.P,self.net,self.dst=P,net,dst
        self.far=[]
        for mm in range(4):
            c=pltpu.make_async_remote_copy(src_ref=src(mm),dst_ref=dst.at[P.t],send_sem=net.send.at[self.k+mm],recv_sem=net.recv.at[self.k+P.t],
                                           device_id=(P.base+mm%2,2*P.b+mm//2),device_id_type=MESH)
            l=pltpu.make_async_copy(src(mm),dst.at[P.t],net.recv.at[self.k+P.t])
            self.far.append((jnp.logical_and(P.home,P.member==mm),c,l))
    def start(self):
        for me,c,l in self.far:
            pl.when(jnp.logical_not(me))(c.start)
            pl.when(me)(l.start)
    def wait_recv(self):
        for s in range(4):
            pltpu.make_async_copy(self.dst.at[s],self.dst.at[s],self.net.recv.at[self.k+s]).wait()
    def wait_send(self):
        for me,c,l in self.far: pl.when(jnp.logical_not(me))(c.wait_send)

def mix2(v, cks, r, c, keeps):
    out = cks[pl.ds(r, HD), c:c + 1] * v
    for j in (1, 2):
        out = out + cks[pl.ds(r, HD), 3 * j + c:3 * j + c + 1] * (pltpu.roll(v, j, 1) * keeps[j - 1])
    return out

def tap_columns(ckv, tmp, cks):
    lw = ckv.shape[2]
    tmp[...] = jnp.zeros(tmp.shape, F32)
    for j in range(3):
        for c in range(3):
            tmp[3 * j + c:3 * j + c + 1, 0:lw] = ckv[j, c:c + 1, :]
    cks[...] = tmp[...].T

NC = 4
def first_kernel(tok, ids, cot, wt, ck, ow, up, dn, vg1, vs1, vob, vg2, vs2, vdb, vub,
                 x_o, ids_o, wt_o, ck_o, proj_o, qt_o, qn_o, kk_o, kt_o, vn_o, of_o, res_o, gm_o, ga_in, ow_o, up_o, dn_o, l_ow, l_up, l_dn, small_o, gupb_o,
                 xv, xn, cotv, idv, wtv, ckv, tmp, cks, proj, qt, qn, kk, kt, vn, vt, att, attin, of, lse,
                 ow_a, up_a, dn_a, upb_a, sec, act, gh, gsec, gms, gas, c_ow, c_up, c_dn, send, recv, lsem, wsem):
    P = Place()
    meet(P.column() + [P.x, P.y, P.xy])
    net = Net(send, recv)
    n, D = tok.shape
    N = 4 * n
    heads = wt.shape[0] // (3 * HD)
    lw = heads * HD
    R = n // NC; H = R // 2
    m = P.member; t = P.t
    sends = []
    def later(src, dst, dev):
        c = net.to(src, dst, dev); sends.append(c); return c
    def push(src, dst, dev):
        c = later(src, dst, dev); c.start(); return c
    def swap(src, dst, dev):
        c = Swap(net, src, dst, dev, P.fixed); sends.append(c); return c
    Q = wt.shape[0] // 4
    w0 = pl.multiple_of(P.quarter * Q, 16)
    idg = ToHeads(net, P, lambda mm: ids, idv)
    idg.start()
    wq = swap(rows(wt, w0, Q), rows(wtv, w0, Q), P.dest); wq.start()
    ckc = swap(ck, ckv, P.dest); ckc.start()
    cotl = pltpu.make_async_copy(cot, cotv, lsem.at[15]); cotl.start()
    def part(ref, tt, k):
        L = ref.shape[2] // 2; r = ref.shape[1] // 4
        return ref.at[tt, pl.ds(pl.multiple_of(k * r, 16), r), pl.ds(pl.multiple_of(P.b * L, 128), L)]
    def part_in(ref):
        L = ref.shape[1] // 2; r = ref.shape[0] // 4
        return ref.at[pl.ds(pl.multiple_of(P.quarter * r, 16), r), pl.ds(pl.multiple_of(P.b * L, 128), L)]
    qx = (P.x[0] // 2) % 4; qy = (P.y[0] // 2) % 4; qd = (P.xy[0] // 2) % 4
    order = [t, t - 1 + 2 * (1 - (t + 3) // 4), 2 + t // 2 - 2 * (t // 3), 3 - 3 * (t // 2)]
    guarded = []
    right = (P.d, (t + 1) % 4); left = (P.d, (t + 3) % 4)
    class Spread:
        def __init__(self, ins, alls, b0):
            self.zr = net.k; net.k += 4 * len(ins)
            self.w = len(ins)
            def z_push(src, tt, j, cond, dev):
                k = net.k; net.k += 1
                c = pltpu.make_async_remote_copy(src_ref=src, dst_ref=part(alls[j], tt, P.quarter), send_sem=send.at[k],
                                                 recv_sem=recv.at[self.zr + self.w * tt + j], device_id=dev, device_id_type=MESH)
                guarded.append((cond, c))
                return lambda: pl.when(cond)(c.start)
            self.first = [z_push(part_in(ins[j]), t, j, cond, dev) for j in range(self.w) for cond, dev in ((t < 3, right), (t > 0, left))]
            self.steps = {}
            for r in (1, 2, 3):
                tt = order[r]
                arrive = []
                for j in range(self.w):
                    z = part(alls[j], tt, P.quarter)
                    wait = pltpu.make_async_copy(z, z, recv.at[self.zr + self.w * tt + j])
                    arrive.append([wait.wait, z_push(z, tt, j, jnp.logical_and(tt < t, t < 3), right),
                                   z_push(z, tt, j, jnp.logical_and(tt > t, t > 0), left)])
                mine = [part(a, tt, P.quarter) for a in alls]
                bx = [part(a, tt, qx) for a in alls]; by = [part(a, tt, qy) for a in alls]; bd = [part(a, tt, qd) for a in alls]
                ax = [later(z, z, P.x) for z in mine]; ay = [later(z, z, P.y) for z in mine]; asib = [later(z, z, P.sib) for z in mine]
                dx = [later(z, z, P.y) for z in bx[:b0]]; dy = [later(z, z, P.x) for z in by[b0:]]
                xs = [later(z, z, P.sib) for z in bx]; ys = [later(z, z, P.sib) for z in by]; ds_ = [later(z, z, P.sib) for z in bd]
                self.steps[r] = (arrive, ax, ay, asib, dx, dy, xs, ys, ds_)
        def start(self):
            for f in self.first: f()
        def a(self, r):
            arrive, ax, ay, asib = self.steps[r][:4]
            for step in arrive:
                for f in step: f()
            for c in ax + ay + asib: c.start()
        def b(self, r):
            _, ax, ay, _, dx, dy, xs, ys, _ = self.steps[r]
            for c in ax: c.wait_recv()
            for c in dx + xs: c.start()
            for c in ay: c.wait_recv()
            for c in dy + ys: c.start()
        def c(self, r):
            _, _, _, _, dx, dy, _, _, ds_ = self.steps[r]
            for c in dx + dy: c.wait_recv()
            for c in ds_: c.start()
        def end(self, r):
            _, _, _, asib, _, _, xs, ys, ds_ = self.steps[r]
            for c in asib + xs + ys + ds_: c.wait_recv()
    so = Spread((ow,), (ow_a,), 1)
    sw = Spread((up, dn), (up_a, dn_a), 1)
    own = [pltpu.make_async_copy(a, b.at[t], lsem.at[j]) for j, (a, b) in enumerate(((ow, ow_a), (up, up_a), (dn, dn_a)))]
    for c in own: c.start()
    upb_a[t] = vub[...].reshape(1, -1)
    bias = [push(upb_a.at[t], upb_a.at[t], P.zed(r)) for r in (1, 2, 3)]
    opp_shard = 2 * P.p + 1 - P.q
    target = P.same * opp_shard + (1 - P.same) * (1 + P.b)
    far_shards = (2 * (1 - P.p), 2 * (1 - P.p) + 1)
    ka = net.k; kb = ka + 4 * NC; kc = kb + NC; kd = kc + 4 * NC; net.k = kd + 4 * NC
    def raw(src, dst, ks, kr, dev):
        return pltpu.make_async_remote_copy(src_ref=src, dst_ref=dst, send_sem=send.at[ks], recv_sem=recv.at[kr], device_id=dev, device_id_type=MESH)
    sent = []
    def give_piece(k):
        z = pl.ds(k * R, R)
        unit, _ = ln(tok[k * R:(k + 1) * R, :].astype(F32))
        xn[k * R:(k + 1) * R, :] = (unit * vg1[...].reshape(1, -1) + vs1[...].reshape(1, -1)).astype(BF)
        for h in range(2):
            zh = pl.ds(k * R + h * H, H)
            c = raw(xn.at[zh], xv.at[t, zh], ka + 4 * k + h, ka + 4 * k + t, (P.base + h, target)); c.start(); sent.append(c)
        c = raw(xn.at[z], xv.at[t, z], kb + k, kb + k, P.sib)
        pl.when(P.home)(c.start); guarded.append((P.home, c))
    def relay(k):
        zb = pl.ds(pl.multiple_of(k * R + P.b * H, 16), H)
        for j, s in enumerate((opp_shard,) + far_shards):
            blk = xv.at[s, zb]
            if j == 0:
                pltpu.make_async_copy(blk, blk, recv.at[ka + 4 * k + s]).wait()
            else:
                on = raw(blk, blk, kd + 4 * k + j, kd + 4 * k + s, P.opp)
                @pl.when(P.near)
                def _():
                    pltpu.make_async_copy(blk, blk, recv.at[ka + 4 * k + s]).wait()
                    on.start()
                guarded.append((P.near, on))
                @pl.when(jnp.logical_not(P.near))
                def _():
                    pltpu.make_async_copy(blk, blk, recv.at[kd + 4 * k + s]).wait()
            c = raw(blk, blk, kc + 4 * k + j, kc + 4 * k + s, P.sib); c.start(); sent.append(c)
    so.start()
    give_piece(0); give_piece(1)
    sw.start()
    relay(0)
    pass
    give_piece(2)
    wq.wait_recv()
    wf = [push(rows(wtv, w0, Q), rows(wtv, w0, Q), dev) for dev in (P.x, P.y, P.xy)]
    relay(1)
    so.a(1)
    give_piece(3)
    relay(2)
    so.a(2); sw.a(1)
    relay(3)
    so.a(3)
    @pl.when(P.home)
    def _(): xv[t] = xn[...]
    for c in wf: c.wait_recv()
    def project(s):
        proj[:, pl.ds(pl.multiple_of(s * n, 128), n)] = nt(wtv[...], xv[s])
    @pl.when(jnp.logical_not(P.home))
    def _():
        for k in range(NC): pltpu.make_async_copy(xv.at[t, pl.ds(k * R, R)], xv.at[t, pl.ds(k * R, R)], recv.at[kb + k]).wait()
    project(t)
    so.b(1); so.b(2)
    for k in range(NC):
        zo = pl.ds(pl.multiple_of(k * R + (1 - P.b) * H, 16), H)
        pltpu.make_async_copy(xv.at[opp_shard, zo], xv.at[opp_shard, zo], recv.at[kc + 4 * k + opp_shard]).wait()
    project(opp_shard)
    so.b(3); so.c(1); sw.a(2)
    for k in range(NC):
        zo = pl.ds(pl.multiple_of(k * R + (1 - P.b) * H, 16), H)
        for s in far_shards:
            pltpu.make_async_copy(xv.at[s, zo], xv.at[s, zo], recv.at[kc + 4 * k + s]).wait()
    for s in far_shards: project(s)
    so.c(2); so.c(3)
    idg.wait_recv()
    ckc.wait_recv()
    outs = [pltpu.make_async_copy(a, b, lsem.at[4 + k]) for k, (a, b) in enumerate(
        ((xv, x_o), (wtv, wt_o), (proj, proj_o), (ckv, ck_o)))]
    for c in outs: c.start()
    idrow = jnp.concatenate([idv[s] for s in range(4)], axis=1)
    idv_out = pltpu.make_async_copy(idv, ids_o, lsem.at[9]); idv_out.start()
    keeps = keep_rows(idrow)
    tap_columns(ckv, tmp, cks)
    fq = feats(idrow, 64, "q").astype(BF); fk = feats(idrow, 64, "k")
    qt[64:128, :] = fq
    vt[64:80, :] = jnp.ones((16, N), BF)
    tri = lax.broadcasted_iota(jnp.int32, (n, n), 0) <= lax.broadcasted_iota(jnp.int32, (n, n), 1)
    eb = net.k; net.k += 4 * heads
    def give(h, tt):
        r = pl.ds(pl.multiple_of(h * HD, HD), HD)
        return raw(att.at[tt, r], attin.at[m, r], eb + 4 * h + tt, eb + 4 * h + m, (P.base + P.p, tt))
    def not_me(tt): return jnp.logical_not(jnp.logical_and(P.home, t == tt))
    def not_mine(mm): return jnp.logical_not(jnp.logical_and(P.home, m == mm))
    def at(*fs):
        def run():
            for f, r in fs: f(r)
        return run
    turns = {0: at((sw.b, 1),(sw.a, 3)), 1: at((sw.b, 2), (sw.c, 1))}
    def head(h, _):
        for hh, fs in turns.items(): pl.when(h == hh)(fs)
        r = pl.multiple_of(h * HD, HD)
        def part_rows(c): return proj[pl.ds(pl.multiple_of(c * lw + h * HD, HD), HD), :]
        q = mix2(part_rows(0), cks, r, 0, keeps)
        qt[0:64, :] = (q.astype(BF).astype(F32) * 0.125).astype(BF)
        k = mix2(part_rows(1), cks, r, 1, keeps)
        kk[...] = jnp.concatenate([k, fk], 0).T.astype(BF)
        vt[0:64, :] = mix2(part_rows(2), cks, r, 2, keeps).astype(BF)
        for iq in range(4):
            qs = iq * n
            qb = qt[:, qs:qs + n]
            ss = []
            for j in range(iq + 1):
                s = nn(kk[j * n:(j + 1) * n, :], qb)
                if j == iq: s = jnp.where(tri, s, -BIG)
                ss.append(s)
            mx = jnp.max(ss[0], axis=0, keepdims=True)
            for s in ss[1:]: mx = jnp.maximum(mx, jnp.max(s, axis=0, keepdims=True))
            o = jnp.zeros((80, n), F32)
            for j, s in enumerate(ss):
                o = o + nn(vt[:, j * n:(j + 1) * n], jnp.exp(s - mx).astype(BF))
            l = o[64:65, :]
            f = o[0:64, :] / l
            of[pl.ds(r, HD), qs:qs + n] = f
            att[iq, pl.ds(r, HD), :] = f.astype(BF)
            lse[h, :, qs:qs + n] = jnp.broadcast_to(mx + jnp.log(l), (8, n))
        for tt in range(4): pl.when(not_me(tt))(give(h, tt).start)
        return 0
    lax.fori_loop(0, heads, head, 0)
    @pl.when(P.home)
    def _(): attin[m] = att[t]
    ends = [pltpu.make_async_copy(a, b, lsem.at[11 + k]) for k, (a, b) in enumerate(((of, of_o),))]
    for c in ends: c.start()
    sw.c(2); sw.b(3)
    for r in (1, 2, 3): so.end(r)
    for c in own: c.wait()
    for h in range(heads):
        r = pl.ds(h * HD, HD)
        for mm in range(4):
            pl.when(not_mine(mm))(pltpu.make_async_copy(attin.at[mm, r], attin.at[mm, r], recv.at[eb + 4 * h + mm]).wait)
            pl.when(not_me(mm))(give(h, mm).wait_send)
    attT = attin[...].reshape(4 * lw, n)
    gms[...] = tok[...].astype(F32) + tn(attT, ow_a[...].reshape(4 * lw, D)) + vob[...].reshape(1, -1)
    unit, inv = ln(gms[...])
    sec[...] = (unit * vg2[...].reshape(1, -1) + vs2[...].reshape(1, -1)).astype(BF)
    for c in bias: c.wait_recv()
    sw.c(3)
    cotl.wait()
    gsec[...] = jnp.zeros_like(gsec)
    def chain(tt):
        rl = jnp.maximum(nn(sec[...], up_a[tt]) + upb_a[tt], 0.0)
        act[tt] = (rl * rl).astype(BF)
        g = (nt(cotv[...], dn_a[tt]) * (2.0 * rl)).astype(BF)
        gh[tt] = g
        gupb_o[tt] = jnp.sum(g.astype(F32), 0, keepdims=True)
        gsec[...] += nt(g, up_a[tt])
    chain(order[0])
    pass
    sw.end(1); chain(order[1])
    pass
    sw.end(2); chain(order[2])
    pass
    sw.end(3); chain(order[3])
    mid = gms[...]
    unit, inv = ln(mid)
    gs = gsec[...]
    cf = cotv[...].astype(F32)
    gm = cf + ln_back(gs, unit, inv, vg2[...].reshape(1, -1))
    gmb = gm.astype(BF)
    gb = ToHeads(net, P, lambda mm: gas.at[mm], ga_in)
    for mm in range(4):
        gas[mm] = nt(ow_a[mm], gmb).astype(BF)
    gb.start()
    gsec[...] = gm
    gmo = pltpu.make_async_copy(gsec, gm_o, lsem.at[14]); gmo.start()
    small_o[0:1] = jnp.sum(gm, 0, keepdims=True)
    small_o[1:2] = jnp.sum(gs * unit, 0, keepdims=True)
    small_o[2:3] = jnp.sum(gs, 0, keepdims=True)
    small_o[3:4] = jnp.sum(cf, 0, keepdims=True)
    small_o[4:8] = jnp.zeros((4, D), F32)
    out = mid + vdb[...].reshape(1, -1)
    for b in range(4): out = out + nn(act[b], dn_a[b])
    res_o[...] = out.astype(BF)
    for c in sends: c.wait_send()
    for cond, c in guarded: pl.when(cond)(c.wait_send)
    L = D // 2
    lo, lx = P.b * L, (1 - P.b) * L
    blocks = [1 - P.q, 3 - P.q, 2 * (1 - P.p) + P.q, t]
    ow_a[...] = nn(attT, gmb).astype(BF).reshape(ow_a.shape)
    trios = ((ow_a, c_ow, ow_o), (dn_a, c_dn, dn_o), (up_a, c_up, up_o))
    halves, fin = [], []
    def grads(k):
        tt = blocks[k]
        dn_a[tt] = tn(act[tt], cotv[...]).astype(BF)
        up_a[tt] = tn(sec[...], gh[tt]).astype(BF)
        cs = []
        for g, cref, _ in trios:
            c = net.to(g.at[tt, :, lanes(lx, L)], cref.at[tt], P.sib); c.start(); cs.append(c)
        halves.append(cs)
    def cores(k):
        tt = blocks[k]
        for j, (g, cref, o) in enumerate(trios):
            halves[k][j].wait_recv()
            cref[tt] = (cref[tt].astype(F32) + g[tt, :, lanes(lo, L)].astype(F32)).astype(BF)
            z = pltpu.make_async_copy(cref.at[tt], o.at[tt], wsem.at[3 * k + j]); z.start(); fin.append(z)
    grads(0); grads(1)
    cores(0)
    ro, ru = ow.shape[0] // 4, up.shape[0] // 4
    pc = []
    def plane(j):
        for src, dst, r_, ks, dev in ((c_ow, l_ow, ro, (qx, qd), P.x), (c_up, l_up, ru, (qx, qd), P.x), (c_dn, l_dn, ru, (qy, qd), P.y)):
            for i, k in enumerate(ks):
                c = net.to(src.at[blocks[j], rws(k * r_, r_)], dst.at[j, i], dev); c.start(); pc.append(c)
    plane(0)
    grads(2); cores(1)
    plane(1)
    grads(3)
    r8 = lax.broadcasted_iota(jnp.int32, (64, N), 0)
    zl = jnp.zeros((64, N), F32)
    fqf = feats(idrow, 64, "q")
    pieces = ((qt, qt_o), (qn, qn_o), (kk, kk_o), (kt, kt_o), (vn, vn_o))
    def prepare(h, _):
        r = pl.multiple_of(h * HD, HD)
        def part_rows(c): return proj[pl.ds(pl.multiple_of(c * lw + h * HD, HD), HD), :]
        q = mix2(part_rows(0), cks, r, 0, keeps).astype(BF).astype(F32) * 0.125
        hi, mid_, low = split3(-lse[h, 0:1, :])
        k = mix2(part_rows(1), cks, r, 1, keeps)
        v = mix2(part_rows(2), cks, r, 2, keeps)
        @pl.when(h > 0)
        def _():
            for j, (a, o) in enumerate(pieces): pltpu.make_async_copy(a, o.at[0], wsem.at[12 + j]).wait()
        qt[0:64, :] = q.astype(BF)
        qt[64:128, :] = (fqf + jnp.where(r8 == 4, hi, 0.0) + jnp.where(r8 == 5, mid_, 0.0) + jnp.where(r8 == 6, low, 0.0)).astype(BF)
        qn[...] = jnp.concatenate([zl, q], 0).T.astype(BF)
        kt[...] = k.astype(BF)
        kk[...] = jnp.concatenate([k, fk], 0).T.astype(BF)
        vn[...] = jnp.concatenate([v, jnp.where(r8 < 3, 1.0, 0.0)], 0).T.astype(BF)
        for j, (a, o) in enumerate(pieces): pltpu.make_async_copy(a, o.at[h], wsem.at[12 + j]).start()
        return 0
    lax.fori_loop(0, heads, prepare, 0)
    cores(2); cores(3)
    for j, (a, o) in enumerate(pieces): pltpu.make_async_copy(a, o.at[0], wsem.at[12 + j]).wait()
    for cs in halves:
        for c in cs: c.wait_send()
    for c in sent: c.wait_send()
    idg.wait_send()
    for c in outs + [idv_out, gmo] + ends + fin: c.wait()
    for c in pc: c.wait()
    gb.wait_send()
    gb.wait_recv()

def first(tok, ids, cot, wt, ck, ow, up, dn, *vecs):
    n, D = tok.shape; S = jax.ShapeDtypeStruct; V = pltpu.VMEM
    lw = wt.shape[0] // 3; heads = lw // HD; N = 4 * n; fb = up.shape[1]
    any_ = pl.BlockSpec(memory_space=pl.ANY); vm = pl.BlockSpec(memory_space=pltpu.VMEM)
    outs = [(S((4, n, D), BF), any_), (S((4, 1, n), jnp.int32), any_), (S(wt.shape, BF), any_), (S(ck.shape, F32), any_),
            (S((3 * lw, N), F32), any_), (S((heads, 128, N), BF), any_), (S((heads, N, 128), BF), any_), (S((heads, N, 128), BF), any_),
            (S((heads, HD, N), BF), any_), (S((heads, N, 128), BF), any_), (S((lw, N), F32), any_),
            (S((n, D), BF), vm), (S((n, D), F32), any_), (S((4, lw, n), BF), any_),
            (S((4, lw, D // 2), BF), any_), (S((4, D, fb // 2), BF), any_), (S((4, fb, D // 2), BF), any_),
            (S((2, 2, lw // 4, D // 2), BF), any_), (S((2, 2, D // 4, D // 2), BF), any_), (S((2, 2, fb // 4, D // 2), BF), any_), (S((8, D), F32), vm), (S((4, 1, fb), F32), vm)]
    return pl.pallas_call(first_kernel, out_shape=tuple(o[0] for o in outs),
        in_specs=[vm] + [any_] * 7 + [vm] * 7, out_specs=tuple(o[1] for o in outs),
        scratch_shapes=[V((4, n, D), BF), V((n, D), BF), V((n, D), BF), V((4, 1, n), jnp.int32), V(wt.shape, BF), V(ck.shape, F32), V((128, 256), F32), V((256, 128), F32),
                        V((3 * lw, N), F32), V((128, N), BF), V((N, 128), BF), V((N, 128), BF), V((HD, N), BF), V((N, 128), BF), V((80, N), BF), V((4, lw, n), BF), V((4, lw, n), BF), V((lw, N), F32), V((heads, 8, N), F32),
                        V((4, lw, D), BF), V((4, D, fb), BF), V((4, fb, D), BF), V((4, 1, fb), F32),
                        V((n, D), BF), V((4, n, fb), BF), V((4, n, fb), BF), V((n, D), F32), V((n, D), F32), V((4, lw, n), BF),
                        V((4, lw, D // 2), BF), V((4, D, fb // 2), BF), V((4, fb, D // 2), BF),
                        pltpu.SemaphoreType.DMA((240,)), pltpu.SemaphoreType.DMA((240,)), pltpu.SemaphoreType.DMA((16,)), pltpu.SemaphoreType.DMA((20,))],
        compiler_params=pltpu.CompilerParams(collective_id=0, has_side_effects=True, vmem_limit_bytes=60 * 2**20),
        name="forward_and_feed",
    )(tok, ids, cot, wt, ck, ow, up, dn, *vecs)
def second_kernel(x_h, wt, ck, ids, proj_h, qt_h, qn_h, kk_h, kt_h, vn_h, of_h, ga, tok, gm, s_ow, s_up, s_dn, l_ow, l_up, l_dn, s4, gupb, vec,
                  gt_o, ow_o, up_o, dn_o, w_o, small_o,
                  x, proj, qt, qn, kk, kt, vn, dot, don, dkv, gconv, gp, gw, gwb, gfs, land1, land2, fin, g_s,
                  tmp, cks, cacc, own_x, own_y, own_o, x_ow, x_up, y_dn, z_ow, z_up, z_dn, o_ow, o_up, o_dn, f_ow, f_up, f_dn,
                  w1, w2, f_w, sl, sa, sb, sc, la, lb, send, recv, lsem):
    P = Place()
    plane = []
    for r in (P.x, P.y, P.xy): plane += [r, (r[0] + 1 - 2 * P.b, r[1])]
    meet(P.column() + plane)
    net = Net(send, recv)
    n, D = tok.shape; N = 4 * n; H = n // 2; L = D // 2
    heads = wt.shape[0] // (3 * HD); lw = heads * HD
    m, t, b, p = P.member, P.t, P.b, P.p
    f32 = lambda v: v.astype(F32)
    started, guarded = [], []
    def later(src, dst, dev):
        c = net.to(src, dst, dev); started.append(c); return c
    def push(src, dst, dev):
        c = later(src, dst, dev); c.start(); return c
    def raw(src, dst, ks, kr, dev):
        return pltpu.make_async_remote_copy(src_ref=src, dst_ref=dst, send_sem=send.at[ks], recv_sem=recv.at[kr], device_id=dev, device_id_type=MESH)
    qr = P.quarter; qx = (P.x[0] // 2) % 4; qy = (P.y[0] // 2) % 4; qd = (P.xy[0] // 2) % 4
    lo = b * L
    ro, ru = s_ow.shape[1] // 4, s_up.shape[1] // 4
    blocks = [1 - P.q, 3 - P.q, 2 * (1 - p) + P.q, t]
    lc = [0]
    def local(src, dst):
        c = pltpu.make_async_copy(src, dst, lsem.at[lc[0]]); lc[0] += 1; c.start(); return c
    class Block:
        def __init__(self, j):
            tt = blocks[j]
            self.j, self.tt = j, tt
            q_ = lambda ref, k, r_: ref.at[tt, rws(k * r_, r_), :]
            self.p1x, self.p1y = [], []
            if j > 1:
                self.p1x = [later(q_(s_ow, k, ro), x_ow.at[j, i], P.x) for i, k in ((0, qx), (1, qd))] + \
                           [later(q_(s_up, k, ru), x_up.at[j, i], P.x) for i, k in ((0, qx), (1, qd))]
                self.p1y = [later(q_(s_dn, k, ru), y_dn.at[j, i], P.y) for i, k in ((0, qy), (1, qd))]
            self.p3 = [later(x_ow.at[j, 1], z_ow.at[j], P.y), later(x_up.at[j, 1], z_up.at[j], P.y), later(y_dn.at[j, 1], z_dn.at[j], P.x)]
        def load(self):
            tt, j = self.tt, self.j
            q_ = lambda ref, k, r_: ref.at[tt, rws(k * r_, r_), :]
            self.loads = [local(q_(s_ow, k, ro), own_o.at[j, i]) for i, k in ((0, qr), (1, qy))] + \
                         [local(q_(s_up, k, ru), own_x.at[j, i]) for i, k in ((0, qr), (1, qy))] + \
                         [local(q_(s_dn, k, ru), own_y.at[j, i]) for i, k in ((0, qr), (1, qx))]
            if j < 2:
                self.loads += [local(a.at[j], z.at[j]) for a, z in ((l_ow, x_ow), (l_up, x_up), (l_dn, y_dn))]
        def a(self):
            if self.j > 1:
                for c in self.p1x + self.p1y: c.start()
        def b(self):
            j = self.j
            for c in self.loads: c.wait()
            for c in self.p1x + self.p1y: c.wait_recv()
            for z, o in ((x_ow, own_o), (x_up, own_x), (y_dn, own_y)):
                z[j] = (f32(z[j]) + f32(o[j])).astype(BF)
            for c in self.p3: c.start()
        def c(self):
            j = self.j
            for c in self.p3: c.wait_recv()
            for z, o in ((z_ow, x_ow), (z_up, x_up), (z_dn, y_dn)):
                z[j] = (f32(z[j]) + f32(o[j, 0])).astype(BF)
    B = [Block(j) for j in range(4)]
    zs = ((z_ow, o_ow, f_ow), (z_up, o_up, f_up), (z_dn, o_dn, f_dn))
    zz = [[later(z.at[j], o.at[j], P.opp) for j in (0, 1)] for z, o, f in zs]
    z2 = [later(z.at[2], f.at[0], P.other) for z, o, f in zs]
    def opp_send(j):
        for cc in zz: cc[j].start()
    def opp_add():
        for (z, o, f), cc in zip(zs, zz):
            for c in cc: c.wait_recv()
            z[2] = (f32(z[2]) + f32(o[1 - p])).astype(BF)
        for c in z2: c.start()
    outs = ((ow_o, f_ow, ro), (up_o, f_up, ru), (dn_o, f_dn, ru))
    def place(o, k, r_): return o.at[rws(k * r_, r_), lanes(lo, L)]
    class Share:
        def __init__(self, o, src, r_, by_x):
            self.own = (src, place(o, qr, r_))
            self.sx = later(src, place(o, qr, r_), P.x); self.sy = later(src, place(o, qr, r_), P.y); self.ss = later(src, place(o, qr, r_), P.sib)
            px, py, pd = place(o, qx, r_), place(o, qy, r_), place(o, qd, r_)
            self.dg = later(px, px, P.y) if by_x else later(py, py, P.x)
            self.by_x = by_x
            self.fx, self.fy, self.fd = later(px, px, P.sib), later(py, py, P.sib), later(pd, pd, P.sib)
        def a(self):
            for c in (self.sx, self.sy, self.ss): c.start()
            self.l = local(*self.own)
        def b(self):
            self.sx.wait_recv()
            if self.by_x: self.dg.start()
            self.fx.start()
            self.sy.wait_recv()
            if not self.by_x: self.dg.start()
            self.fy.start()
        def c(self):
            self.dg.wait_recv(); self.fd.start()
        def end(self):
            for c in (self.ss, self.fx, self.fy, self.fd): c.wait_recv()
            self.l.wait()
    sh = [Share(o, f.at[1], r_, bx) for (o, f, r_), bx in zip(outs, (True, True, False))]
    shw = Share(w_o, f_w, wt.shape[0] // 4, False)
    def final_add():
        for (z, o, f), c in zip(zs, z2):
            c.wait_recv()
            f[1] = (f32(f[0]) + f32(z[3]) + f32(o[p])).astype(BF)
    B[2].a()
    ldo = local(of_h, gconv.at[pl.ds(0, lw)])
    lda = [local(a, z) for a, z in ((qt_h, qt), (kk_h, kk), (vn_h, vn), (qn_h, qn), (kt_h, kt))]
    for j in range(4): B[j].load()
    ldp = local(proj_h, proj)
    ldx = local(x_h, x)
    idrow = jnp.concatenate([ids[s] for s in range(4)], axis=1)
    keeps = keep_rows(idrow)
    tap_columns(ck, tmp, cks)
    cacc[...] = jnp.zeros(cacc.shape, F32)
    r8 = lax.broadcasted_iota(jnp.int32, (64, N), 0)
    zl = jnp.zeros((64, N), F32)
    ldo.wait()
    def setup(h, _):
        r = pl.multiple_of(h * HD, HD)
        do = f32(jnp.concatenate([ga[s, pl.ds(r, HD), :] for s in range(4)], axis=1))
        inner = jnp.sum(do * gconv[pl.ds(r, HD), :], axis=0, keepdims=True)
        hi, mid, low = split3(-inner)
        f = jnp.where(r8 == 0, hi, 0.0) + jnp.where(r8 == 1, mid, 0.0) + jnp.where(r8 == 2, low, 0.0)
        dot[h, 0:64, :] = do.astype(BF); dot[h, 64:128, :] = f.astype(BF)
        don[h] = jnp.concatenate([do, zl], 0).T.astype(BF)
        return 0
    lax.fori_loop(0, heads, setup, 0)
    B[0].b(); B[1].b()
    B[3].a()
    for c in lda: c.wait()
    tri = lax.broadcasted_iota(jnp.int32, (n, n), 0) <= lax.broadcasted_iota(jnp.int32, (n, n), 1)
    opp_shard = 2 * p + 1 - P.q
    h0 = pl.multiple_of(b * H, 16); h1 = pl.multiple_of((1 - b) * H, 16)
    e1 = [later(gfs.at[s, pl.ds(h1, H)], land1.at[s], P.sib) for s in range(4)]
    k2 = net.k; k3 = k2 + 4; k4 = k3 + 4; net.k = k4 + 2
    def far_side(s): return s // 2 != p
    def to_opp(s):
        cond = jnp.logical_or(opp_shard == s, jnp.logical_and(far_side(s), jnp.logical_not(P.near)))
        return cond, raw(land1.at[s], land2.at[s], k2 + s, k2 + s, P.opp)
    def summing(s): return jnp.logical_or(t == s, jnp.logical_and(far_side(s), P.near))
    def to_owner(s):
        cond = jnp.logical_and(summing(s), jnp.logical_not(jnp.logical_and(P.home, t == s)))
        return cond, raw(land2.at[s], fin.at[b], k3 + s, k4 + b, (P.base + p, s))
    opps = [to_opp(s) for s in range(4)]; owners = [to_owner(s) for s in range(4)]
    guarded += opps + owners
    def s1(s): e1[s].start()
    def s2(s):
        e1[s].wait_recv()
        land1[s] = (f32(land1[s]) + f32(gfs[s, pl.ds(h0, H)])).astype(BF)
        cond, c = opps[s]; pl.when(cond)(c.start)
    def s3(s):
        @pl.when(summing(s))
        def _():
            pltpu.make_async_copy(land2.at[s], land2.at[s], recv.at[k2 + s]).wait()
            land2[s] = (f32(land2[s]) + f32(land1[s])).astype(BF)
        cond, c = owners[s]; pl.when(cond)(c.start)
    def rows_of(i, points):
        qs = i * n
        def head(h, _):
            for hh, f in points.items(): pl.when(h == hh)(f)
            dq = jnp.zeros((64, n), F32)
            for j in range(i + 1):
                js = j * n
                st = nn(kk[h, js:js + n, :], qt[h, :, qs:qs + n])
                pr = jnp.exp(st)
                if i == j: pr = jnp.where(tri, pr, 0.0)
                dp = nn(vn[h, js:js + n, :], dot[h, :, qs:qs + n])
                ds = (pr * dp).astype(BF)
                add = nn(pr.astype(BF), don[h, qs:qs + n, :]) + nn(ds, qn[h, qs:qs + n, :])
                if i == 3: dkv[h, js:js + n, :] = add
                else: dkv[h, js:js + n, :] += add
                dq = dq + nn(kt[h, :, js:js + n], ds)
            gconv[pl.ds(pl.multiple_of(h * HD, HD), HD), qs:qs + n] = dq * 0.125
            if i == 3: pl.when(h == 0)(ldp.wait)
            tt = dkv[h, qs:qs + n, :].T
            gconv[pl.ds(pl.multiple_of(2 * lw + h * HD, HD), HD), qs:qs + n] = tt[0:64]
            gconv[pl.ds(pl.multiple_of(lw + h * HD, HD), HD), qs:qs + n] = tt[64:128]
            for c in range(3):
                r = pl.ds(pl.multiple_of(c * lw + h * HD, HD), HD); rk = pl.ds(pl.multiple_of(h * HD, HD), HD)
                g = gconv[r, qs:qs + n]
                nxt = jnp.zeros((HD, 128), F32) if i == 3 else gconv[r, qs + n:qs + n + 128]
                gx = jnp.concatenate([g, nxt], 1)
                pc = proj[r, qs:qs + n]
                prv = jnp.zeros((HD, 128), F32) if i == 0 else proj[r, qs - 128:qs]
                px = jnp.concatenate([prv, pc], 1)
                o = cks[rk, c:c + 1] * g
                cacc[rk, c:c + 1] += jnp.sum(g * pc, axis=1, keepdims=True)
                for jj in (1, 2):
                    kr = keeps[jj - 1][:, qs:qs + n]
                    kn = jnp.zeros((1, 128), F32) if i == 3 else keeps[jj - 1][:, qs + n:qs + n + 128]
                    kg = gx * jnp.concatenate([kr, kn], 1)
                    cacc[rk, 3 * jj + c:3 * jj + c + 1] += jnp.sum(kg[:, 0:n] * pltpu.roll(px, jj, 1)[:, 128:], axis=1, keepdims=True)
                    o = o + cks[rk, 3 * jj + c:3 * jj + c + 1] * pltpu.roll(kg, n + 128 - jj, 1)[:, 0:n]
                gp[r, :] = o.astype(BF)
            return 0
        lax.fori_loop(0, heads, head, 0)
        gfs[i] = tn(gp[...], wt[...]).astype(BF)
        s1(i)
        if i == 3: ldx.wait()
        g = nn(gp[...], x[i])
        if i == 3: gw[...] = g
        else: gw[...] += g
    def at(*fs):
        def run():
            for f in fs: f()
        return run
    rows_of(3, {2: at(B[0].c, lambda: opp_send(0), B[1].c, lambda: opp_send(1))})
    rows_of(2, {0: at(B[2].b), 1: at(lambda: s2(3))})
    rows_of(1, {0: at(lambda: s3(3), B[2].c, B[3].b), 1: at(lambda: s2(2)), 2: at(opp_add)})
    rows_of(0, {0: at(lambda: s2(1), B[3].c), 1: at(lambda: s3(2))})
    Q = wt.shape[0] // 4
    gwb[...] = gw[...].astype(BF)
    wx = [push(gwb.at[rws(k * Q, Q)], w1.at[j], dev) for j, (k, dev) in enumerate(((qx, P.x), (qy, P.y), (qd, P.xy)))]
    me = P.d % 8
    peers = plane + [P.sib]
    sl[...] = jnp.zeros(sl.shape, F32)
    def put(row, v): sl[row // 6, pl.ds(row % 6, 1), 0:v.shape[1]] = v
    for k in range(4): put(k, s4[k:k + 1])
    for k in range(4): put(6 + k, gupb[k])
    ct = cacc[...].T
    for k in range(9): put(10 + 9 * m + k, ct[k:k + 1, 0:lw])
    k6 = net.k; k7 = k6 + 8; k8 = k7 + 4; k9 = k8 + 8; ka = k9 + 8; k5 = ka + 4; net.k = k5 + 2
    hop1 = [raw(sl.at[dev[0] % 8], sa.at[me], k6 + j, k6 + me, dev) for j, dev in enumerate(peers)]
    for c in hop1: c.start()
    sa[me] = sl[me]
    s2(0); s3(1)
    unit, inv = ln(f32(tok[...]))
    for c in wx: c.wait_recv()
    w1[0] = (f32(w1[0]) + f32(w1[1]) + f32(w1[2]) + f32(gwb[rws(qr * Q, Q)])).astype(BF)
    for h in range(2):
        mine = jnp.logical_and(t == m, b == h)
        src, dst = w1.at[0, :, pl.ds(h * L, L)], w2.at[p]
        c = raw(src, dst, k5 + h, k5 + p, (P.base + h, m))
        l = pltpu.make_async_copy(src, dst, recv.at[k5 + p])
        pl.when(jnp.logical_not(mine))(c.start); pl.when(mine)(l.start)
        guarded.append((jnp.logical_not(mine), c))
    for dev in peers: pltpu.make_async_copy(sl.at[0], sa.at[dev[0] % 8], recv.at[k6 + dev[0] % 8]).wait()
    tot = sa[0]
    for k in range(1, 8): tot = tot + sa[k]
    sb[t] = tot
    hop2 = [raw(sb.at[t], sb.at[t], k7 + r, k7 + t, P.zed(r)) for r in (1, 2, 3)]
    for c in hop2: c.start()
    final_add()
    for s in sh: s.a()
    s3(0)
    for h in range(2): pltpu.make_async_copy(w2.at[h], w2.at[h], recv.at[k5 + h]).wait()
    f_w[...] = (f32(w2[0]) + f32(w2[1])).astype(BF)
    shw.a()
    for r in (1, 2, 3): pltpu.make_async_copy(sb.at[(t + r) % 4], sb.at[(t + r) % 4], recv.at[k7 + (t + r) % 4]).wait()
    sc[me] = sb[0] + sb[1] + sb[2] + sb[3]
    hop3 = [raw(sc.at[me], sc.at[me], k8 + j, k8 + me, dev) for j, dev in enumerate(peers)]
    for c in hop3: c.start()
    @pl.when(P.home)
    def _(): fin[b] = land2[t]
    @pl.when(jnp.logical_not(P.home))
    def _(): pltpu.make_async_copy(fin.at[b], fin.at[b], recv.at[k4 + b]).wait()
    pltpu.make_async_copy(fin.at[1 - b], fin.at[1 - b], recv.at[k4 + 1 - b]).wait()
    g_s[0:H] = f32(fin[0]); g_s[H:n] = f32(fin[1])
    g = g_s[...]
    la[me] = jnp.concatenate([jnp.sum(g * unit, 0, keepdims=True), jnp.sum(g, 0, keepdims=True), jnp.zeros((6, D), F32)], 0)
    late1 = [raw(la.at[me], la.at[me], k9 + j, k9 + me, dev) for j, dev in enumerate(peers)]
    for c in late1: c.start()
    gt_o[...] = gm[...] + ln_back(g, unit, inv, vec[...].reshape(1, -1))
    for s in sh + [shw]: s.b()
    for dev in peers: pltpu.make_async_copy(la.at[me], la.at[dev[0] % 8], recv.at[k9 + dev[0] % 8]).wait()
    tot = la[0]
    for k in range(1, 8): tot = tot + la[k]
    lb[t] = tot
    late2 = [raw(lb.at[t], lb.at[t], ka + r, ka + t, P.zed(r)) for r in (1, 2, 3)]
    for c in late2: c.start()
    for s in sh + [shw]: s.c()
    for dev in peers: pltpu.make_async_copy(sc.at[0], sc.at[dev[0] % 8], recv.at[k8 + dev[0] % 8]).wait()
    small_o[0:8] = sc[...]
    for r in (1, 2, 3): pltpu.make_async_copy(lb.at[(t + r) % 4], lb.at[(t + r) % 4], recv.at[ka + (t + r) % 4]).wait()
    small_o[8] = lb[0] + lb[1] + lb[2] + lb[3]
    for s in sh + [shw]: s.end()
    for c in hop1 + hop2 + hop3 + late1 + late2: c.wait_send()
    for c in started: c.wait_send()
    for cond, c in guarded: pl.when(cond)(c.wait_send)

def second(x, wt, ck, ids, proj, qt, qn, kk, kt, vn, of, ga, tok, gm, s_ow, s_up, s_dn, l_ow, l_up, l_dn, s4, gupb, vec):
    S = jax.ShapeDtypeStruct; V = pltpu.VMEM
    n, D = tok.shape; N = 4 * n; H = n // 2; L = D // 2
    w = wt.shape[0]; lw = w // 3; heads = lw // HD
    a, q, o = s_ow.shape[1] // 4, s_up.shape[1] // 4, w // 4
    any_ = pl.BlockSpec(memory_space=pl.ANY); vm = pl.BlockSpec(memory_space=pltpu.VMEM)
    outs = [(S((n, D), F32), vm), (S((4 * a, D), BF), any_), (S((4 * q, D), BF), any_), (S((4 * q, D), BF), any_), (S((w, D), BF), any_), (S((9, 8, D), F32), vm)]
    sc = [V((4, n, D), BF), V((w, N), F32), V((heads, 128, N), BF), V((heads, N, 128), BF), V((heads, N, 128), BF), V((heads, HD, N), BF),
          V((heads, N, 128), BF), V((heads, 128, N), BF), V((heads, N, 128), BF), V((heads, N, 128), F32), V((w, N), F32), V((w, n), BF),
          V((w, D), F32), V((w, D), BF), V((4, n, D), BF), V((4, H, D), BF), V((4, H, D), BF), V((2, H, D), BF), V((n, D), F32),
          V((128, 256), F32), V((256, 128), F32), V((256, 128), F32),
          V((4, 2, q, L), BF), V((4, 2, q, L), BF), V((4, 2, a, L), BF), V((4, 2, a, L), BF), V((4, 2, q, L), BF), V((4, 2, q, L), BF),
          V((4, a, L), BF), V((4, q, L), BF), V((4, q, L), BF), V((2, a, L), BF), V((2, q, L), BF), V((2, q, L), BF),
          V((2, a, L), BF), V((2, q, L), BF), V((2, q, L), BF),
          V((3, o, D), BF), V((2, o, L), BF), V((o, L), BF), V((8, 8, D), F32), V((8, 8, D), F32), V((4, 8, D), F32), V((8, 8, D), F32), V((8, 8, D), F32), V((4, 8, D), F32),
          pltpu.SemaphoreType.DMA((160,)), pltpu.SemaphoreType.DMA((160,)), pltpu.SemaphoreType.DMA((60,))]
    return pl.pallas_call(second_kernel, out_shape=tuple(z[0] for z in outs),
        in_specs=[any_, vm, vm, vm] + [any_] * 7 + [vm] * 3 + [any_] * 6 + [vm] * 3, out_specs=tuple(z[1] for z in outs), scratch_shapes=sc,
        compiler_params=pltpu.CompilerParams(collective_id=1, has_side_effects=True, vmem_limit_bytes=60 * 2**20), name="attend_back_and_reduce",
    )(x, wt, ck, ids, proj, qt, qn, kk, kt, vn, of, ga, tok, gm, s_ow, s_up, s_dn, l_ow, l_up, l_dn, s4, gupb, vec)
def finish_kernel(ow, up, dn, w, gt, res, sm, ow_f, up_f, dn_f, w_f, gt_f, res_f, v0, v1, v2, v3, v4, v5, vub, vck):
    ow_f[...] = ow[...].astype(F32)
    up_f[...] = up[...].astype(F32)
    dn_f[...] = dn[...].astype(F32)
    w_f[...] = w[...].astype(F32)
    gt_f[...] = gt[...]
    res_f[...] = res[...]
    @pl.when(pl.program_id(0) == 0)
    def _():
        t = lax.axis_index("tensor")
        def row(k): return sm[k // 6, pl.ds(k % 6, 1), :]
        for k, o in enumerate((v0, v1, v2, v3)): o[...] = row(k).reshape(-1)
        v4[...] = sm[8, 0:1, :].reshape(-1)
        v5[...] = sm[8, 1:2, :].reshape(-1)
        vub[...] = row(6 + t).reshape(-1)
        for j in range(3):
            for c in range(3): vck[j, c:c + 1, :] = row(10 + 9 * t + 3 * j + c)[:, 0:vck.shape[2]]

def finish(ow, up, dn, w, gt, res, sm, G=2):
    spec = lambda a: pl.BlockSpec((a.shape[0] // G, a.shape[1]), lambda g: (g, 0))
    whole = lambda s: pl.BlockSpec(s, lambda g: (0,) * len(s))
    S = jax.ShapeDtypeStruct
    arrays = (ow, up, dn, w, gt, res)
    kinds = (F32, F32, F32, F32, F32, BF)
    D = ow.shape[1]; lw = ow.shape[0]
    small = [(D,)] * 6 + [(up.shape[0],), (3, 3, lw)]
    return pl.pallas_call(finish_kernel, grid=(G,),
        out_shape=tuple(S(a.shape, k) for a, k in zip(arrays, kinds)) + tuple(S(s, F32) for s in small),
        in_specs=[spec(a) for a in arrays] + [whole(sm.shape)], out_specs=tuple(spec(a) for a in arrays) + tuple(whole(s) for s in small),
        name="finish", cost_estimate=pl.CostEstimate(flops=4 * 10**6, bytes_accessed=15 * 10**6, transcendentals=0),
    )(*arrays, sm)


def per_device(planes, tokens, segment_ids, cotangent, norm1_gain, norm1_shift, qkv_weight, conv_kernel, out_weight, out_bias, norm2_gain, norm2_shift, up_weight, up_bias, down_weight, down_bias):
    n, D = tokens.shape
    lw = qkv_weight.shape[2]
    row = lambda v: v.reshape(1, -1)
    wt = jnp.transpose(qkv_weight, (1, 2, 0)).reshape(3 * lw, D)
    x, ids, wtp, ckp, proj, qt, qn, kk, kt, vn, of, res, gm, ga, s_ow, s_up, s_dn, l_ow, l_up, l_dn, s4, gupb = first(
        tokens, row(segment_ids), cotangent, wt, conv_kernel, out_weight, up_weight, down_weight,
        norm1_gain, norm1_shift, out_bias, norm2_gain, norm2_shift, down_bias, up_bias)
    gt, ow_o, up_o, dn_o, w_o, sm = second(x, wtp, ckp, ids, proj, qt, qn, kk, kt, vn, of, ga, tokens, gm, s_ow, s_up, s_dn, l_ow, l_up, l_dn, s4, gupb, norm1_gain)
    ow_o, up_o, dn_o, w_o, gt, res, g_ob, g_n2, g_s2, g_db, g_n1, g_s1, gub, gck = finish(ow_o, up_o, dn_o, w_o, gt, res, sm)
    sums = (w_o, ow_o, up_o, dn_o, g_ob, g_n2, g_s2, g_db, g_n1, g_s1, gub, gck)
    if planes is not None:
        sums = lax.psum(sums, "dp", axis_index_groups=planes)
    w_o, ow_o, up_o, dn_o, g_ob, g_n2, g_s2, g_db, g_n1, g_s1, gub, gck = sums
    gqkv = jnp.transpose(w_o.reshape(3, lw, D), (2, 0, 1))
    return (res, gt, g_n1, g_s1, gqkv, gck, ow_o, g_ob, g_n2, g_s2, up_o, gub, dn_o, g_db)


def solution(mesh):
    dp = mesh.shape["dp"]
    planes = None
    if dp > 8:
        planes = [[8 * k + j for k in range(dp // 8)] for j in range(8)]
    rows_, rep = P_(("dp", "tensor"), None), P_()
    third, cols, first = P_(None, None, "tensor"), P_(None, "tensor"), P_("tensor", None)
    return jax.shard_map(
        functools.partial(per_device, planes),
        mesh=mesh,
        in_specs=(rows_, P_(("dp", "tensor")), rows_, rep, rep, third, third, first, rep, rep, rep, cols, P_("tensor"), first, rep),
        out_specs=(rows_, rows_, rep, rep, third, third, first, rep, rep, rep, cols, P_("tensor"), first, rep),
        check_vma=False,
    )
```

```python
import functools
import jax, jax.numpy as jnp
from jax import lax
from jax.experimental import pallas as pl
from jax.experimental.pallas import tpu as pltpu
from jax.sharding import PartitionSpec as P_

HD=64
BF=jnp.bfloat16; F32=jnp.float32
BIG=1e30
def nt(a,b): return lax.dot_general(a,b,(((1,),(1,)),((),())),preferred_element_type=F32)
def tn(a,b): return lax.dot_general(a,b,(((0,),(0,)),((),())),preferred_element_type=F32)
def nn(a,b): return jnp.dot(a,b,preferred_element_type=F32)

def keep_rows(ids):
    n=ids.shape[1]
    pos=lax.broadcasted_iota(jnp.int32,(1,n),1)
    out=[]
    for j in (1,2):
        prev=pltpu.roll(ids,j,1)
        out.append(jnp.where((prev==ids)&(pos>=j),1.0,0.0).astype(F32))
    return out

def feats(ids,rows,kind):
    n=ids.shape[1]
    r=lax.broadcasted_iota(jnp.int32,(rows,n),0)
    idb=jnp.broadcast_to(ids,(rows,n))
    if kind=="q":
        return jnp.where((r<4)&(idb!=r),-BIG,0.0).astype(F32)
    return jnp.where(((r<4)&(idb==r))|((r>=4)&(r<7)),1.0,0.0).astype(F32)

def split3(x):
    hi=x.astype(BF).astype(F32); r=x-hi; mid=r.astype(BF).astype(F32); lo=r-mid
    return hi,mid,lo

EPS=1e-5
def ln(x):
    mu=jnp.mean(x,-1,keepdims=True)
    c=x-mu
    inv=lax.rsqrt(jnp.mean(c*c,-1,keepdims=True)+EPS)
    return c*inv,inv
def ln_back(g,unit,inv,gain):
    s=g*gain
    return (s-jnp.mean(s,-1,keepdims=True)-unit*jnp.mean(s*unit,-1,keepdims=True))*inv
MESH=pl.DeviceIdType.MESH

class Place:
    def __init__(self):
        d=lax.axis_index("dp"); t=lax.axis_index("tensor")
        self.d,self.t=d,t
        b=d%2; p=t//2; q=t%2; base=d-b
        self.b,self.p,self.q,self.base=b,p,q,base
        self.same=1-(b+p)%2
        self.home=self.same==1
        self.near=(p+q)%2==1
        self.member=2*q+b
        self.quarter=(d//2)%4
        self.sib=(base+1-b,t)
        self.opp=(d,2*p+1-q)
        self.cross=(base+1-b,2*p+1-q)
        self.other=(d,2*(1-p)+q)
        self.dest=(base+q,2*b+p)
        self.source=(base+p,2*q+b)
        self.fixed=jnp.logical_and(b==p,b==q)
        dx=d+2-4*((d//2)%2); dy=d+4-8*((d//4)%2)
        self.x=(dx,t); self.y=(dy,t); self.xy=(dx+dy-d,t)
    def zed(self,r): return (self.d,(self.t+r)%4)
    def column(self):
        base=self.d-self.b
        out=[]
        for r in range(1,4):
            out.append((self.d,(self.t+r)%4))
        for r in range(4):
            out.append((base+1-self.b,(self.t+r)%4))
        return out

def meet(peers):
    bar=pltpu.get_barrier_semaphore()
    for dev in peers:
        pl.semaphore_signal(bar,inc=1,device_id=dev,device_id_type=MESH)
    pl.semaphore_wait(bar,len(peers))

class Net:
    def __init__(self,send,recv):
        self.send,self.recv,self.k=send,recv,0
    def to(self,src,dst,dev):
        k=self.k; self.k+=1
        return pltpu.make_async_remote_copy(src_ref=src,dst_ref=dst,send_sem=self.send.at[k],recv_sem=self.recv.at[k],device_id=dev,device_id_type=MESH)

class Swap:
    def __init__(self,net,src,dst,dev,fixed):
        self.r=net.to(src,dst,dev); self.fixed=fixed
        self.l=pltpu.make_async_copy(src,dst,net.recv.at[net.k-1])
    def start(self):
        pl.when(jnp.logical_not(self.fixed))(self.r.start)
        pl.when(self.fixed)(self.l.start)
    def wait_recv(self): self.l.wait()
    def wait_send(self): pl.when(jnp.logical_not(self.fixed))(self.r.wait_send)

def rows(ref,start,size): return ref.at[pl.ds(start,size)]

def lanes(start,size): return pl.ds(pl.multiple_of(start,128),size)
def rws(start,size): return pl.ds(pl.multiple_of(start,16),size)


class ToHeads:
    def __init__(self,net,P,src,dst):
        self.k=net.k; net.k+=4
        self.P,self.net,self.dst=P,net,dst
        self.far=[]
        for mm in range(4):
            c=pltpu.make_async_remote_copy(src_ref=src(mm),dst_ref=dst.at[P.t],send_sem=net.send.at[self.k+mm],recv_sem=net.recv.at[self.k+P.t],
                                           device_id=(P.base+mm%2,2*P.b+mm//2),device_id_type=MESH)
            l=pltpu.make_async_copy(src(mm),dst.at[P.t],net.recv.at[self.k+P.t])
            self.far.append((jnp.logical_and(P.home,P.member==mm),c,l))
    def start_one(self,k):
        me,c,l=self.far[k]
        pl.when(jnp.logical_not(me))(c.start)
        pl.when(me)(l.start)
    def start(self):
        for k in range(4): self.start_one(k)
    def wait_recv(self):
        for s in range(4):
            pltpu.make_async_copy(self.dst.at[s],self.dst.at[s],self.net.recv.at[self.k+s]).wait()
    def wait_send(self):
        for me,c,l in self.far: pl.when(jnp.logical_not(me))(c.wait_send)

def mix2(v, cks, r, c, keeps):
    out = cks[pl.ds(r, HD), c:c + 1] * v
    for j in (1, 2):
        out = out + cks[pl.ds(r, HD), 3 * j + c:3 * j + c + 1] * (pltpu.roll(v, j, 1) * keeps[j - 1])
    return out

def tap_columns(ckv, tmp, cks):
    lw = ckv.shape[2]
    tmp[...] = jnp.zeros(tmp.shape, F32)
    for j in range(3):
        for c in range(3):
            tmp[3 * j + c:3 * j + c + 1, 0:lw] = ckv[j, c:c + 1, :]
    cks[...] = tmp[...].T

NC = 4
def first_kernel(tok, ids, cot, wt, ck, ow, up, dn, vg1, vs1, vob, vg2, vs2, vdb, vub,
                 x_o, ids_o, wt_o, ck_o, proj_o, qt_o, qn_o, kk_o, kt_o, vn_o, of_o, res_o, gm_o, ga_in, ow_o, up_o, dn_o, l_ow, l_up, l_dn, small_o, gupb_o,
                 xv, xn, cotv, idv, wtv, ckv, tmp, cks, proj, qt, qn, kk, kt, vn, vt, att, attin, of, lse,
                 ow_a, up_a, dn_a, upb_a, sec, act, gh, gsec, gms, gas, c_ow, c_up, c_dn, send, recv, lsem, wsem):
    P = Place()
    net = Net(send, recv)
    n, D = tok.shape
    N = 4 * n
    heads = wt.shape[0] // (3 * HD)
    lw = heads * HD
    R = n // NC; H = R // 2
    m = P.member; t = P.t
    cotl = pltpu.make_async_copy(cot, cotv, lsem.at[15]); cotl.start()
    own = [pltpu.make_async_copy(a, b.at[t], lsem.at[j]) for j, (a, b) in enumerate(((ow, ow_a), (up, up_a), (dn, dn_a)))]
    for c in own: c.start()
    upb_a[t] = vub[...].reshape(1, -1)
    for k in range(NC):
        unit, _ = ln(tok[k * R:(k + 1) * R, :].astype(F32))
        xn[k * R:(k + 1) * R, :] = (unit * vg1[...].reshape(1, -1) + vs1[...].reshape(1, -1)).astype(BF)
    meet(P.column() + [P.x, P.y, P.xy])
    sends = []
    def later(src, dst, dev):
        c = net.to(src, dst, dev); sends.append(c); return c
    def push(src, dst, dev):
        c = later(src, dst, dev); c.start(); return c
    def swap(src, dst, dev):
        c = Swap(net, src, dst, dev, P.fixed); sends.append(c); return c
    Q = wt.shape[0] // 4
    w0 = pl.multiple_of(P.quarter * Q, 16)
    idg = ToHeads(net, P, lambda mm: ids, idv)
    idg.start()
    wq = swap(rows(wt, w0, Q), rows(wtv, w0, Q), P.dest); wq.start()
    ckc = swap(ck, ckv, P.dest); ckc.start()
    def part(ref, tt, k):
        L = ref.shape[2] // 2; r = ref.shape[1] // 4
        return ref.at[tt, pl.ds(pl.multiple_of(k * r, 16), r), pl.ds(pl.multiple_of(P.b * L, 128), L)]
    def part_in(ref):
        L = ref.shape[1] // 2; r = ref.shape[0] // 4
        return ref.at[pl.ds(pl.multiple_of(P.quarter * r, 16), r), pl.ds(pl.multiple_of(P.b * L, 128), L)]
    qx = (P.x[0] // 2) % 4; qy = (P.y[0] // 2) % 4; qd = (P.xy[0] // 2) % 4
    order = [t, t - 1 + 2 * (1 - (t + 3) // 4), 2 + t // 2 - 2 * (t // 3), 3 - 3 * (t // 2)]
    guarded = []
    right = (P.d, (t + 1) % 4); left = (P.d, (t + 3) % 4)
    class Spread:
        def __init__(self, ins, alls, b0):
            self.zr = net.k; net.k += 4 * len(ins)
            self.w = len(ins)
            def z_push(src, tt, j, cond, dev):
                k = net.k; net.k += 1
                c = pltpu.make_async_remote_copy(src_ref=src, dst_ref=part(alls[j], tt, P.quarter), send_sem=send.at[k],
                                                 recv_sem=recv.at[self.zr + self.w * tt + j], device_id=dev, device_id_type=MESH)
                guarded.append((cond, c))
                return lambda: pl.when(cond)(c.start)
            self.first = [z_push(part_in(ins[j]), t, j, cond, dev) for j in range(self.w) for cond, dev in ((t < 3, right), (t > 0, left))]
            self.steps = {}
            for r in (1, 2, 3):
                tt = order[r]
                arrive = []
                for j in range(self.w):
                    z = part(alls[j], tt, P.quarter)
                    wait = pltpu.make_async_copy(z, z, recv.at[self.zr + self.w * tt + j])
                    arrive.append([wait.wait, z_push(z, tt, j, jnp.logical_and(tt < t, t < 3), right),
                                   z_push(z, tt, j, jnp.logical_and(tt > t, t > 0), left)])
                mine = [part(a, tt, P.quarter) for a in alls]
                bx = [part(a, tt, qx) for a in alls]; by = [part(a, tt, qy) for a in alls]; bd = [part(a, tt, qd) for a in alls]
                ax = [later(z, z, P.x) for z in mine]; ay = [later(z, z, P.y) for z in mine]; asib = [later(z, z, P.sib) for z in mine]
                dx = [later(z, z, P.y) for z in bx[:b0]]; dy = [later(z, z, P.x) for z in by[b0:]]
                xs = [later(z, z, P.sib) for z in bx]; ys = [later(z, z, P.sib) for z in by]; ds_ = [later(z, z, P.sib) for z in bd]
                self.steps[r] = (arrive, ax, ay, asib, dx, dy, xs, ys, ds_)
        def start(self):
            for f in self.first: f()
        def a(self, r):
            arrive, ax, ay, asib = self.steps[r][:4]
            for step in arrive:
                for f in step: f()
            for c in ax + ay + asib: c.start()
        def b(self, r):
            _, ax, ay, _, dx, dy, xs, ys, _ = self.steps[r]
            for c in ax: c.wait_recv()
            for c in dx + xs: c.start()
            for c in ay: c.wait_recv()
            for c in dy + ys: c.start()
        def c(self, r):
            _, _, _, _, dx, dy, _, _, ds_ = self.steps[r]
            for c in dx + dy: c.wait_recv()
            for c in ds_: c.start()
        def end(self, r):
            _, _, _, asib, _, _, xs, ys, ds_ = self.steps[r]
            for c in asib + xs + ys + ds_: c.wait_recv()
    so = Spread((ow,), (ow_a,), 1)
    sw = Spread((up, dn), (up_a, dn_a), 1)
    bias = [push(upb_a.at[t], upb_a.at[t], P.zed(r)) for r in (1, 2, 3)]
    opp_shard = 2 * P.p + 1 - P.q
    target = P.same * opp_shard + (1 - P.same) * (1 + P.b)
    far_shards = (2 * (1 - P.p), 2 * (1 - P.p) + 1)
    ka = net.k; kb = ka + 4 * NC; kc = kb + NC; kd = kc + 4 * NC; net.k = kd + 4 * NC
    def raw(src, dst, ks, kr, dev):
        return pltpu.make_async_remote_copy(src_ref=src, dst_ref=dst, send_sem=send.at[ks], recv_sem=recv.at[kr], device_id=dev, device_id_type=MESH)
    sent = []
    def give_piece(k):
        z = pl.ds(k * R, R)
        for h in range(2):
            zh = pl.ds(k * R + h * H, H)
            c = raw(xn.at[zh], xv.at[t, zh], ka + 4 * k + h, ka + 4 * k + t, (P.base + h, target)); c.start(); sent.append(c)
        c = raw(xn.at[z], xv.at[t, z], kb + k, kb + k, P.sib)
        pl.when(P.home)(c.start); guarded.append((P.home, c))
    def relay(k):
        zb = pl.ds(pl.multiple_of(k * R + P.b * H, 16), H)
        for j, s in enumerate((opp_shard,) + far_shards):
            blk = xv.at[s, zb]
            if j == 0:
                pltpu.make_async_copy(blk, blk, recv.at[ka + 4 * k + s]).wait()
            else:
                on = raw(blk, blk, kd + 4 * k + j, kd + 4 * k + s, P.opp)
                @pl.when(P.near)
                def _():
                    pltpu.make_async_copy(blk, blk, recv.at[ka + 4 * k + s]).wait()
                    on.start()
                guarded.append((P.near, on))
                @pl.when(jnp.logical_not(P.near))
                def _():
                    pltpu.make_async_copy(blk, blk, recv.at[kd + 4 * k + s]).wait()
            c = raw(blk, blk, kc + 4 * k + j, kc + 4 * k + s, P.sib); c.start(); sent.append(c)
    so.start()
    give_piece(0); give_piece(1)
    sw.start()
    relay(0)
    give_piece(2)
    wq.wait_recv()
    wf = [push(rows(wtv, w0, Q), rows(wtv, w0, Q), dev) for dev in (P.x, P.y, P.xy)]
    relay(1)
    so.a(1)
    give_piece(3)
    relay(2)
    so.a(2); sw.a(1)
    relay(3)
    so.a(3)
    @pl.when(P.home)
    def _(): xv[t] = xn[...]
    for c in wf: c.wait_recv()
    def project(s):
        proj[:, pl.ds(pl.multiple_of(s * n, 128), n)] = nt(wtv[...], xv[s])
    @pl.when(jnp.logical_not(P.home))
    def _():
        for k in range(NC): pltpu.make_async_copy(xv.at[t, pl.ds(k * R, R)], xv.at[t, pl.ds(k * R, R)], recv.at[kb + k]).wait()
    project(t)
    so.b(1); so.b(2)
    for k in range(NC):
        zo = pl.ds(pl.multiple_of(k * R + (1 - P.b) * H, 16), H)
        pltpu.make_async_copy(xv.at[opp_shard, zo], xv.at[opp_shard, zo], recv.at[kc + 4 * k + opp_shard]).wait()
    project(opp_shard)
    so.b(3); so.c(1); sw.a(2)
    for k in range(NC):
        zo = pl.ds(pl.multiple_of(k * R + (1 - P.b) * H, 16), H)
        for s in far_shards:
            pltpu.make_async_copy(xv.at[s, zo], xv.at[s, zo], recv.at[kc + 4 * k + s]).wait()
    for s in far_shards: project(s)
    so.c(2); so.c(3)
    idg.wait_recv()
    ckc.wait_recv()
    outs = [pltpu.make_async_copy(a, b, lsem.at[4 + k]) for k, (a, b) in enumerate(
        ((xv, x_o), (wtv, wt_o), (proj, proj_o), (ckv, ck_o)))]
    for c in outs: c.start()
    idrow = jnp.concatenate([idv[s] for s in range(4)], axis=1)
    idv_out = pltpu.make_async_copy(idv, ids_o, lsem.at[9]); idv_out.start()
    keeps = keep_rows(idrow)
    tap_columns(ckv, tmp, cks)
    fq = feats(idrow, 64, "q").astype(BF); fk = feats(idrow, 64, "k")
    qt[64:128, :] = fq
    vt[64:80, :] = jnp.ones((16, N), BF)
    tri = lax.broadcasted_iota(jnp.int32, (n, n), 0) <= lax.broadcasted_iota(jnp.int32, (n, n), 1)
    eb = net.k; net.k += 4 * heads
    def give(h, tt):
        r = pl.ds(pl.multiple_of(h * HD, HD), HD)
        return raw(att.at[tt, r], attin.at[m, r], eb + 4 * h + tt, eb + 4 * h + m, (P.base + P.p, tt))
    def not_me(tt): return jnp.logical_not(jnp.logical_and(P.home, t == tt))
    def not_mine(mm): return jnp.logical_not(jnp.logical_and(P.home, m == mm))
    def at(*fs):
        def run():
            for f, r in fs: f(r)
        return run
    turns = {0: at((sw.b, 1)), 1: at((sw.a, 3)), 2: at((sw.b, 2), (sw.c, 1))}
    def head(h, _):
        for hh, fs in turns.items(): pl.when(h == hh)(fs)
        r = pl.multiple_of(h * HD, HD)
        def part_rows(c): return proj[pl.ds(pl.multiple_of(c * lw + h * HD, HD), HD), :]
        q = mix2(part_rows(0), cks, r, 0, keeps)
        qt[0:64, :] = (q.astype(BF).astype(F32) * 0.125).astype(BF)
        k = mix2(part_rows(1), cks, r, 1, keeps)
        kk[...] = jnp.concatenate([k, fk], 0).T.astype(BF)
        vt[0:64, :] = mix2(part_rows(2), cks, r, 2, keeps).astype(BF)
        for iq in range(4):
            qs = iq * n
            qb = qt[:, qs:qs + n]
            ss = []
            for j in range(iq + 1):
                s = nn(kk[j * n:(j + 1) * n, :], qb)
                if j == iq: s = jnp.where(tri, s, -BIG)
                ss.append(s)
            mx = jnp.max(ss[0], axis=0, keepdims=True)
            for s in ss[1:]: mx = jnp.maximum(mx, jnp.max(s, axis=0, keepdims=True))
            o = jnp.zeros((80, n), F32)
            for j, s in enumerate(ss):
                o = o + nn(vt[:, j * n:(j + 1) * n], jnp.exp(s - mx).astype(BF))
            l = o[64:65, :]
            f = o[0:64, :] / l
            of[pl.ds(r, HD), qs:qs + n] = f
            att[iq, pl.ds(r, HD), :] = f.astype(BF)
            lse[h, :, qs:qs + n] = jnp.broadcast_to(mx + jnp.log(l), (8, n))
        for tt in range(4): pl.when(not_me(tt))(give(h, tt).start)
        return 0
    lax.fori_loop(0, heads, head, 0)
    @pl.when(P.home)
    def _(): attin[m] = att[t]
    ends = [pltpu.make_async_copy(a, b, lsem.at[11 + k]) for k, (a, b) in enumerate(((of, of_o),))]
    for c in ends: c.start()
    sw.c(2); sw.b(3)
    for r in (1, 2, 3): so.end(r)
    for c in own: c.wait()
    for h in range(heads):
        r = pl.ds(h * HD, HD)
        for mm in range(4):
            pl.when(not_mine(mm))(pltpu.make_async_copy(attin.at[mm, r], attin.at[mm, r], recv.at[eb + 4 * h + mm]).wait)
            pl.when(not_me(mm))(give(h, mm).wait_send)
    attT = attin[...].reshape(4 * lw, n)
    gms[...] = tok[...].astype(F32) + tn(attT, ow_a[...].reshape(4 * lw, D)) + vob[...].reshape(1, -1)
    unit, inv = ln(gms[...])
    sec[...] = (unit * vg2[...].reshape(1, -1) + vs2[...].reshape(1, -1)).astype(BF)
    for c in bias: c.wait_recv()
    sw.c(3)
    cotl.wait()
    gsec[...] = jnp.zeros_like(gsec)
    def chain(tt):
        rl = jnp.maximum(nn(sec[...], up_a[tt]) + upb_a[tt], 0.0)
        act[tt] = (rl * rl).astype(BF)
        g = (nt(cotv[...], dn_a[tt]) * (2.0 * rl)).astype(BF)
        gh[tt] = g
        gupb_o[tt] = jnp.sum(g.astype(F32), 0, keepdims=True)
        gsec[...] += nt(g, up_a[tt])
    chain(order[0])
    sw.end(1); chain(order[1])
    sw.end(2); chain(order[2])
    sw.end(3); chain(order[3])
    mid = gms[...]
    unit, inv = ln(mid)
    gs = gsec[...]
    cf = cotv[...].astype(F32)
    gm = cf + ln_back(gs, unit, inv, vg2[...].reshape(1, -1))
    gmb = gm.astype(BF)
    gb = ToHeads(net, P, lambda mm: gas.at[mm], ga_in)
    for mm in range(4):
        gas[mm] = nt(ow_a[mm], gmb).astype(BF)
        gb.start_one(mm)
    gsec[...] = gm
    gmo = pltpu.make_async_copy(gsec, gm_o, lsem.at[14]); gmo.start()
    small_o[0:1] = jnp.sum(gm, 0, keepdims=True)
    small_o[1:2] = jnp.sum(gs * unit, 0, keepdims=True)
    small_o[2:3] = jnp.sum(gs, 0, keepdims=True)
    small_o[3:4] = jnp.sum(cf, 0, keepdims=True)
    small_o[4:8] = jnp.zeros((4, D), F32)
    out = mid + vdb[...].reshape(1, -1)
    for b in range(4): out = out + nn(act[b], dn_a[b])
    res_o[...] = out.astype(BF)
    for c in sends: c.wait_send()
    for cond, c in guarded: pl.when(cond)(c.wait_send)
    L = D // 2
    lo, lx = P.b * L, (1 - P.b) * L
    blocks = [1 - P.q, 3 - P.q, 2 * (1 - P.p) + P.q, t]
    ow_a[...] = nn(attT, gmb).astype(BF).reshape(ow_a.shape)
    trios = ((ow_a, c_ow, ow_o), (dn_a, c_dn, dn_o), (up_a, c_up, up_o))
    halves, fin = [], []
    def grads(k):
        tt = blocks[k]
        dn_a[tt] = tn(act[tt], cotv[...]).astype(BF)
        up_a[tt] = tn(sec[...], gh[tt]).astype(BF)
        cs = []
        for g, cref, _ in trios:
            c = net.to(g.at[tt, :, lanes(lx, L)], cref.at[tt], P.sib); c.start(); cs.append(c)
        halves.append(cs)
    def cores(k):
        tt = blocks[k]
        for j, (g, cref, o) in enumerate(trios):
            halves[k][j].wait_recv()
            cref[tt] = (cref[tt].astype(F32) + g[tt, :, lanes(lo, L)].astype(F32)).astype(BF)
            z = pltpu.make_async_copy(cref.at[tt], o.at[tt], wsem.at[3 * k + j]); z.start(); fin.append(z)
    grads(0); grads(1)
    cores(0)
    ro, ru = ow.shape[0] // 4, up.shape[0] // 4
    pc = []
    def plane(j):
        for src, dst, r_, ks, dev in ((c_ow, l_ow, ro, (qx, qd), P.x), (c_up, l_up, ru, (qx, qd), P.x), (c_dn, l_dn, ru, (qy, qd), P.y)):
            for i, k in enumerate(ks):
                c = net.to(src.at[blocks[j], rws(k * r_, r_)], dst.at[j, i], dev); c.start(); pc.append(c)
    plane(0)
    grads(2); cores(1)
    grads(3)
    r8 = lax.broadcasted_iota(jnp.int32, (64, N), 0)
    zl = jnp.zeros((64, N), F32)
    fqf = feats(idrow, 64, "q")
    pieces = ((qt, qt_o), (qn, qn_o), (kk, kk_o), (kt, kt_o), (vn, vn_o))
    def prepare(h, _):
        r = pl.multiple_of(h * HD, HD)
        def part_rows(c): return proj[pl.ds(pl.multiple_of(c * lw + h * HD, HD), HD), :]
        q = mix2(part_rows(0), cks, r, 0, keeps).astype(BF).astype(F32) * 0.125
        hi, mid_, low = split3(-lse[h, 0:1, :])
        k = mix2(part_rows(1), cks, r, 1, keeps)
        v = mix2(part_rows(2), cks, r, 2, keeps)
        @pl.when(h > 0)
        def _():
            for j, (a, o) in enumerate(pieces): pltpu.make_async_copy(a, o.at[0], wsem.at[12 + j]).wait()
        qt[0:64, :] = q.astype(BF)
        qt[64:128, :] = (fqf + jnp.where(r8 == 4, hi, 0.0) + jnp.where(r8 == 5, mid_, 0.0) + jnp.where(r8 == 6, low, 0.0)).astype(BF)
        qn[...] = jnp.concatenate([zl, q], 0).T.astype(BF)
        kt[...] = k.astype(BF)
        kk[...] = jnp.concatenate([k, fk], 0).T.astype(BF)
        vn[...] = jnp.concatenate([v, jnp.where(r8 < 3, 1.0, 0.0)], 0).T.astype(BF)
        for j, (a, o) in enumerate(pieces): pltpu.make_async_copy(a, o.at[h], wsem.at[12 + j]).start()
        return 0
    lax.fori_loop(0, heads, prepare, 0)
    cores(2); cores(3)
    for j, (a, o) in enumerate(pieces): pltpu.make_async_copy(a, o.at[0], wsem.at[12 + j]).wait()
    for cs in halves:
        for c in cs: c.wait_send()
    for c in sent: c.wait_send()
    idg.wait_send()
    for c in outs + [idv_out, gmo] + ends + fin: c.wait()
    for c in pc: c.wait()
    gb.wait_send()
    gb.wait_recv()

def first(tok, ids, cot, wt, ck, ow, up, dn, *vecs):
    n, D = tok.shape; S = jax.ShapeDtypeStruct; V = pltpu.VMEM
    lw = wt.shape[0] // 3; heads = lw // HD; N = 4 * n; fb = up.shape[1]
    any_ = pl.BlockSpec(memory_space=pl.ANY); vm = pl.BlockSpec(memory_space=pltpu.VMEM)
    outs = [(S((4, n, D), BF), any_), (S((4, 1, n), jnp.int32), any_), (S(wt.shape, BF), any_), (S(ck.shape, F32), any_),
            (S((3 * lw, N), F32), any_), (S((heads, 128, N), BF), any_), (S((heads, N, 128), BF), any_), (S((heads, N, 128), BF), any_),
            (S((heads, HD, N), BF), any_), (S((heads, N, 128), BF), any_), (S((lw, N), F32), any_),
            (S((n, D), BF), vm), (S((n, D), F32), any_), (S((4, lw, n), BF), any_),
            (S((4, lw, D // 2), BF), any_), (S((4, D, fb // 2), BF), any_), (S((4, fb, D // 2), BF), any_),
            (S((2, 2, lw // 4, D // 2), BF), any_), (S((2, 2, D // 4, D // 2), BF), any_), (S((2, 2, fb // 4, D // 2), BF), any_), (S((8, D), F32), vm), (S((4, 1, fb), F32), vm)]
    return pl.pallas_call(first_kernel, out_shape=tuple(o[0] for o in outs),
        in_specs=[vm] + [any_] * 7 + [vm] * 7, out_specs=tuple(o[1] for o in outs),
        scratch_shapes=[V((4, n, D), BF), V((n, D), BF), V((n, D), BF), V((4, 1, n), jnp.int32), V(wt.shape, BF), V(ck.shape, F32), V((128, 256), F32), V((256, 128), F32),
                        V((3 * lw, N), F32), V((128, N), BF), V((N, 128), BF), V((N, 128), BF), V((HD, N), BF), V((N, 128), BF), V((80, N), BF), V((4, lw, n), BF), V((4, lw, n), BF), V((lw, N), F32), V((heads, 8, N), F32),
                        V((4, lw, D), BF), V((4, D, fb), BF), V((4, fb, D), BF), V((4, 1, fb), F32),
                        V((n, D), BF), V((4, n, fb), BF), V((4, n, fb), BF), V((n, D), F32), V((n, D), F32), V((4, lw, n), BF),
                        V((4, lw, D // 2), BF), V((4, D, fb // 2), BF), V((4, fb, D // 2), BF),
                        pltpu.SemaphoreType.DMA((240,)), pltpu.SemaphoreType.DMA((240,)), pltpu.SemaphoreType.DMA((16,)), pltpu.SemaphoreType.DMA((20,))],
        compiler_params=pltpu.CompilerParams(collective_id=0, has_side_effects=True, vmem_limit_bytes=60 * 2**20),
        name="forward_and_feed",
    )(tok, ids, cot, wt, ck, ow, up, dn, *vecs)
def second_kernel(x_h, wt, ck, ids, proj_h, qt_h, qn_h, kk_h, kt_h, vn_h, of_h, ga, tok, gm, s_ow, s_up, s_dn, l_ow, l_up, l_dn, s4, gupb, vec,
                  gt_o, ow_o, up_o, dn_o, w_o, small_o,
                  x, proj, qt, qn, kk, kt, vn, dot, don, dkv, gconv, gp, gw, gwb, gfs, land1, land2, fin, g_s,
                  tmp, cks, cacc, own_x, own_y, own_o, x_ow, x_up, y_dn, z_ow, z_up, z_dn, o_ow, o_up, o_dn, f_ow, f_up, f_dn,
                  w1, w2, f_w, sl, sa, sb, sc, la, lb, send, recv, lsem):
    P = Place()
    plane = []
    for r in (P.x, P.y, P.xy): plane += [r, (r[0] + 1 - 2 * P.b, r[1])]
    net = Net(send, recv)
    n, D = tok.shape; N = 4 * n; H = n // 2; L = D // 2
    heads = wt.shape[0] // (3 * HD); lw = heads * HD
    m, t, b, p = P.member, P.t, P.b, P.p
    f32 = lambda v: v.astype(F32)
    started, guarded = [], []
    def later(src, dst, dev):
        c = net.to(src, dst, dev); started.append(c); return c
    def push(src, dst, dev):
        c = later(src, dst, dev); c.start(); return c
    def raw(src, dst, ks, kr, dev):
        return pltpu.make_async_remote_copy(src_ref=src, dst_ref=dst, send_sem=send.at[ks], recv_sem=recv.at[kr], device_id=dev, device_id_type=MESH)
    qr = P.quarter; qx = (P.x[0] // 2) % 4; qy = (P.y[0] // 2) % 4; qd = (P.xy[0] // 2) % 4
    lo = b * L
    ro, ru = s_ow.shape[1] // 4, s_up.shape[1] // 4
    blocks = [1 - P.q, 3 - P.q, 2 * (1 - p) + P.q, t]
    lc = [0]
    def local(src, dst):
        c = pltpu.make_async_copy(src, dst, lsem.at[lc[0]]); lc[0] += 1; c.start(); return c
    class Block:
        def __init__(self, j):
            tt = blocks[j]
            self.j, self.tt = j, tt
            q_ = lambda ref, k, r_: ref.at[tt, rws(k * r_, r_), :]
            self.p1x, self.p1y = [], []
            if j > 0:
                self.p1x = [later(q_(s_ow, k, ro), x_ow.at[j, i], P.x) for i, k in ((0, qx), (1, qd))] + \
                           [later(q_(s_up, k, ru), x_up.at[j, i], P.x) for i, k in ((0, qx), (1, qd))]
                self.p1y = [later(q_(s_dn, k, ru), y_dn.at[j, i], P.y) for i, k in ((0, qy), (1, qd))]
            self.p3 = [later(x_ow.at[j, 1], z_ow.at[j], P.y), later(x_up.at[j, 1], z_up.at[j], P.y), later(y_dn.at[j, 1], z_dn.at[j], P.x)]
        def load(self):
            tt, j = self.tt, self.j
            q_ = lambda ref, k, r_: ref.at[tt, rws(k * r_, r_), :]
            self.loads = [local(q_(s_ow, k, ro), own_o.at[j, i]) for i, k in ((0, qr), (1, qy))] + \
                         [local(q_(s_up, k, ru), own_x.at[j, i]) for i, k in ((0, qr), (1, qy))] + \
                         [local(q_(s_dn, k, ru), own_y.at[j, i]) for i, k in ((0, qr), (1, qx))]
            if j < 1:
                self.loads += [local(a.at[j], z.at[j]) for a, z in ((l_ow, x_ow), (l_up, x_up), (l_dn, y_dn))]
        def a(self):
            if self.j > 0:
                for c in self.p1x + self.p1y: c.start()
        def b(self):
            j = self.j
            for c in self.loads: c.wait()
            for c in self.p1x + self.p1y: c.wait_recv()
            for z, o in ((x_ow, own_o), (x_up, own_x), (y_dn, own_y)):
                z[j] = (f32(z[j]) + f32(o[j])).astype(BF)
            for c in self.p3: c.start()
        def c(self):
            j = self.j
            for c in self.p3: c.wait_recv()
            for z, o in ((z_ow, x_ow), (z_up, x_up), (z_dn, y_dn)):
                z[j] = (f32(z[j]) + f32(o[j, 0])).astype(BF)
    B = [Block(j) for j in range(4)]
    zs = ((z_ow, o_ow, f_ow), (z_up, o_up, f_up), (z_dn, o_dn, f_dn))
    zz = [[later(z.at[j], o.at[j], P.opp) for j in (0, 1)] for z, o, f in zs]
    z2 = [later(z.at[2], f.at[0], P.other) for z, o, f in zs]
    def opp_send(j):
        for cc in zz: cc[j].start()
    def opp_add():
        for (z, o, f), cc in zip(zs, zz):
            for c in cc: c.wait_recv()
            z[2] = (f32(z[2]) + f32(o[1 - p])).astype(BF)
        for c in z2: c.start()
    outs = ((ow_o, f_ow, ro), (up_o, f_up, ru), (dn_o, f_dn, ru))
    def place(o, k, r_): return o.at[rws(k * r_, r_), lanes(lo, L)]
    class Share:
        def __init__(self, o, src, r_, by_x):
            self.own = (src, place(o, qr, r_))
            self.sx = later(src, place(o, qr, r_), P.x); self.sy = later(src, place(o, qr, r_), P.y); self.ss = later(src, place(o, qr, r_), P.sib)
            px, py, pd = place(o, qx, r_), place(o, qy, r_), place(o, qd, r_)
            self.dg = later(px, px, P.y) if by_x else later(py, py, P.x)
            self.by_x = by_x
            self.fx, self.fy, self.fd = later(px, px, P.sib), later(py, py, P.sib), later(pd, pd, P.sib)
        def a(self):
            for c in (self.sx, self.sy, self.ss): c.start()
            self.l = local(*self.own)
        def b(self):
            self.sx.wait_recv()
            if self.by_x: self.dg.start()
            self.fx.start()
            self.sy.wait_recv()
            if not self.by_x: self.dg.start()
            self.fy.start()
        def c(self):
            self.dg.wait_recv(); self.fd.start()
        def end(self):
            for c in (self.ss, self.fx, self.fy, self.fd): c.wait_recv()
            self.l.wait()
    sh = [Share(o, f.at[1], r_, bx) for (o, f, r_), bx in zip(outs, (True, True, False))]
    shw = Share(w_o, f_w, wt.shape[0] // 4, False)
    def final_add():
        for (z, o, f), c in zip(zs, z2):
            c.wait_recv()
            f[1] = (f32(f[0]) + f32(z[3]) + f32(o[p])).astype(BF)
    ldo = local(of_h, gconv.at[pl.ds(0, lw)])
    for j in range(4): B[j].load()
    lda = [local(a, z) for a, z in ((qt_h, qt), (kk_h, kk), (vn_h, vn), (qn_h, qn), (kt_h, kt))]
    ldp = local(proj_h, proj)
    ldx = local(x_h, x)
    meet(P.column() + plane)
    B[1].a()
    B[0].b()
    B[2].a()
    idrow = jnp.concatenate([ids[s] for s in range(4)], axis=1)
    keeps = keep_rows(idrow)
    tap_columns(ck, tmp, cks)
    cacc[...] = jnp.zeros(cacc.shape, F32)
    r8 = lax.broadcasted_iota(jnp.int32, (64, N), 0)
    zl = jnp.zeros((64, N), F32)
    ldo.wait()
    def setup(h, _):
        r = pl.multiple_of(h * HD, HD)
        do = f32(jnp.concatenate([ga[s, pl.ds(r, HD), :] for s in range(4)], axis=1))
        inner = jnp.sum(do * gconv[pl.ds(r, HD), :], axis=0, keepdims=True)
        hi, mid, low = split3(-inner)
        f = jnp.where(r8 == 0, hi, 0.0) + jnp.where(r8 == 1, mid, 0.0) + jnp.where(r8 == 2, low, 0.0)
        dot[h, 0:64, :] = do.astype(BF); dot[h, 64:128, :] = f.astype(BF)
        don[h] = jnp.concatenate([do, zl], 0).T.astype(BF)
        return 0
    lax.fori_loop(0, heads, setup, 0)
    for c in lda: c.wait()
    tri = lax.broadcasted_iota(jnp.int32, (n, n), 0) <= lax.broadcasted_iota(jnp.int32, (n, n), 1)
    opp_shard = 2 * p + 1 - P.q
    h0 = pl.multiple_of(b * H, 16); h1 = pl.multiple_of((1 - b) * H, 16)
    e1 = [later(gfs.at[s, pl.ds(h1, H)], land1.at[s], P.sib) for s in range(4)]
    k2 = net.k; k3 = k2 + 4; k4 = k3 + 4; net.k = k4 + 2
    def far_side(s): return s // 2 != p
    def to_opp(s):
        cond = jnp.logical_or(opp_shard == s, jnp.logical_and(far_side(s), jnp.logical_not(P.near)))
        return cond, raw(land1.at[s], land2.at[s], k2 + s, k2 + s, P.opp)
    def summing(s): return jnp.logical_or(t == s, jnp.logical_and(far_side(s), P.near))
    def to_owner(s):
        cond = jnp.logical_and(summing(s), jnp.logical_not(jnp.logical_and(P.home, t == s)))
        return cond, raw(land2.at[s], fin.at[b], k3 + s, k4 + b, (P.base + p, s))
    opps = [to_opp(s) for s in range(4)]; owners = [to_owner(s) for s in range(4)]
    guarded += opps + owners
    def s1(s): e1[s].start()
    def s2(s):
        e1[s].wait_recv()
        land1[s] = (f32(land1[s]) + f32(gfs[s, pl.ds(h0, H)])).astype(BF)
        cond, c = opps[s]; pl.when(cond)(c.start)
    def s3(s):
        @pl.when(summing(s))
        def _():
            pltpu.make_async_copy(land2.at[s], land2.at[s], recv.at[k2 + s]).wait()
            land2[s] = (f32(land2[s]) + f32(land1[s])).astype(BF)
        cond, c = owners[s]; pl.when(cond)(c.start)
    def rows_of(i, points):
        qs = i * n
        def head(h, _):
            for hh, f in points.items(): pl.when(h == hh)(f)
            dq = jnp.zeros((64, n), F32)
            for j in range(i + 1):
                js = j * n
                st = nn(kk[h, js:js + n, :], qt[h, :, qs:qs + n])
                pr = jnp.exp(st)
                if i == j: pr = jnp.where(tri, pr, 0.0)
                dp = nn(vn[h, js:js + n, :], dot[h, :, qs:qs + n])
                ds = (pr * dp).astype(BF)
                add = nn(pr.astype(BF), don[h, qs:qs + n, :]) + nn(ds, qn[h, qs:qs + n, :])
                if i == 3: dkv[h, js:js + n, :] = add
                else: dkv[h, js:js + n, :] += add
                dq = dq + nn(kt[h, :, js:js + n], ds)
            gconv[pl.ds(pl.multiple_of(h * HD, HD), HD), qs:qs + n] = dq * 0.125
            if i == 3: pl.when(h == 0)(ldp.wait)
            tt = dkv[h, qs:qs + n, :].T
            gconv[pl.ds(pl.multiple_of(2 * lw + h * HD, HD), HD), qs:qs + n] = tt[0:64]
            gconv[pl.ds(pl.multiple_of(lw + h * HD, HD), HD), qs:qs + n] = tt[64:128]
            for c in range(3):
                r = pl.ds(pl.multiple_of(c * lw + h * HD, HD), HD); rk = pl.ds(pl.multiple_of(h * HD, HD), HD)
                g = gconv[r, qs:qs + n]
                nxt = jnp.zeros((HD, 128), F32) if i == 3 else gconv[r, qs + n:qs + n + 128]
                gx = jnp.concatenate([g, nxt], 1)
                pc = proj[r, qs:qs + n]
                prv = jnp.zeros((HD, 128), F32) if i == 0 else proj[r, qs - 128:qs]
                px = jnp.concatenate([prv, pc], 1)
                o = cks[rk, c:c + 1] * g
                cacc[rk, c:c + 1] += jnp.sum(g * pc, axis=1, keepdims=True)
                for jj in (1, 2):
                    kr = keeps[jj - 1][:, qs:qs + n]
                    kn = jnp.zeros((1, 128), F32) if i == 3 else keeps[jj - 1][:, qs + n:qs + n + 128]
                    kg = gx * jnp.concatenate([kr, kn], 1)
                    cacc[rk, 3 * jj + c:3 * jj + c + 1] += jnp.sum(kg[:, 0:n] * pltpu.roll(px, jj, 1)[:, 128:], axis=1, keepdims=True)
                    o = o + cks[rk, 3 * jj + c:3 * jj + c + 1] * pltpu.roll(kg, n + 128 - jj, 1)[:, 0:n]
                gp[r, :] = o.astype(BF)
            return 0
        lax.fori_loop(0, heads, head, 0)
        gfs[i] = tn(gp[...], wt[...]).astype(BF)
        s1(i)
        if i == 3: ldx.wait()
        g = nn(gp[...], x[i])
        if i == 3: gw[...] = g
        else: gw[...] += g
    def at(*fs):
        def run():
            for f in fs: f()
        return run
    rows_of(3, {1: at(B[1].b, B[3].a), 2: at(B[0].c, lambda: opp_send(0))})
    rows_of(2, {0: at(B[1].c, lambda: opp_send(1)), 1: at(lambda: s2(3), B[2].b)})
    rows_of(1, {0: at(lambda: s3(3), B[2].c, B[3].b), 1: at(lambda: s2(2))})
    rows_of(0, {0: at(lambda: s2(1), opp_add, B[3].c), 1: at(lambda: s3(2))})
    Q = wt.shape[0] // 4
    gwb[...] = gw[...].astype(BF)
    wx = [push(gwb.at[rws(k * Q, Q)], w1.at[j], dev) for j, (k, dev) in enumerate(((qx, P.x), (qy, P.y), (qd, P.xy)))]
    me = P.d % 8
    peers = plane + [P.sib]
    sl[...] = jnp.zeros(sl.shape, F32)
    def put(row, v): sl[row // 6, pl.ds(row % 6, 1), 0:v.shape[1]] = v
    for k in range(4): put(k, s4[k:k + 1])
    for k in range(4): put(6 + k, gupb[k])
    ct = cacc[...].T
    for k in range(9): put(10 + 9 * m + k, ct[k:k + 1, 0:lw])
    k6 = net.k; k7 = k6 + 8; k8 = k7 + 4; k9 = k8 + 8; ka = k9 + 8; k5 = ka + 4; net.k = k5 + 2
    hop1 = [raw(sl.at[dev[0] % 8], sa.at[me], k6 + j, k6 + me, dev) for j, dev in enumerate(peers)]
    for c in hop1: c.start()
    sa[me] = sl[me]
    s2(0); s3(1)
    unit, inv = ln(f32(tok[...]))
    for c in wx: c.wait_recv()
    w1[0] = (f32(w1[0]) + f32(w1[1]) + f32(w1[2]) + f32(gwb[rws(qr * Q, Q)])).astype(BF)
    for h in range(2):
        mine = jnp.logical_and(t == m, b == h)
        src, dst = w1.at[0, :, pl.ds(h * L, L)], w2.at[p]
        c = raw(src, dst, k5 + h, k5 + p, (P.base + h, m))
        l = pltpu.make_async_copy(src, dst, recv.at[k5 + p])
        pl.when(jnp.logical_not(mine))(c.start); pl.when(mine)(l.start)
        guarded.append((jnp.logical_not(mine), c))
    for dev in peers: pltpu.make_async_copy(sl.at[0], sa.at[dev[0] % 8], recv.at[k6 + dev[0] % 8]).wait()
    tot = sa[0]
    for k in range(1, 8): tot = tot + sa[k]
    sb[t] = tot
    hop2 = [raw(sb.at[t], sb.at[t], k7 + r, k7 + t, P.zed(r)) for r in (1, 2, 3)]
    for c in hop2: c.start()
    final_add()
    for s in sh: s.a()
    s3(0)
    for h in range(2): pltpu.make_async_copy(w2.at[h], w2.at[h], recv.at[k5 + h]).wait()
    f_w[...] = (f32(w2[0]) + f32(w2[1])).astype(BF)
    shw.a()
    for r in (1, 2, 3): pltpu.make_async_copy(sb.at[(t + r) % 4], sb.at[(t + r) % 4], recv.at[k7 + (t + r) % 4]).wait()
    sc[me] = sb[0] + sb[1] + sb[2] + sb[3]
    hop3 = [raw(sc.at[me], sc.at[me], k8 + j, k8 + me, dev) for j, dev in enumerate(peers)]
    for c in hop3: c.start()
    @pl.when(P.home)
    def _(): fin[b] = land2[t]
    @pl.when(jnp.logical_not(P.home))
    def _(): pltpu.make_async_copy(fin.at[b], fin.at[b], recv.at[k4 + b]).wait()
    pltpu.make_async_copy(fin.at[1 - b], fin.at[1 - b], recv.at[k4 + 1 - b]).wait()
    g_s[0:H] = f32(fin[0]); g_s[H:n] = f32(fin[1])
    g = g_s[...]
    la[me] = jnp.concatenate([jnp.sum(g * unit, 0, keepdims=True), jnp.sum(g, 0, keepdims=True), jnp.zeros((6, D), F32)], 0)
    late1 = [raw(la.at[me], la.at[me], k9 + j, k9 + me, dev) for j, dev in enumerate(peers)]
    for c in late1: c.start()
    gt_o[...] = gm[...] + ln_back(g, unit, inv, vec[...].reshape(1, -1))
    for s in sh + [shw]: s.b()
    for dev in peers: pltpu.make_async_copy(la.at[me], la.at[dev[0] % 8], recv.at[k9 + dev[0] % 8]).wait()
    tot = la[0]
    for k in range(1, 8): tot = tot + la[k]
    lb[t] = tot
    late2 = [raw(lb.at[t], lb.at[t], ka + r, ka + t, P.zed(r)) for r in (1, 2, 3)]
    for c in late2: c.start()
    for s in sh + [shw]: s.c()
    for dev in peers: pltpu.make_async_copy(sc.at[0], sc.at[dev[0] % 8], recv.at[k8 + dev[0] % 8]).wait()
    small_o[0:8] = sc[...]
    for r in (1, 2, 3): pltpu.make_async_copy(lb.at[(t + r) % 4], lb.at[(t + r) % 4], recv.at[ka + (t + r) % 4]).wait()
    small_o[8] = lb[0] + lb[1] + lb[2] + lb[3]
    for s in sh + [shw]: s.end()
    for c in hop1 + hop2 + hop3 + late1 + late2: c.wait_send()
    for c in started: c.wait_send()
    for cond, c in guarded: pl.when(cond)(c.wait_send)

def second(x, wt, ck, ids, proj, qt, qn, kk, kt, vn, of, ga, tok, gm, s_ow, s_up, s_dn, l_ow, l_up, l_dn, s4, gupb, vec):
    S = jax.ShapeDtypeStruct; V = pltpu.VMEM
    n, D = tok.shape; N = 4 * n; H = n // 2; L = D // 2
    w = wt.shape[0]; lw = w // 3; heads = lw // HD
    a, q, o = s_ow.shape[1] // 4, s_up.shape[1] // 4, w // 4
    any_ = pl.BlockSpec(memory_space=pl.ANY); vm = pl.BlockSpec(memory_space=pltpu.VMEM)
    outs = [(S((n, D), F32), vm), (S((4 * a, D), BF), any_), (S((4 * q, D), BF), any_), (S((4 * q, D), BF), any_), (S((w, D), BF), any_), (S((9, 8, D), F32), vm)]
    sc = [V((4, n, D), BF), V((w, N), F32), V((heads, 128, N), BF), V((heads, N, 128), BF), V((heads, N, 128), BF), V((heads, HD, N), BF),
          V((heads, N, 128), BF), V((heads, 128, N), BF), V((heads, N, 128), BF), V((heads, N, 128), F32), V((w, N), F32), V((w, n), BF),
          V((w, D), F32), V((w, D), BF), V((4, n, D), BF), V((4, H, D), BF), V((4, H, D), BF), V((2, H, D), BF), V((n, D), F32),
          V((128, 256), F32), V((256, 128), F32), V((256, 128), F32),
          V((4, 2, q, L), BF), V((4, 2, q, L), BF), V((4, 2, a, L), BF), V((4, 2, a, L), BF), V((4, 2, q, L), BF), V((4, 2, q, L), BF),
          V((4, a, L), BF), V((4, q, L), BF), V((4, q, L), BF), V((2, a, L), BF), V((2, q, L), BF), V((2, q, L), BF),
          V((2, a, L), BF), V((2, q, L), BF), V((2, q, L), BF),
          V((3, o, D), BF), V((2, o, L), BF), V((o, L), BF), V((8, 8, D), F32), V((8, 8, D), F32), V((4, 8, D), F32), V((8, 8, D), F32), V((8, 8, D), F32), V((4, 8, D), F32),
          pltpu.SemaphoreType.DMA((160,)), pltpu.SemaphoreType.DMA((160,)), pltpu.SemaphoreType.DMA((60,))]
    return pl.pallas_call(second_kernel, out_shape=tuple(z[0] for z in outs),
        in_specs=[any_, vm, vm, vm] + [any_] * 7 + [vm] * 3 + [any_] * 6 + [vm] * 3, out_specs=tuple(z[1] for z in outs), scratch_shapes=sc,
        compiler_params=pltpu.CompilerParams(collective_id=1, has_side_effects=True, vmem_limit_bytes=60 * 2**20), name="attend_back_and_reduce",
    )(x, wt, ck, ids, proj, qt, qn, kk, kt, vn, of, ga, tok, gm, s_ow, s_up, s_dn, l_ow, l_up, l_dn, s4, gupb, vec)
def finish_kernel(ow, up, dn, w, gt, res, sm, ow_f, up_f, dn_f, w_f, gt_f, res_f, v0, v1, v2, v3, v4, v5, vub, vck):
    ow_f[...] = ow[...].astype(F32)
    up_f[...] = up[...].astype(F32)
    dn_f[...] = dn[...].astype(F32)
    w_f[...] = w[...].astype(F32)
    gt_f[...] = gt[...]
    res_f[...] = res[...]
    @pl.when(pl.program_id(0) == 0)
    def _():
        t = lax.axis_index("tensor")
        def row(k): return sm[k // 6, pl.ds(k % 6, 1), :]
        for k, o in enumerate((v0, v1, v2, v3)): o[...] = row(k).reshape(-1)
        v4[...] = sm[8, 0:1, :].reshape(-1)
        v5[...] = sm[8, 1:2, :].reshape(-1)
        vub[...] = row(6 + t).reshape(-1)
        for j in range(3):
            for c in range(3): vck[j, c:c + 1, :] = row(10 + 9 * t + 3 * j + c)[:, 0:vck.shape[2]]

def finish(ow, up, dn, w, gt, res, sm, G=2):
    spec = lambda a: pl.BlockSpec((a.shape[0] // G, a.shape[1]), lambda g: (g, 0))
    whole = lambda s: pl.BlockSpec(s, lambda g: (0,) * len(s))
    S = jax.ShapeDtypeStruct
    arrays = (ow, up, dn, w, gt, res)
    kinds = (F32, F32, F32, F32, F32, BF)
    D = ow.shape[1]; lw = ow.shape[0]
    small = [(D,)] * 6 + [(up.shape[0],), (3, 3, lw)]
    return pl.pallas_call(finish_kernel, grid=(G,),
        out_shape=tuple(S(a.shape, k) for a, k in zip(arrays, kinds)) + tuple(S(s, F32) for s in small),
        in_specs=[spec(a) for a in arrays] + [whole(sm.shape)], out_specs=tuple(spec(a) for a in arrays) + tuple(whole(s) for s in small),
        name="finish", cost_estimate=pl.CostEstimate(flops=4 * 10**6, bytes_accessed=15 * 10**6, transcendentals=0),
    )(*arrays, sm)


def per_device(planes, tokens, segment_ids, cotangent, norm1_gain, norm1_shift, qkv_weight, conv_kernel, out_weight, out_bias, norm2_gain, norm2_shift, up_weight, up_bias, down_weight, down_bias):
    n, D = tokens.shape
    lw = qkv_weight.shape[2]
    row = lambda v: v.reshape(1, -1)
    wt = jnp.transpose(qkv_weight, (1, 2, 0)).reshape(3 * lw, D)
    x, ids, wtp, ckp, proj, qt, qn, kk, kt, vn, of, res, gm, ga, s_ow, s_up, s_dn, l_ow, l_up, l_dn, s4, gupb = first(
        tokens, row(segment_ids), cotangent, wt, conv_kernel, out_weight, up_weight, down_weight,
        norm1_gain, norm1_shift, out_bias, norm2_gain, norm2_shift, down_bias, up_bias)
    gt, ow_o, up_o, dn_o, w_o, sm = second(x, wtp, ckp, ids, proj, qt, qn, kk, kt, vn, of, ga, tokens, gm, s_ow, s_up, s_dn, l_ow, l_up, l_dn, s4, gupb, norm1_gain)
    ow_o, up_o, dn_o, w_o, gt, res, g_ob, g_n2, g_s2, g_db, g_n1, g_s1, gub, gck = finish(ow_o, up_o, dn_o, w_o, gt, res, sm)
    sums = (w_o, ow_o, up_o, dn_o, g_ob, g_n2, g_s2, g_db, g_n1, g_s1, gub, gck)
    if planes is not None:
        sums = lax.psum(sums, "dp", axis_index_groups=planes)
    w_o, ow_o, up_o, dn_o, g_ob, g_n2, g_s2, g_db, g_n1, g_s1, gub, gck = sums
    gqkv = jnp.transpose(w_o.reshape(3, lw, D), (2, 0, 1))
    return (res, gt, g_n1, g_s1, gqkv, gck, ow_o, g_ob, g_n2, g_s2, up_o, gub, dn_o, g_db)


def solution(mesh):
    dp = mesh.shape["dp"]
    planes = None
    if dp > 8:
        planes = [[8 * k + j for k in range(dp // 8)] for j in range(8)]
    rows_, rep = P_(("dp", "tensor"), None), P_()
    third, cols, first = P_(None, None, "tensor"), P_(None, "tensor"), P_("tensor", None)
    return jax.shard_map(
        functools.partial(per_device, planes),
        mesh=mesh,
        in_specs=(rows_, P_(("dp", "tensor")), rows_, rep, rep, third, third, first, rep, rep, rep, cols, P_("tensor"), first, rep),
        out_specs=(rows_, rows_, rep, rep, third, third, first, rep, rep, rep, cols, P_("tensor"), first, rep),
        check_vma=False,
    )
```

```python
import functools
import jax, jax.numpy as jnp
from jax import lax
from jax.experimental import pallas as pl
from jax.experimental.pallas import tpu as pltpu
from jax.sharding import PartitionSpec as P_

HD=64
BF=jnp.bfloat16; F32=jnp.float32
BIG=1e30
def nt(a,b): return lax.dot_general(a,b,(((1,),(1,)),((),())),preferred_element_type=F32)
def tn(a,b): return lax.dot_general(a,b,(((0,),(0,)),((),())),preferred_element_type=F32)
def nn(a,b): return jnp.dot(a,b,preferred_element_type=F32)

def keep_rows(ids):
    n=ids.shape[1]
    pos=lax.broadcasted_iota(jnp.int32,(1,n),1)
    out=[]
    for j in (1,2):
        prev=pltpu.roll(ids,j,1)
        out.append(jnp.where((prev==ids)&(pos>=j),1.0,0.0).astype(F32))
    return out

def feats(ids,rows,kind):
    n=ids.shape[1]
    r=lax.broadcasted_iota(jnp.int32,(rows,n),0)
    idb=jnp.broadcast_to(ids,(rows,n))
    if kind=="q":
        return jnp.where((r<4)&(idb!=r),-BIG,0.0).astype(F32)
    return jnp.where(((r<4)&(idb==r))|((r>=4)&(r<7)),1.0,0.0).astype(F32)

def split3(x):
    hi=x.astype(BF).astype(F32); r=x-hi; mid=r.astype(BF).astype(F32); lo=r-mid
    return hi,mid,lo

EPS=1e-5
def ln(x):
    mu=jnp.mean(x,-1,keepdims=True)
    c=x-mu
    inv=lax.rsqrt(jnp.mean(c*c,-1,keepdims=True)+EPS)
    return c*inv,inv
def ln_back(g,unit,inv,gain):
    s=g*gain
    return (s-jnp.mean(s,-1,keepdims=True)-unit*jnp.mean(s*unit,-1,keepdims=True))*inv
MESH=pl.DeviceIdType.MESH

class Place:
    def __init__(self):
        d=lax.axis_index("dp"); t=lax.axis_index("tensor")
        self.d,self.t=d,t
        b=d%2; p=t//2; q=t%2; base=d-b
        self.b,self.p,self.q,self.base=b,p,q,base
        self.same=1-(b+p)%2
        self.home=self.same==1
        self.near=(p+q)%2==1
        self.member=2*q+b
        self.quarter=(d//2)%4
        self.sib=(base+1-b,t)
        self.opp=(d,2*p+1-q)
        self.cross=(base+1-b,2*p+1-q)
        self.other=(d,2*(1-p)+q)
        self.dest=(base+q,2*b+p)
        self.source=(base+p,2*q+b)
        self.fixed=jnp.logical_and(b==p,b==q)
        dx=d+2-4*((d//2)%2); dy=d+4-8*((d//4)%2)
        self.x=(dx,t); self.y=(dy,t); self.xy=(dx+dy-d,t)
    def zed(self,r): return (self.d,(self.t+r)%4)
    def column(self):
        base=self.d-self.b
        out=[]
        for r in range(1,4):
            out.append((self.d,(self.t+r)%4))
        for r in range(4):
            out.append((base+1-self.b,(self.t+r)%4))
        return out

def meet(peers):
    bar=pltpu.get_barrier_semaphore()
    for dev in peers:
        pl.semaphore_signal(bar,inc=1,device_id=dev,device_id_type=MESH)
    pl.semaphore_wait(bar,len(peers))

class Net:
    def __init__(self,send,recv):
        self.send,self.recv,self.k=send,recv,0
    def to(self,src,dst,dev):
        k=self.k; self.k+=1
        return pltpu.make_async_remote_copy(src_ref=src,dst_ref=dst,send_sem=self.send.at[k],recv_sem=self.recv.at[k],device_id=dev,device_id_type=MESH)

class Swap:
    def __init__(self,net,src,dst,dev,fixed):
        self.r=net.to(src,dst,dev); self.fixed=fixed
        self.l=pltpu.make_async_copy(src,dst,net.recv.at[net.k-1])
    def start(self):
        pl.when(jnp.logical_not(self.fixed))(self.r.start)
        pl.when(self.fixed)(self.l.start)
    def wait_recv(self): self.l.wait()
    def wait_send(self): pl.when(jnp.logical_not(self.fixed))(self.r.wait_send)

def rows(ref,start,size): return ref.at[pl.ds(start,size)]

def lanes(start,size): return pl.ds(pl.multiple_of(start,128),size)
def rws(start,size): return pl.ds(pl.multiple_of(start,16),size)


class ToHeads:
    def __init__(self,net,P,src,dst):
        self.k=net.k; net.k+=4
        self.P,self.net,self.dst=P,net,dst
        self.far=[]
        for mm in range(4):
            c=pltpu.make_async_remote_copy(src_ref=src(mm),dst_ref=dst.at[P.t],send_sem=net.send.at[self.k+mm],recv_sem=net.recv.at[self.k+P.t],
                                           device_id=(P.base+mm%2,2*P.b+mm//2),device_id_type=MESH)
            l=pltpu.make_async_copy(src(mm),dst.at[P.t],net.recv.at[self.k+P.t])
            self.far.append((jnp.logical_and(P.home,P.member==mm),c,l))
    def start_one(self,k):
        me,c,l=self.far[k]
        pl.when(jnp.logical_not(me))(c.start)
        pl.when(me)(l.start)
    def start(self):
        for k in range(4): self.start_one(k)
    def wait_recv(self):
        for s in range(4):
            pltpu.make_async_copy(self.dst.at[s],self.dst.at[s],self.net.recv.at[self.k+s]).wait()
    def wait_send(self):
        for me,c,l in self.far: pl.when(jnp.logical_not(me))(c.wait_send)

def mix2(v, cks, r, c, keeps):
    out = cks[pl.ds(r, HD), c:c + 1] * v
    for j in (1, 2):
        out = out + cks[pl.ds(r, HD), 3 * j + c:3 * j + c + 1] * (pltpu.roll(v, j, 1) * keeps[j - 1])
    return out

def tap_columns(ckv, tmp, cks):
    lw = ckv.shape[2]
    tmp[...] = jnp.zeros(tmp.shape, F32)
    for j in range(3):
        for c in range(3):
            tmp[3 * j + c:3 * j + c + 1, 0:lw] = ckv[j, c:c + 1, :]
    cks[...] = tmp[...].T

NC = 4
def first_kernel(tok, ids, cot, wt, ck, ow, up, dn, vg1, vs1, vob, vg2, vs2, vdb, vub,
                 x_o, ids_o, wt_o, ck_o, proj_o, qt_o, qn_o, kk_o, kt_o, vn_o, of_o, res_o, gm_o, ga_in, ow_o, up_o, dn_o, l_ow, l_up, l_dn, small_o, gupb_o,
                 xv, xn, cotv, idv, wtv, ckv, tmp, cks, proj, qt, qn, kk, kt, vn, vt, att, attin, of, lse,
                 ow_a, up_a, dn_a, upb_a, sec, act, gh, gsec, gms, gas, c_ow, c_up, c_dn, send, recv, lsem, wsem):
    P = Place()
    net = Net(send, recv)
    n, D = tok.shape
    N = 4 * n
    heads = wt.shape[0] // (3 * HD)
    lw = heads * HD
    R = n // NC; H = R // 2
    m = P.member; t = P.t
    cotl = pltpu.make_async_copy(cot, cotv, lsem.at[15]); cotl.start()
    own = [pltpu.make_async_copy(a, b.at[t], lsem.at[j]) for j, (a, b) in enumerate(((ow, ow_a), (up, up_a), (dn, dn_a)))]
    for c in own: c.start()
    upb_a[t] = vub[...].reshape(1, -1)
    for k in range(NC):
        unit, _ = ln(tok[k * R:(k + 1) * R, :].astype(F32))
        xn[k * R:(k + 1) * R, :] = (unit * vg1[...].reshape(1, -1) + vs1[...].reshape(1, -1)).astype(BF)
    meet(P.column() + [P.x, P.y, P.xy])
    sends = []
    def later(src, dst, dev):
        c = net.to(src, dst, dev); sends.append(c); return c
    def push(src, dst, dev):
        c = later(src, dst, dev); c.start(); return c
    def swap(src, dst, dev):
        c = Swap(net, src, dst, dev, P.fixed); sends.append(c); return c
    Q = wt.shape[0] // 4
    w0 = pl.multiple_of(P.quarter * Q, 16)
    idg = ToHeads(net, P, lambda mm: ids, idv)
    idg.start()
    wq = swap(rows(wt, w0, Q), rows(wtv, w0, Q), P.dest); wq.start()
    ckc = swap(ck, ckv, P.dest); ckc.start()
    def part(ref, tt, k):
        L = ref.shape[2] // 2; r = ref.shape[1] // 4
        return ref.at[tt, pl.ds(pl.multiple_of(k * r, 16), r), pl.ds(pl.multiple_of(P.b * L, 128), L)]
    def part_in(ref):
        L = ref.shape[1] // 2; r = ref.shape[0] // 4
        return ref.at[pl.ds(pl.multiple_of(P.quarter * r, 16), r), pl.ds(pl.multiple_of(P.b * L, 128), L)]
    qx = (P.x[0] // 2) % 4; qy = (P.y[0] // 2) % 4; qd = (P.xy[0] // 2) % 4
    order = [t, t - 1 + 2 * (1 - (t + 3) // 4), 2 + t // 2 - 2 * (t // 3), 3 - 3 * (t // 2)]
    guarded = []
    right = (P.d, (t + 1) % 4); left = (P.d, (t + 3) % 4)
    class Spread:
        def __init__(self, ins, alls, b0):
            self.zr = net.k; net.k += 4 * len(ins)
            self.w = len(ins)
            def z_push(src, tt, j, cond, dev):
                k = net.k; net.k += 1
                c = pltpu.make_async_remote_copy(src_ref=src, dst_ref=part(alls[j], tt, P.quarter), send_sem=send.at[k],
                                                 recv_sem=recv.at[self.zr + self.w * tt + j], device_id=dev, device_id_type=MESH)
                guarded.append((cond, c))
                return lambda: pl.when(cond)(c.start)
            self.first = [z_push(part_in(ins[j]), t, j, cond, dev) for j in range(self.w) for cond, dev in ((t < 3, right), (t > 0, left))]
            self.steps = {}
            for r in (1, 2, 3):
                tt = order[r]
                arrive = []
                for j in range(self.w):
                    z = part(alls[j], tt, P.quarter)
                    wait = pltpu.make_async_copy(z, z, recv.at[self.zr + self.w * tt + j])
                    arrive.append([wait.wait, z_push(z, tt, j, jnp.logical_and(tt < t, t < 3), right),
                                   z_push(z, tt, j, jnp.logical_and(tt > t, t > 0), left)])
                mine = [part(a, tt, P.quarter) for a in alls]
                bx = [part(a, tt, qx) for a in alls]; by = [part(a, tt, qy) for a in alls]; bd = [part(a, tt, qd) for a in alls]
                ax = [later(z, z, P.x) for z in mine]; ay = [later(z, z, P.y) for z in mine]; asib = [later(z, z, P.sib) for z in mine]
                dx = [later(z, z, P.y) for z in bx[:b0]]; dy = [later(z, z, P.x) for z in by[b0:]]
                xs = [later(z, z, P.sib) for z in bx]; ys = [later(z, z, P.sib) for z in by]; ds_ = [later(z, z, P.sib) for z in bd]
                self.steps[r] = (arrive, ax, ay, asib, dx, dy, xs, ys, ds_)
        def start(self):
            for f in self.first: f()
        def a(self, r):
            arrive, ax, ay, asib = self.steps[r][:4]
            for step in arrive:
                for f in step: f()
            for c in ax + ay + asib: c.start()
        def b(self, r):
            _, ax, ay, _, dx, dy, xs, ys, _ = self.steps[r]
            for c in ax: c.wait_recv()
            for c in dx + xs: c.start()
            for c in ay: c.wait_recv()
            for c in dy + ys: c.start()
        def c(self, r):
            _, _, _, _, dx, dy, _, _, ds_ = self.steps[r]
            for c in dx + dy: c.wait_recv()
            for c in ds_: c.start()
        def end(self, r):
            _, _, _, asib, _, _, xs, ys, ds_ = self.steps[r]
            for c in asib + xs + ys + ds_: c.wait_recv()
    so = Spread((ow,), (ow_a,), 1)
    sw = Spread((up, dn), (up_a, dn_a), 1)
    bias = [push(upb_a.at[t], upb_a.at[t], P.zed(r)) for r in (1, 2, 3)]
    opp_shard = 2 * P.p + 1 - P.q
    target = P.same * opp_shard + (1 - P.same) * (1 + P.b)
    far_shards = (2 * (1 - P.p), 2 * (1 - P.p) + 1)
    ka = net.k; kb = ka + 4 * NC; kc = kb + NC; kd = kc + 4 * NC; net.k = kd + 4 * NC
    def raw(src, dst, ks, kr, dev):
        return pltpu.make_async_remote_copy(src_ref=src, dst_ref=dst, send_sem=send.at[ks], recv_sem=recv.at[kr], device_id=dev, device_id_type=MESH)
    sent = []
    def give_piece(k):
        z = pl.ds(k * R, R)
        for h in range(2):
            zh = pl.ds(k * R + h * H, H)
            c = raw(xn.at[zh], xv.at[t, zh], ka + 4 * k + h, ka + 4 * k + t, (P.base + h, target)); c.start(); sent.append(c)
        c = raw(xn.at[z], xv.at[t, z], kb + k, kb + k, P.sib)
        pl.when(P.home)(c.start); guarded.append((P.home, c))
    def relay(k):
        zb = pl.ds(pl.multiple_of(k * R + P.b * H, 16), H)
        for j, s in enumerate((opp_shard,) + far_shards):
            blk = xv.at[s, zb]
            if j == 0:
                pltpu.make_async_copy(blk, blk, recv.at[ka + 4 * k + s]).wait()
            else:
                on = raw(blk, blk, kd + 4 * k + j, kd + 4 * k + s, P.opp)
                @pl.when(P.near)
                def _():
                    pltpu.make_async_copy(blk, blk, recv.at[ka + 4 * k + s]).wait()
                    on.start()
                guarded.append((P.near, on))
                @pl.when(jnp.logical_not(P.near))
                def _():
                    pltpu.make_async_copy(blk, blk, recv.at[kd + 4 * k + s]).wait()
            c = raw(blk, blk, kc + 4 * k + j, kc + 4 * k + s, P.sib); c.start(); sent.append(c)
    so.start()
    give_piece(0); give_piece(1)
    sw.start()
    relay(0)
    give_piece(2)
    wq.wait_recv()
    wf = [push(rows(wtv, w0, Q), rows(wtv, w0, Q), dev) for dev in (P.x, P.y, P.xy)]
    relay(1)
    so.a(1)
    give_piece(3)
    relay(2)
    so.a(2); sw.a(1)
    relay(3)
    so.a(3)
    @pl.when(P.home)
    def _(): xv[t] = xn[...]
    for c in wf: c.wait_recv()
    def project(s):
        proj[:, pl.ds(pl.multiple_of(s * n, 128), n)] = nt(wtv[...], xv[s])
    @pl.when(jnp.logical_not(P.home))
    def _():
        for k in range(NC): pltpu.make_async_copy(xv.at[t, pl.ds(k * R, R)], xv.at[t, pl.ds(k * R, R)], recv.at[kb + k]).wait()
    project(t)
    so.b(1); so.b(2)
    for k in range(NC):
        zo = pl.ds(pl.multiple_of(k * R + (1 - P.b) * H, 16), H)
        pltpu.make_async_copy(xv.at[opp_shard, zo], xv.at[opp_shard, zo], recv.at[kc + 4 * k + opp_shard]).wait()
    project(opp_shard)
    so.b(3); so.c(1); sw.a(2)
    for k in range(NC):
        zo = pl.ds(pl.multiple_of(k * R + (1 - P.b) * H, 16), H)
        for s in far_shards:
            pltpu.make_async_copy(xv.at[s, zo], xv.at[s, zo], recv.at[kc + 4 * k + s]).wait()
    for s in far_shards: project(s)
    so.c(2); so.c(3)
    idg.wait_recv()
    ckc.wait_recv()
    outs = [pltpu.make_async_copy(a, b, lsem.at[4 + k]) for k, (a, b) in enumerate(
        ((xv, x_o), (wtv, wt_o), (proj, proj_o), (ckv, ck_o)))]
    for c in outs: c.start()
    idrow = jnp.concatenate([idv[s] for s in range(4)], axis=1)
    idv_out = pltpu.make_async_copy(idv, ids_o, lsem.at[9]); idv_out.start()
    keeps = keep_rows(idrow)
    tap_columns(ckv, tmp, cks)
    fq = feats(idrow, 64, "q").astype(BF); fk = feats(idrow, 64, "k")
    qt[64:128, :] = fq
    vt[64:80, :] = jnp.ones((16, N), BF)
    tri = lax.broadcasted_iota(jnp.int32, (n, n), 0) <= lax.broadcasted_iota(jnp.int32, (n, n), 1)
    eb = net.k; net.k += 4 * heads
    def give(h, tt):
        r = pl.ds(pl.multiple_of(h * HD, HD), HD)
        return raw(att.at[tt, r], attin.at[m, r], eb + 4 * h + tt, eb + 4 * h + m, (P.base + P.p, tt))
    def not_me(tt): return jnp.logical_not(jnp.logical_and(P.home, t == tt))
    def not_mine(mm): return jnp.logical_not(jnp.logical_and(P.home, m == mm))
    def at(*fs):
        def run():
            for f, r in fs: f(r)
        return run
    turns = {0: at((sw.b, 1)), 1: at((sw.a, 3)), 2: at((sw.b, 2), (sw.c, 1))}
    def head(h, _):
        for hh, fs in turns.items(): pl.when(h == hh)(fs)
        r = pl.multiple_of(h * HD, HD)
        def part_rows(c): return proj[pl.ds(pl.multiple_of(c * lw + h * HD, HD), HD), :]
        q = mix2(part_rows(0), cks, r, 0, keeps)
        qt[0:64, :] = (q.astype(BF).astype(F32) * 0.125).astype(BF)
        k = mix2(part_rows(1), cks, r, 1, keeps)
        kk[...] = jnp.concatenate([k, fk], 0).T.astype(BF)
        vt[0:64, :] = mix2(part_rows(2), cks, r, 2, keeps).astype(BF)
        for iq in range(4):
            qs = iq * n
            qb = qt[:, qs:qs + n]
            ss = []
            for j in range(iq): ss.append(nn(kk[j * n:(j + 1) * n, :], qb))
            hn = n // 2
            ss.append(jnp.where(tri[0:hn], nn(kk[qs:qs + hn, :], qb), -BIG))
            late = jnp.where(tri[0:hn, 0:hn], nn(kk[qs + hn:qs + n, :], qb[:, hn:n]), -BIG)
            mx = jnp.max(ss[0], axis=0, keepdims=True)
            for s in ss[1:]: mx = jnp.maximum(mx, jnp.max(s, axis=0, keepdims=True))
            mx = jnp.concatenate([mx[:, 0:hn], jnp.maximum(mx[:, hn:n], jnp.max(late, axis=0, keepdims=True))], 1)
            o = jnp.concatenate([jnp.zeros((80, hn), F32), nn(vt[:, qs + hn:qs + n], jnp.exp(late - mx[:, hn:n]).astype(BF))], 1)
            for j, s in enumerate(ss):
                o = o + nn(vt[:, j * n:j * n + s.shape[0]], jnp.exp(s - mx).astype(BF))
            l = o[64:65, :]
            f = o[0:64, :] / l
            of[pl.ds(r, HD), qs:qs + n] = f
            att[iq, pl.ds(r, HD), :] = f.astype(BF)
            lse[h, :, qs:qs + n] = jnp.broadcast_to(mx + jnp.log(l), (8, n))
        for tt in range(4): pl.when(not_me(tt))(give(h, tt).start)
        return 0
    lax.fori_loop(0, heads, head, 0)
    @pl.when(P.home)
    def _(): attin[m] = att[t]
    ends = [pltpu.make_async_copy(a, b, lsem.at[11 + k]) for k, (a, b) in enumerate(((of, of_o),))]
    for c in ends: c.start()
    sw.c(2); sw.b(3)
    for r in (1, 2, 3): so.end(r)
    for c in own: c.wait()
    for h in range(heads):
        r = pl.ds(h * HD, HD)
        for mm in range(4):
            pl.when(not_mine(mm))(pltpu.make_async_copy(attin.at[mm, r], attin.at[mm, r], recv.at[eb + 4 * h + mm]).wait)
            pl.when(not_me(mm))(give(h, mm).wait_send)
    attT = attin[...].reshape(4 * lw, n)
    gms[...] = tok[...].astype(F32) + tn(attT, ow_a[...].reshape(4 * lw, D)) + vob[...].reshape(1, -1)
    unit, inv = ln(gms[...])
    sec[...] = (unit * vg2[...].reshape(1, -1) + vs2[...].reshape(1, -1)).astype(BF)
    for c in bias: c.wait_recv()
    sw.c(3)
    cotl.wait()
    gsec[...] = jnp.zeros_like(gsec)
    def chain(tt):
        rl = jnp.maximum(nn(sec[...], up_a[tt]) + upb_a[tt], 0.0)
        act[tt] = (rl * rl).astype(BF)
        g = (nt(cotv[...], dn_a[tt]) * (2.0 * rl)).astype(BF)
        gh[tt] = g
        gupb_o[tt] = jnp.sum(g.astype(F32), 0, keepdims=True)
        gsec[...] += nt(g, up_a[tt])
    chain(order[0])
    sw.end(1); chain(order[1])
    sw.end(2); chain(order[2])
    sw.end(3); chain(order[3])
    mid = gms[...]
    unit, inv = ln(mid)
    gs = gsec[...]
    cf = cotv[...].astype(F32)
    gm = cf + ln_back(gs, unit, inv, vg2[...].reshape(1, -1))
    gmb = gm.astype(BF)
    gb = ToHeads(net, P, lambda mm: gas.at[mm], ga_in)
    for mm in range(4):
        gas[mm] = nt(ow_a[mm], gmb).astype(BF)
        gb.start_one(mm)
    gsec[...] = gm
    gmo = pltpu.make_async_copy(gsec, gm_o, lsem.at[14]); gmo.start()
    small_o[0:1] = jnp.sum(gm, 0, keepdims=True)
    small_o[1:2] = jnp.sum(gs * unit, 0, keepdims=True)
    small_o[2:3] = jnp.sum(gs, 0, keepdims=True)
    small_o[3:4] = jnp.sum(cf, 0, keepdims=True)
    small_o[4:8] = jnp.zeros((4, D), F32)
    out = mid + vdb[...].reshape(1, -1)
    for b in range(4): out = out + nn(act[b], dn_a[b])
    res_o[...] = out.astype(BF)
    for c in sends: c.wait_send()
    for cond, c in guarded: pl.when(cond)(c.wait_send)
    L = D // 2
    lo, lx = P.b * L, (1 - P.b) * L
    blocks = [1 - P.q, 3 - P.q, 2 * (1 - P.p) + P.q, t]
    ow_a[...] = nn(attT, gmb).astype(BF).reshape(ow_a.shape)
    trios = ((ow_a, c_ow, ow_o), (dn_a, c_dn, dn_o), (up_a, c_up, up_o))
    halves, fin = [], []
    def grads(k):
        tt = blocks[k]
        dn_a[tt] = tn(act[tt], cotv[...]).astype(BF)
        up_a[tt] = tn(sec[...], gh[tt]).astype(BF)
        cs = []
        for g, cref, _ in trios:
            c = net.to(g.at[tt, :, lanes(lx, L)], cref.at[tt], P.sib); c.start(); cs.append(c)
        halves.append(cs)
    def cores(k):
        tt = blocks[k]
        for j, (g, cref, o) in enumerate(trios):
            halves[k][j].wait_recv()
            cref[tt] = (cref[tt].astype(F32) + g[tt, :, lanes(lo, L)].astype(F32)).astype(BF)
            z = pltpu.make_async_copy(cref.at[tt], o.at[tt], wsem.at[3 * k + j]); z.start(); fin.append(z)
    grads(0); grads(1)
    cores(0)
    ro, ru = ow.shape[0] // 4, up.shape[0] // 4
    pc = []
    def plane(j):
        for src, dst, r_, ks, dev in ((c_ow, l_ow, ro, (qx, qd), P.x), (c_up, l_up, ru, (qx, qd), P.x), (c_dn, l_dn, ru, (qy, qd), P.y)):
            for i, k in enumerate(ks):
                c = net.to(src.at[blocks[j], rws(k * r_, r_)], dst.at[j, i], dev); c.start(); pc.append(c)
    plane(0)
    grads(2); cores(1)
    grads(3)
    r8 = lax.broadcasted_iota(jnp.int32, (64, N), 0)
    zl = jnp.zeros((64, N), F32)
    fqf = feats(idrow, 64, "q")
    pieces = ((qt, qt_o), (qn, qn_o), (kk, kk_o), (kt, kt_o), (vn, vn_o))
    def prepare(h, _):
        r = pl.multiple_of(h * HD, HD)
        def part_rows(c): return proj[pl.ds(pl.multiple_of(c * lw + h * HD, HD), HD), :]
        q = mix2(part_rows(0), cks, r, 0, keeps).astype(BF).astype(F32) * 0.125
        hi, mid_, low = split3(-lse[h, 0:1, :])
        k = mix2(part_rows(1), cks, r, 1, keeps)
        v = mix2(part_rows(2), cks, r, 2, keeps)
        @pl.when(h > 0)
        def _():
            for j, (a, o) in enumerate(pieces): pltpu.make_async_copy(a, o.at[0], wsem.at[12 + j]).wait()
        qt[0:64, :] = q.astype(BF)
        qt[64:128, :] = (fqf + jnp.where(r8 == 4, hi, 0.0) + jnp.where(r8 == 5, mid_, 0.0) + jnp.where(r8 == 6, low, 0.0)).astype(BF)
        qn[...] = jnp.concatenate([zl, q], 0).T.astype(BF)
        kt[...] = k.astype(BF)
        kk[...] = jnp.concatenate([k, fk], 0).T.astype(BF)
        vn[...] = jnp.concatenate([v, jnp.where(r8 < 3, 1.0, 0.0)], 0).T.astype(BF)
        for j, (a, o) in enumerate(pieces): pltpu.make_async_copy(a, o.at[h], wsem.at[12 + j]).start()
        return 0
    lax.fori_loop(0, heads, prepare, 0)
    cores(2); cores(3)
    for j, (a, o) in enumerate(pieces): pltpu.make_async_copy(a, o.at[0], wsem.at[12 + j]).wait()
    for cs in halves:
        for c in cs: c.wait_send()
    for c in sent: c.wait_send()
    idg.wait_send()
    for c in outs + [idv_out, gmo] + ends + fin: c.wait()
    for c in pc: c.wait()
    gb.wait_send()
    gb.wait_recv()

def first(tok, ids, cot, wt, ck, ow, up, dn, *vecs):
    n, D = tok.shape; S = jax.ShapeDtypeStruct; V = pltpu.VMEM
    lw = wt.shape[0] // 3; heads = lw // HD; N = 4 * n; fb = up.shape[1]
    any_ = pl.BlockSpec(memory_space=pl.ANY); vm = pl.BlockSpec(memory_space=pltpu.VMEM)
    outs = [(S((4, n, D), BF), any_), (S((4, 1, n), jnp.int32), any_), (S(wt.shape, BF), any_), (S(ck.shape, F32), any_),
            (S((3 * lw, N), F32), any_), (S((heads, 128, N), BF), any_), (S((heads, N, 128), BF), any_), (S((heads, N, 128), BF), any_),
            (S((heads, HD, N), BF), any_), (S((heads, N, 128), BF), any_), (S((lw, N), F32), any_),
            (S((n, D), BF), vm), (S((n, D), F32), any_), (S((4, lw, n), BF), any_),
            (S((4, lw, D // 2), BF), any_), (S((4, D, fb // 2), BF), any_), (S((4, fb, D // 2), BF), any_),
            (S((2, 2, lw // 4, D // 2), BF), any_), (S((2, 2, D // 4, D // 2), BF), any_), (S((2, 2, fb // 4, D // 2), BF), any_), (S((8, D), F32), vm), (S((4, 1, fb), F32), vm)]
    return pl.pallas_call(first_kernel, out_shape=tuple(o[0] for o in outs),
        in_specs=[vm] + [any_] * 7 + [vm] * 7, out_specs=tuple(o[1] for o in outs),
        scratch_shapes=[V((4, n, D), BF), V((n, D), BF), V((n, D), BF), V((4, 1, n), jnp.int32), V(wt.shape, BF), V(ck.shape, F32), V((128, 256), F32), V((256, 128), F32),
                        V((3 * lw, N), F32), V((128, N), BF), V((N, 128), BF), V((N, 128), BF), V((HD, N), BF), V((N, 128), BF), V((80, N), BF), V((4, lw, n), BF), V((4, lw, n), BF), V((lw, N), F32), V((heads, 8, N), F32),
                        V((4, lw, D), BF), V((4, D, fb), BF), V((4, fb, D), BF), V((4, 1, fb), F32),
                        V((n, D), BF), V((4, n, fb), BF), V((4, n, fb), BF), V((n, D), F32), V((n, D), F32), V((4, lw, n), BF),
                        V((4, lw, D // 2), BF), V((4, D, fb // 2), BF), V((4, fb, D // 2), BF),
                        pltpu.SemaphoreType.DMA((240,)), pltpu.SemaphoreType.DMA((240,)), pltpu.SemaphoreType.DMA((16,)), pltpu.SemaphoreType.DMA((20,))],
        compiler_params=pltpu.CompilerParams(collective_id=0, has_side_effects=True, vmem_limit_bytes=60 * 2**20),
        name="forward_and_feed",
    )(tok, ids, cot, wt, ck, ow, up, dn, *vecs)
def second_kernel(x_h, wt, ck, ids, proj_h, qt_h, qn_h, kk_h, kt_h, vn_h, of_h, ga, tok, gm, s_ow, s_up, s_dn, l_ow, l_up, l_dn, s4, gupb, vec,
                  gt_o, ow_o, up_o, dn_o, w_o, small_o,
                  x, proj, qt, qn, kk, kt, vn, dot, don, dkv, gconv, gp, gw, gwb, gfs, land1, land2, fin, g_s,
                  tmp, cks, cacc, own_x, own_y, own_o, x_ow, x_up, y_dn, z_ow, z_up, z_dn, o_ow, o_up, o_dn, f_ow, f_up, f_dn,
                  w1, w2, f_w, sl, sa, sb, sc, la, lb, send, recv, lsem):
    P = Place()
    plane = []
    for r in (P.x, P.y, P.xy): plane += [r, (r[0] + 1 - 2 * P.b, r[1])]
    net = Net(send, recv)
    n, D = tok.shape; N = 4 * n; H = n // 2; L = D // 2
    heads = wt.shape[0] // (3 * HD); lw = heads * HD
    m, t, b, p = P.member, P.t, P.b, P.p
    f32 = lambda v: v.astype(F32)
    started, guarded = [], []
    def later(src, dst, dev):
        c = net.to(src, dst, dev); started.append(c); return c
    def push(src, dst, dev):
        c = later(src, dst, dev); c.start(); return c
    def raw(src, dst, ks, kr, dev):
        return pltpu.make_async_remote_copy(src_ref=src, dst_ref=dst, send_sem=send.at[ks], recv_sem=recv.at[kr], device_id=dev, device_id_type=MESH)
    qr = P.quarter; qx = (P.x[0] // 2) % 4; qy = (P.y[0] // 2) % 4; qd = (P.xy[0] // 2) % 4
    lo = b * L
    ro, ru = s_ow.shape[1] // 4, s_up.shape[1] // 4
    blocks = [1 - P.q, 3 - P.q, 2 * (1 - p) + P.q, t]
    lc = [0]
    def local(src, dst):
        c = pltpu.make_async_copy(src, dst, lsem.at[lc[0]]); lc[0] += 1; c.start(); return c
    class Block:
        def __init__(self, j):
            tt = blocks[j]
            self.j, self.tt = j, tt
            q_ = lambda ref, k, r_: ref.at[tt, rws(k * r_, r_), :]
            self.p1x, self.p1y = [], []
            if j > 0:
                self.p1x = [later(q_(s_ow, k, ro), x_ow.at[j, i], P.x) for i, k in ((0, qx), (1, qd))] + \
                           [later(q_(s_up, k, ru), x_up.at[j, i], P.x) for i, k in ((0, qx), (1, qd))]
                self.p1y = [later(q_(s_dn, k, ru), y_dn.at[j, i], P.y) for i, k in ((0, qy), (1, qd))]
            self.p3 = [later(x_ow.at[j, 1], z_ow.at[j], P.y), later(x_up.at[j, 1], z_up.at[j], P.y), later(y_dn.at[j, 1], z_dn.at[j], P.x)]
        def load(self):
            tt, j = self.tt, self.j
            q_ = lambda ref, k, r_: ref.at[tt, rws(k * r_, r_), :]
            self.loads = [local(q_(s_ow, k, ro), own_o.at[j, i]) for i, k in ((0, qr), (1, qy))] + \
                         [local(q_(s_up, k, ru), own_x.at[j, i]) for i, k in ((0, qr), (1, qy))] + \
                         [local(q_(s_dn, k, ru), own_y.at[j, i]) for i, k in ((0, qr), (1, qx))]
            if j < 1:
                self.loads += [local(a.at[j], z.at[j]) for a, z in ((l_ow, x_ow), (l_up, x_up), (l_dn, y_dn))]
        def a(self):
            if self.j > 0:
                for c in self.p1x + self.p1y: c.start()
        def b(self):
            j = self.j
            for c in self.loads: c.wait()
            for c in self.p1x + self.p1y: c.wait_recv()
            for z, o in ((x_ow, own_o), (x_up, own_x), (y_dn, own_y)):
                z[j] = (f32(z[j]) + f32(o[j])).astype(BF)
            for c in self.p3: c.start()
        def c(self):
            j = self.j
            for c in self.p3: c.wait_recv()
            for z, o in ((z_ow, x_ow), (z_up, x_up), (z_dn, y_dn)):
                z[j] = (f32(z[j]) + f32(o[j, 0])).astype(BF)
    B = [Block(j) for j in range(4)]
    zs = ((z_ow, o_ow, f_ow), (z_up, o_up, f_up), (z_dn, o_dn, f_dn))
    zz = [[later(z.at[j], o.at[j], P.opp) for j in (0, 1)] for z, o, f in zs]
    z2 = [later(z.at[2], f.at[0], P.other) for z, o, f in zs]
    def opp_send(j):
        for cc in zz: cc[j].start()
    def opp_add():
        for (z, o, f), cc in zip(zs, zz):
            for c in cc: c.wait_recv()
            z[2] = (f32(z[2]) + f32(o[1 - p])).astype(BF)
        for c in z2: c.start()
    outs = ((ow_o, f_ow, ro), (up_o, f_up, ru), (dn_o, f_dn, ru))
    def place(o, k, r_): return o.at[rws(k * r_, r_), lanes(lo, L)]
    class Share:
        def __init__(self, o, src, r_, by_x):
            self.own = (src, place(o, qr, r_))
            self.sx = later(src, place(o, qr, r_), P.x); self.sy = later(src, place(o, qr, r_), P.y); self.ss = later(src, place(o, qr, r_), P.sib)
            px, py, pd = place(o, qx, r_), place(o, qy, r_), place(o, qd, r_)
            self.dg = later(px, px, P.y) if by_x else later(py, py, P.x)
            self.by_x = by_x
            self.fx, self.fy, self.fd = later(px, px, P.sib), later(py, py, P.sib), later(pd, pd, P.sib)
        def a(self):
            for c in (self.sx, self.sy, self.ss): c.start()
            self.l = local(*self.own)
        def b(self):
            self.sx.wait_recv()
            if self.by_x: self.dg.start()
            self.fx.start()
            self.sy.wait_recv()
            if not self.by_x: self.dg.start()
            self.fy.start()
        def c(self):
            self.dg.wait_recv(); self.fd.start()
        def end(self):
            for c in (self.ss, self.fx, self.fy, self.fd): c.wait_recv()
            self.l.wait()
    sh = [Share(o, f.at[1], r_, bx) for (o, f, r_), bx in zip(outs, (True, True, False))]
    shw = Share(w_o, f_w, wt.shape[0] // 4, False)
    def final_add():
        for (z, o, f), c in zip(zs, z2):
            c.wait_recv()
            f[1] = (f32(f[0]) + f32(z[3]) + f32(o[p])).astype(BF)
    ldo = local(of_h, gconv.at[pl.ds(0, lw)])
    for j in range(4): B[j].load()
    lda = [local(a, z) for a, z in ((qt_h, qt), (kk_h, kk), (vn_h, vn), (qn_h, qn), (kt_h, kt))]
    ldp = local(proj_h, proj)
    ldx = local(x_h, x)
    meet(P.column() + plane)
    B[1].a()
    B[0].b()
    idrow = jnp.concatenate([ids[s] for s in range(4)], axis=1)
    keeps = keep_rows(idrow)
    tap_columns(ck, tmp, cks)
    cacc[...] = jnp.zeros(cacc.shape, F32)
    r8 = lax.broadcasted_iota(jnp.int32, (64, N), 0)
    zl = jnp.zeros((64, N), F32)
    ldo.wait()
    def setup(h, _):
        r = pl.multiple_of(h * HD, HD)
        do = f32(jnp.concatenate([ga[s, pl.ds(r, HD), :] for s in range(4)], axis=1))
        inner = jnp.sum(do * gconv[pl.ds(r, HD), :], axis=0, keepdims=True)
        hi, mid, low = split3(-inner)
        f = jnp.where(r8 == 0, hi, 0.0) + jnp.where(r8 == 1, mid, 0.0) + jnp.where(r8 == 2, low, 0.0)
        dot[h, 0:64, :] = do.astype(BF); dot[h, 64:128, :] = f.astype(BF)
        don[h] = jnp.concatenate([do, zl], 0).T.astype(BF)
        return 0
    lax.fori_loop(0, heads, setup, 0)
    for c in lda: c.wait()
    tri = lax.broadcasted_iota(jnp.int32, (n, n), 0) <= lax.broadcasted_iota(jnp.int32, (n, n), 1)
    opp_shard = 2 * p + 1 - P.q
    h0 = pl.multiple_of(b * H, 16); h1 = pl.multiple_of((1 - b) * H, 16)
    e1 = [later(gfs.at[s, pl.ds(h1, H)], land1.at[s], P.sib) for s in range(4)]
    k2 = net.k; k3 = k2 + 4; k4 = k3 + 4; net.k = k4 + 2
    def far_side(s): return s // 2 != p
    def to_opp(s):
        cond = jnp.logical_or(opp_shard == s, jnp.logical_and(far_side(s), jnp.logical_not(P.near)))
        return cond, raw(land1.at[s], land2.at[s], k2 + s, k2 + s, P.opp)
    def summing(s): return jnp.logical_or(t == s, jnp.logical_and(far_side(s), P.near))
    def to_owner(s):
        cond = jnp.logical_and(summing(s), jnp.logical_not(jnp.logical_and(P.home, t == s)))
        return cond, raw(land2.at[s], fin.at[b], k3 + s, k4 + b, (P.base + p, s))
    opps = [to_opp(s) for s in range(4)]; owners = [to_owner(s) for s in range(4)]
    guarded += opps + owners
    def s1(s): e1[s].start()
    def s2(s):
        e1[s].wait_recv()
        land1[s] = (f32(land1[s]) + f32(gfs[s, pl.ds(h0, H)])).astype(BF)
        cond, c = opps[s]; pl.when(cond)(c.start)
    def s3(s):
        @pl.when(summing(s))
        def _():
            pltpu.make_async_copy(land2.at[s], land2.at[s], recv.at[k2 + s]).wait()
            land2[s] = (f32(land2[s]) + f32(land1[s])).astype(BF)
        cond, c = owners[s]; pl.when(cond)(c.start)
    def rows_of(i, points):
        qs = i * n
        def head(h, _):
            for hh, f in points.items(): pl.when(h == hh)(f)
            dq = jnp.zeros((64, n), F32)
            for j in range(i + 1):
                js = j * n
                st = nn(kk[h, js:js + n, :], qt[h, :, qs:qs + n])
                pr = jnp.exp(st)
                if i == j: pr = jnp.where(tri, pr, 0.0)
                dp = nn(vn[h, js:js + n, :], dot[h, :, qs:qs + n])
                ds = (pr * dp).astype(BF)
                add = nn(pr.astype(BF), don[h, qs:qs + n, :]) + nn(ds, qn[h, qs:qs + n, :])
                if i == 3: dkv[h, js:js + n, :] = add
                else: dkv[h, js:js + n, :] += add
                dq = dq + nn(kt[h, :, js:js + n], ds)
            gconv[pl.ds(pl.multiple_of(h * HD, HD), HD), qs:qs + n] = dq * 0.125
            if i == 3: pl.when(h == 0)(ldp.wait)
            tt = dkv[h, qs:qs + n, :].T
            gconv[pl.ds(pl.multiple_of(2 * lw + h * HD, HD), HD), qs:qs + n] = tt[0:64]
            gconv[pl.ds(pl.multiple_of(lw + h * HD, HD), HD), qs:qs + n] = tt[64:128]
            for c in range(3):
                r = pl.ds(pl.multiple_of(c * lw + h * HD, HD), HD); rk = pl.ds(pl.multiple_of(h * HD, HD), HD)
                g = gconv[r, qs:qs + n]
                nxt = jnp.zeros((HD, 128), F32) if i == 3 else gconv[r, qs + n:qs + n + 128]
                gx = jnp.concatenate([g, nxt], 1)
                pc = proj[r, qs:qs + n]
                prv = jnp.zeros((HD, 128), F32) if i == 0 else proj[r, qs - 128:qs]
                px = jnp.concatenate([prv, pc], 1)
                o = cks[rk, c:c + 1] * g
                cacc[rk, c:c + 1] += jnp.sum(g * pc, axis=1, keepdims=True)
                for jj in (1, 2):
                    kr = keeps[jj - 1][:, qs:qs + n]
                    kn = jnp.zeros((1, 128), F32) if i == 3 else keeps[jj - 1][:, qs + n:qs + n + 128]
                    kg = gx * jnp.concatenate([kr, kn], 1)
                    cacc[rk, 3 * jj + c:3 * jj + c + 1] += jnp.sum(kg[:, 0:n] * pltpu.roll(px, jj, 1)[:, 128:], axis=1, keepdims=True)
                    o = o + cks[rk, 3 * jj + c:3 * jj + c + 1] * pltpu.roll(kg, n + 128 - jj, 1)[:, 0:n]
                gp[r, :] = o.astype(BF)
            return 0
        lax.fori_loop(0, heads, head, 0)
        gfs[i] = tn(gp[...], wt[...]).astype(BF)
        s1(i)
        if i == 3: ldx.wait()
        g = nn(gp[...], x[i])
        if i == 3: gw[...] = g
        else: gw[...] += g
    def at(*fs):
        def run():
            for f in fs: f()
        return run
    rows_of(3, {1: at(B[1].b, B[2].a, B[0].c, lambda: opp_send(0)), 2: at(B[3].a)})
    rows_of(2, {0: at(B[1].c, lambda: opp_send(1)), 1: at(lambda: s2(3), B[2].b)})
    rows_of(1, {0: at(lambda: s3(3), B[2].c, B[3].b), 1: at(lambda: s2(2))})
    rows_of(0, {0: at(lambda: s2(1), opp_add, B[3].c), 1: at(lambda: s3(2))})
    Q = wt.shape[0] // 4
    gwb[...] = gw[...].astype(BF)
    wx = [push(gwb.at[rws(k * Q, Q)], w1.at[j], dev) for j, (k, dev) in enumerate(((qx, P.x), (qy, P.y), (qd, P.xy)))]
    me = P.d % 8
    peers = plane + [P.sib]
    sl[...] = jnp.zeros(sl.shape, F32)
    def put(row, v): sl[row // 6, pl.ds(row % 6, 1), 0:v.shape[1]] = v
    for k in range(4): put(k, s4[k:k + 1])
    for k in range(4): put(6 + k, gupb[k])
    ct = cacc[...].T
    for k in range(9): put(10 + 9 * m + k, ct[k:k + 1, 0:lw])
    k6 = net.k; k7 = k6 + 8; k8 = k7 + 4; k9 = k8 + 8; ka = k9 + 8; k5 = ka + 4; net.k = k5 + 2
    hop1 = [raw(sl.at[dev[0] % 8], sa.at[me], k6 + j, k6 + me, dev) for j, dev in enumerate(peers)]
    for c in hop1: c.start()
    sa[me] = sl[me]
    s2(0); s3(1)
    unit, inv = ln(f32(tok[...]))
    for c in wx: c.wait_recv()
    w1[0] = (f32(w1[0]) + f32(w1[1]) + f32(w1[2]) + f32(gwb[rws(qr * Q, Q)])).astype(BF)
    for h in range(2):
        mine = jnp.logical_and(t == m, b == h)
        src, dst = w1.at[0, :, pl.ds(h * L, L)], w2.at[p]
        c = raw(src, dst, k5 + h, k5 + p, (P.base + h, m))
        l = pltpu.make_async_copy(src, dst, recv.at[k5 + p])
        pl.when(jnp.logical_not(mine))(c.start); pl.when(mine)(l.start)
        guarded.append((jnp.logical_not(mine), c))
    for dev in peers: pltpu.make_async_copy(sl.at[0], sa.at[dev[0] % 8], recv.at[k6 + dev[0] % 8]).wait()
    tot = sa[0]
    for k in range(1, 8): tot = tot + sa[k]
    sb[t] = tot
    hop2 = [raw(sb.at[t], sb.at[t], k7 + r, k7 + t, P.zed(r)) for r in (1, 2, 3)]
    for c in hop2: c.start()
    final_add()
    for s in sh: s.a()
    s3(0)
    for h in range(2): pltpu.make_async_copy(w2.at[h], w2.at[h], recv.at[k5 + h]).wait()
    f_w[...] = (f32(w2[0]) + f32(w2[1])).astype(BF)
    shw.a()
    for r in (1, 2, 3): pltpu.make_async_copy(sb.at[(t + r) % 4], sb.at[(t + r) % 4], recv.at[k7 + (t + r) % 4]).wait()
    sc[me] = sb[0] + sb[1] + sb[2] + sb[3]
    hop3 = [raw(sc.at[me], sc.at[me], k8 + j, k8 + me, dev) for j, dev in enumerate(peers)]
    for c in hop3: c.start()
    @pl.when(P.home)
    def _(): fin[b] = land2[t]
    @pl.when(jnp.logical_not(P.home))
    def _(): pltpu.make_async_copy(fin.at[b], fin.at[b], recv.at[k4 + b]).wait()
    pltpu.make_async_copy(fin.at[1 - b], fin.at[1 - b], recv.at[k4 + 1 - b]).wait()
    g_s[0:H] = f32(fin[0]); g_s[H:n] = f32(fin[1])
    g = g_s[...]
    la[me] = jnp.concatenate([jnp.sum(g * unit, 0, keepdims=True), jnp.sum(g, 0, keepdims=True), jnp.zeros((6, D), F32)], 0)
    late1 = [raw(la.at[me], la.at[me], k9 + j, k9 + me, dev) for j, dev in enumerate(peers)]
    for c in late1: c.start()
    gt_o[...] = gm[...] + ln_back(g, unit, inv, vec[...].reshape(1, -1))
    for s in sh + [shw]: s.b()
    for dev in peers: pltpu.make_async_copy(la.at[me], la.at[dev[0] % 8], recv.at[k9 + dev[0] % 8]).wait()
    tot = la[0]
    for k in range(1, 8): tot = tot + la[k]
    lb[t] = tot
    late2 = [raw(lb.at[t], lb.at[t], ka + r, ka + t, P.zed(r)) for r in (1, 2, 3)]
    for c in late2: c.start()
    for s in sh + [shw]: s.c()
    for dev in peers: pltpu.make_async_copy(sc.at[0], sc.at[dev[0] % 8], recv.at[k8 + dev[0] % 8]).wait()
    small_o[0:8] = sc[...]
    for r in (1, 2, 3): pltpu.make_async_copy(lb.at[(t + r) % 4], lb.at[(t + r) % 4], recv.at[ka + (t + r) % 4]).wait()
    small_o[8] = lb[0] + lb[1] + lb[2] + lb[3]
    for s in sh + [shw]: s.end()
    for c in hop1 + hop2 + hop3 + late1 + late2: c.wait_send()
    for c in started: c.wait_send()
    for cond, c in guarded: pl.when(cond)(c.wait_send)

def second(x, wt, ck, ids, proj, qt, qn, kk, kt, vn, of, ga, tok, gm, s_ow, s_up, s_dn, l_ow, l_up, l_dn, s4, gupb, vec):
    S = jax.ShapeDtypeStruct; V = pltpu.VMEM
    n, D = tok.shape; N = 4 * n; H = n // 2; L = D // 2
    w = wt.shape[0]; lw = w // 3; heads = lw // HD
    a, q, o = s_ow.shape[1] // 4, s_up.shape[1] // 4, w // 4
    any_ = pl.BlockSpec(memory_space=pl.ANY); vm = pl.BlockSpec(memory_space=pltpu.VMEM)
    outs = [(S((n, D), F32), vm), (S((4 * a, D), BF), any_), (S((4 * q, D), BF), any_), (S((4 * q, D), BF), any_), (S((w, D), BF), any_), (S((9, 8, D), F32), vm)]
    sc = [V((4, n, D), BF), V((w, N), F32), V((heads, 128, N), BF), V((heads, N, 128), BF), V((heads, N, 128), BF), V((heads, HD, N), BF),
          V((heads, N, 128), BF), V((heads, 128, N), BF), V((heads, N, 128), BF), V((heads, N, 128), F32), V((w, N), F32), V((w, n), BF),
          V((w, D), F32), V((w, D), BF), V((4, n, D), BF), V((4, H, D), BF), V((4, H, D), BF), V((2, H, D), BF), V((n, D), F32),
          V((128, 256), F32), V((256, 128), F32), V((256, 128), F32),
          V((4, 2, q, L), BF), V((4, 2, q, L), BF), V((4, 2, a, L), BF), V((4, 2, a, L), BF), V((4, 2, q, L), BF), V((4, 2, q, L), BF),
          V((4, a, L), BF), V((4, q, L), BF), V((4, q, L), BF), V((2, a, L), BF), V((2, q, L), BF), V((2, q, L), BF),
          V((2, a, L), BF), V((2, q, L), BF), V((2, q, L), BF),
          V((3, o, D), BF), V((2, o, L), BF), V((o, L), BF), V((8, 8, D), F32), V((8, 8, D), F32), V((4, 8, D), F32), V((8, 8, D), F32), V((8, 8, D), F32), V((4, 8, D), F32),
          pltpu.SemaphoreType.DMA((160,)), pltpu.SemaphoreType.DMA((160,)), pltpu.SemaphoreType.DMA((60,))]
    return pl.pallas_call(second_kernel, out_shape=tuple(z[0] for z in outs),
        in_specs=[any_, vm, vm, vm] + [any_] * 7 + [vm] * 3 + [any_] * 6 + [vm] * 3, out_specs=tuple(z[1] for z in outs), scratch_shapes=sc,
        compiler_params=pltpu.CompilerParams(collective_id=1, has_side_effects=True, vmem_limit_bytes=60 * 2**20), name="attend_back_and_reduce",
    )(x, wt, ck, ids, proj, qt, qn, kk, kt, vn, of, ga, tok, gm, s_ow, s_up, s_dn, l_ow, l_up, l_dn, s4, gupb, vec)
def finish_kernel(ow, up, dn, w, gt, res, sm, ow_f, up_f, dn_f, w_f, gt_f, res_f, v0, v1, v2, v3, v4, v5, vub, vck):
    ow_f[...] = ow[...].astype(F32)
    up_f[...] = up[...].astype(F32)
    dn_f[...] = dn[...].astype(F32)
    w_f[...] = w[...].astype(F32)
    gt_f[...] = gt[...]
    res_f[...] = res[...]
    @pl.when(pl.program_id(0) == 0)
    def _():
        t = lax.axis_index("tensor")
        def row(k): return sm[k // 6, pl.ds(k % 6, 1), :]
        for k, o in enumerate((v0, v1, v2, v3)): o[...] = row(k).reshape(-1)
        v4[...] = sm[8, 0:1, :].reshape(-1)
        v5[...] = sm[8, 1:2, :].reshape(-1)
        vub[...] = row(6 + t).reshape(-1)
        for j in range(3):
            for c in range(3): vck[j, c:c + 1, :] = row(10 + 9 * t + 3 * j + c)[:, 0:vck.shape[2]]

def finish(ow, up, dn, w, gt, res, sm, G=2):
    spec = lambda a: pl.BlockSpec((a.shape[0] // G, a.shape[1]), lambda g: (g, 0))
    whole = lambda s: pl.BlockSpec(s, lambda g: (0,) * len(s))
    S = jax.ShapeDtypeStruct
    arrays = (ow, up, dn, w, gt, res)
    kinds = (F32, F32, F32, F32, F32, BF)
    D = ow.shape[1]; lw = ow.shape[0]
    small = [(D,)] * 6 + [(up.shape[0],), (3, 3, lw)]
    return pl.pallas_call(finish_kernel, grid=(G,),
        out_shape=tuple(S(a.shape, k) for a, k in zip(arrays, kinds)) + tuple(S(s, F32) for s in small),
        in_specs=[spec(a) for a in arrays] + [whole(sm.shape)], out_specs=tuple(spec(a) for a in arrays) + tuple(whole(s) for s in small),
        name="finish", cost_estimate=pl.CostEstimate(flops=4 * 10**6, bytes_accessed=15 * 10**6, transcendentals=0),
    )(*arrays, sm)


def per_device(planes, tokens, segment_ids, cotangent, norm1_gain, norm1_shift, qkv_weight, conv_kernel, out_weight, out_bias, norm2_gain, norm2_shift, up_weight, up_bias, down_weight, down_bias):
    n, D = tokens.shape
    lw = qkv_weight.shape[2]
    row = lambda v: v.reshape(1, -1)
    wt = jnp.transpose(qkv_weight, (1, 2, 0)).reshape(3 * lw, D)
    x, ids, wtp, ckp, proj, qt, qn, kk, kt, vn, of, res, gm, ga, s_ow, s_up, s_dn, l_ow, l_up, l_dn, s4, gupb = first(
        tokens, row(segment_ids), cotangent, wt, conv_kernel, out_weight, up_weight, down_weight,
        norm1_gain, norm1_shift, out_bias, norm2_gain, norm2_shift, down_bias, up_bias)
    gt, ow_o, up_o, dn_o, w_o, sm = second(x, wtp, ckp, ids, proj, qt, qn, kk, kt, vn, of, ga, tokens, gm, s_ow, s_up, s_dn, l_ow, l_up, l_dn, s4, gupb, norm1_gain)
    ow_o, up_o, dn_o, w_o, gt, res, g_ob, g_n2, g_s2, g_db, g_n1, g_s1, gub, gck = finish(ow_o, up_o, dn_o, w_o, gt, res, sm)
    sums = (w_o, ow_o, up_o, dn_o, g_ob, g_n2, g_s2, g_db, g_n1, g_s1, gub, gck)
    if planes is not None:
        sums = lax.psum(sums, "dp", axis_index_groups=planes)
    w_o, ow_o, up_o, dn_o, g_ob, g_n2, g_s2, g_db, g_n1, g_s1, gub, gck = sums
    gqkv = jnp.transpose(w_o.reshape(3, lw, D), (2, 0, 1))
    return (res, gt, g_n1, g_s1, gqkv, gck, ow_o, g_ob, g_n2, g_s2, up_o, gub, dn_o, g_db)


def solution(mesh):
    dp = mesh.shape["dp"]
    planes = None
    if dp > 8:
        planes = [[8 * k + j for k in range(dp // 8)] for j in range(8)]
    rows_, rep = P_(("dp", "tensor"), None), P_()
    third, cols, first = P_(None, None, "tensor"), P_(None, "tensor"), P_("tensor", None)
    return jax.shard_map(
        functools.partial(per_device, planes),
        mesh=mesh,
        in_specs=(rows_, P_(("dp", "tensor")), rows_, rep, rep, third, third, first, rep, rep, rep, cols, P_("tensor"), first, rep),
        out_specs=(rows_, rows_, rep, rep, third, third, first, rep, rep, rep, cols, P_("tensor"), first, rep),
        check_vma=False,
    )
```
